32 devices in a mesh: dp: 16 (over z, y, x), tensor: 2 (over core).
Axes of the slice: x: 2, y: 2, z: 4, core: 2. Of those that a mesh axis runs over, the one named last changes fastest.
Arguments:
- tokens: bfloat16 [64, 502, 768], P('dp'), may hold values from -6 to 6
- memory: bfloat16 [64, 20, 768], P('dp'), may hold values from -6 to 6
- lengths: int32 [8], replicated, may hold values from 1024 to 8199, as said below
- owners: int32 [4, 16], replicated, may hold values from 0 to 15, as said below
- w_query: bfloat16 [768, 768], P('dp', 'tensor'), may hold values from -0.21875 to 0.21875
- w_key: bfloat16 [768, 768], P('dp', 'tensor'), may hold values from -0.21875 to 0.21875
- w_value: bfloat16 [768, 768], P('dp', 'tensor'), may hold values from -0.21875 to 0.21875
- w_out: bfloat16 [768, 768], P('dp', 'tensor'), may hold values from -0.875 to 0.875
- w_up: bfloat16 [768, 3072], P('dp', 'tensor'), may hold values from -0.21875 to 0.21875
- w_down: bfloat16 [768, 3072], P('dp', 'tensor'), may hold values from -0.15625 to 0.15625
- b_query: bfloat16 [768], P('tensor'), may hold values from -3 to 3
- b_value: bfloat16 [768], P('tensor'), may hold values from -3 to 3
- b_up: bfloat16 [3072], P('tensor'), may hold values from -3 to 3
- b_out: bfloat16 [768], P('dp'), may hold values from -3 to 3
- b_down: bfloat16 [768], P('dp'), may hold values from -3 to 3
- gain_attn: bfloat16 [768], P('dp'), may hold values from 0.5 to 1.5
- shift_attn: bfloat16 [768], P('dp'), may hold values from -3 to 3
- gain_ffn: bfloat16 [768], P('dp'), may hold values from 0.5 to 1.5
- shift_ffn: bfloat16 [768], P('dp'), may hold values from -3 to 3
- cot_tokens: bfloat16 [64, 502, 768], P('dp'), may hold values from -6 to 6
- cot_memory: bfloat16 [64, 20, 768], P('dp'), may hold values from -6 to 6
Outputs:
- out_tokens: bfloat16 [64, 502, 768], P('dp')
- out_memory: bfloat16 [64, 20, 768], P('dp')
- grad_tokens: bfloat16 [64, 502, 768], P('dp')
- grad_memory: bfloat16 [64, 20, 768], P('dp')
- grad_w_query: float32 [768, 768], P('dp', 'tensor')
- grad_w_key: float32 [768, 768], P('dp', 'tensor')
- grad_w_value: float32 [768, 768], P('dp', 'tensor')
- grad_w_out: float32 [768, 768], P('dp', 'tensor')
- grad_w_up: float32 [768, 3072], P('dp', 'tensor')
- grad_w_down: float32 [768, 3072], P('dp', 'tensor')
- grad_b_out: float32 [768], P('dp')
- grad_b_down: float32 [768], P('dp')
- grad_gain_attn: float32 [768], P('dp')
- grad_shift_attn: float32 [768], P('dp')
- grad_gain_ffn: float32 [768], P('dp')
- grad_shift_ffn: float32 [768], P('dp')
- grad_b_query: float32 [768], P('tensor')
- grad_b_value: float32 [768], P('tensor')
- grad_b_up: float32 [3072], P('tensor')
The draws below stay inside these ranges and needn't reach their ends.
Inputs may be any that keep to these rules, and one draw needn't show every extreme that they name: Sequence j takes ceil(lengths[j] / 502) segments; these counts add up to exactly 64, and the segments stand sequence after sequence in the order of lengths. Each row of owners is a permutation of 0 to 15; for every k and every row, the numbers (owners[m, i] mod 2^(k+1)) + i - (i mod 2^(k+1)) over all i are all different.
All inputs are finite; a program needn't handle non-finite values.
Results may differ from the reference program's by a relative error of at most 0.019.
Values may be sent and summed in bfloat16 or wider, within the bound.
A program may use at most 320 MiB of HBM per device.

```python
import jax
import jax.numpy as jnp
from jax import lax

D = 768
HEADS = 12
HEAD = 64
FF = 3072
SEG_TOK = 502
MEM = 10
MB = 4
ROWS = 522
SEGS = 64
N_DP = 16


def draw_lengths(key, part):
    count_seq = SEGS // 8
    pair_key = jax.random.fold_in(key, 11)
    tail_key = jax.random.fold_in(key, 12)
    order_key = jax.random.fold_in(key, 13)
    spread = jax.random.randint(pair_key, ((count_seq - 4) // 2,), 0, 5)
    paired = jnp.stack([8 + spread, 8 - spread], axis=1).reshape(-1).astype(jnp.int32)
    counts = jnp.concatenate([jnp.array([17, 3, 6, 6], dtype=jnp.int32), paired])
    tails = jax.random.randint(tail_key, (count_seq,), 1, SEG_TOK + 1).astype(jnp.int32)
    seq_sizes = (counts - 1) * SEG_TOK + tails
    seq_sizes = jnp.where(counts == 17, 16 * SEG_TOK + SEG_TOK // 3, seq_sizes)
    seq_sizes = jnp.where(counts == 3, 2 * SEG_TOK + SEG_TOK // 25, seq_sizes)
    shuffle = jax.random.permutation(order_key, count_seq)
    return seq_sizes[shuffle].astype(jnp.int32)


def draw_owners(key, part):
    level_count = N_DP.bit_length() - 1
    rows_out = []
    for micro in range(MB):
        position = jnp.arange(N_DP, dtype=jnp.int32)
        for section_bit in range(level_count):
            stride = 2 ** section_bit
            switches = jax.random.randint(jax.random.fold_in(jax.random.fold_in(key, micro + 100), section_bit), (N_DP,), 0, 2).astype(jnp.int32)
            bit_value = position // stride % 2
            paired = position - bit_value * stride
            position = position + switches[paired] * stride * (1 - 2 * bit_value)
        rows_out.append(position)
    return jnp.stack(rows_out).astype(jnp.int32)


def raised(values, stream_key, source, target, blocks, factor):
    def block_of(axis_at):
        return (jnp.arange(values.shape[axis_at]) // (values.shape[axis_at] // blocks)).reshape((-1,) + (1,) * (values.ndim - 1 - axis_at))

    one_side = jax.random.permutation(stream_key, blocks)[block_of(target)]
    second = (block_of(target) + blocks // 2) % blocks
    return jnp.where((block_of(source) == one_side) | (block_of(source) == second), factor * values, values)


def level_of(rng, extent, cuts, low, high):
    level, own = 1.0, jax.random.fold_in(rng, 6)
    for axis_at, parts in cuts:
        draws = jnp.exp(jax.random.uniform(jax.random.fold_in(own, axis_at), (parts,), jnp.float32, low / len(cuts), high / len(cuts)))
        level = level * jnp.repeat(draws, extent[axis_at] // parts).reshape([-1 if axis == axis_at else 1 for axis in range(len(extent))])
    return level


def normal_values(key, extent, width, most, cuts=(), held_as=jnp.bfloat16):
    drawn = jax.random.normal(key, extent, jnp.float32) * width
    if len(cuts) > 0:
        drawn = level_of(key, extent, cuts, -0.22, 0.18) * drawn
    return jnp.clip(drawn, min=-most, max=most).astype(held_as)


def noise_with(rng, dims, deviation, most, pieces, heavy, kind=jnp.bfloat16):
    values = deviation * jax.random.normal(rng, dims, jnp.float32)
    if pieces:
        values = values * level_of(rng, dims, pieces, -0.22, 0.18)
    return jnp.clip(raised(values, jax.random.fold_in(rng, 3), *heavy), -most, most).astype(kind)


def setup_inputs(seed: int = 0) -> dict:
    key_of = jax.random.split(jax.random.key(seed), 22)
    tokens = noise_with(key_of[0], (SEGS, SEG_TOK, D), 1.0, 6.0, ((0, 16),), (0, 2, 16, 2.0))
    memory = normal_values(key_of[1], (SEGS, 2 * MEM, D), 1.0, 6.0, ((0, 16),))
    lengths = draw_lengths(jax.random.fold_in(key_of[21], 71), 0)
    owners = draw_owners(jax.random.fold_in(key_of[21], 71), 0)
    w_query = normal_values(key_of[4], (D, D), D ** -0.5, 0.21875, ((0, 16), (1, 2)))
    w_key = normal_values(key_of[5], (D, D), D ** -0.5, 0.21875, ((0, 16), (1, 2)))
    w_value = normal_values(key_of[6], (D, D), D ** -0.5, 0.21875, ((0, 16), (1, 2)))
    w_out = normal_values(key_of[7], (D, D), (D // 16) ** -0.5, 0.875, ((0, 16), (1, 2)))
    w_up = normal_values(key_of[8], (D, FF), D ** -0.5, 0.21875, ((0, 16), (1, 2)))
    w_down = normal_values(key_of[9], (D, FF), (FF // 2) ** -0.5, 0.15625, ((0, 16), (1, 2)))
    b_query = normal_values(key_of[10], (D,), 0.5, 3.0, ((0, 2),))
    b_value = normal_values(key_of[11], (D,), 0.5, 3.0, ((0, 2),))
    b_up = normal_values(key_of[12], (FF,), 0.5, 3.0, ((0, 2),))
    b_out = normal_values(key_of[13], (D,), 0.5, 3.0, ((0, 16),))
    b_down = normal_values(key_of[14], (D,), 0.5, 3.0, ((0, 16),))
    gain_attn = jnp.clip(1.0 + 0.1 * jax.random.normal(key_of[15], (D,), jnp.float32), 0.5, 1.5).astype(jnp.bfloat16)
    shift_attn = normal_values(key_of[16], (D,), 0.5, 3.0, ((0, 16),))
    gain_ffn = jnp.clip(1.0 + 0.1 * jax.random.normal(key_of[17], (D,), jnp.float32), 0.5, 1.5).astype(jnp.bfloat16)
    shift_ffn = normal_values(key_of[18], (D,), 0.5, 3.0, ((0, 16),))
    cot_tokens = normal_values(key_of[19], (SEGS, SEG_TOK, D), 1.0, 6.0, ((0, 16),))
    cot_memory = normal_values(key_of[20], (SEGS, 2 * MEM, D), 1.0, 6.0, ((0, 16),))
    return {"tokens": tokens, "memory": memory, "lengths": lengths, "owners": owners, "w_query": w_query, "w_key": w_key, "w_value": w_value, "w_out": w_out, "w_up": w_up, "w_down": w_down, "b_query": b_query, "b_value": b_value, "b_up": b_up, "b_out": b_out, "b_down": b_down, "gain_attn": gain_attn, "shift_attn": shift_attn, "gain_ffn": gain_ffn, "shift_ffn": shift_ffn, "cot_tokens": cot_tokens, "cot_memory": cot_memory}


@jax.custom_vjp
def low(v):
    return lax.optimization_barrier(v.astype(jnp.bfloat16)).astype(jnp.float32)

@jax.custom_vjp
def low_back(v):
    return v

def low_keep(v):
    return (low(v), None)

def low_pass(kept, grad):
    return (grad,)

def back_keep(v):
    return (v, None)

def back_low(kept, grad):
    return (low(grad),)
low.defvjp(low_keep, low_pass)
low_back.defvjp(back_keep, back_low)
highest = lax.Precision.HIGHEST
epsilon = 1e-05
masked_score = -1000000000.0

def both_round(values):
    return low(low_back(values))

def valid_counts(lengths):
    counts = ((lengths + SEG_TOK - 1) // SEG_TOK).astype(jnp.int32)
    ends = jnp.cumsum(counts).astype(jnp.int32)
    starts = (ends - counts).astype(jnp.int32)
    index = jnp.arange(SEGS, dtype=jnp.int32)[:, None]
    inside = (index >= starts[None, :]) & (index < ends[None, :])
    remain = lengths[None, :] - (index - starts[None, :]) * SEG_TOK
    return lax.optimization_barrier(jnp.sum(jnp.where(inside, jnp.minimum(remain, SEG_TOK), 0), axis=1)).astype(jnp.int32)

def layer_norm(values, gain, shift):
    row_mean = lax.optimization_barrier(jnp.mean(values, -1, keepdims=True))
    centered = values - row_mean
    row_var = lax.optimization_barrier(jnp.mean(centered * centered, -1, keepdims=True))
    return centered * lax.rsqrt(row_var + epsilon) * gain + shift

def segment_forward(params, rows, live):
    w_query, w_key, w_value, w_out, w_up, w_down, b_query, b_value, b_up, b_out, b_down, gain_attn, shift_attn, gain_ffn, shift_ffn = params
    count_rows = rows.shape[0]
    queries = both_round(jnp.dot(rows, w_query, precision=highest) + b_query)
    key_rows = both_round(jnp.dot(rows, w_key, precision=highest))
    value_rows = both_round(jnp.dot(rows, w_value, precision=highest) + b_value)
    query_heads = queries.reshape(count_rows, HEADS, HEAD)
    key_heads = key_rows.reshape(count_rows, HEADS, HEAD)
    value_heads = value_rows.reshape(count_rows, HEADS, HEAD)
    scores = jnp.einsum('qhd,khd->hqk', query_heads, key_heads, precision=highest) * (1.0 / jnp.sqrt(jnp.float32(HEAD)))
    scores = low_back(scores)
    scores = scores + jnp.where(live > 0, 0.0, masked_score)[None, None, :]
    peak = lax.optimization_barrier(jnp.max(scores, -1, keepdims=True))
    exponent = jnp.exp(scores - peak)
    probs = low(exponent / lax.optimization_barrier(jnp.sum(exponent, -1, keepdims=True)))
    attended = jnp.einsum('hqk,khd->qhd', probs, value_heads, precision=highest).reshape(count_rows, D)
    attended = both_round(attended)
    branch = low_back(jnp.dot(attended, w_out.T, precision=highest))
    normal_one = layer_norm(rows + branch + b_out, gain_attn, shift_attn)
    pre_act = low_back(jnp.dot(low(normal_one), w_up, precision=highest) + b_up)
    activated = low(jax.nn.gelu(pre_act, approximate=False))
    feed = low_back(jnp.dot(activated, w_down.T, precision=highest))
    return layer_norm(normal_one + feed + b_down, gain_ffn, shift_ffn) * live[:, None]

def reference(tokens, memory, lengths, owners, w_query, w_key, w_value, w_out, w_up, w_down, b_query, b_value, b_up, b_out, b_down, gain_attn, shift_attn, gain_ffn, shift_ffn, cot_tokens, cot_memory):
    params = tuple((w.astype(jnp.float32) for w in (w_query, w_key, w_value, w_out, w_up, w_down, b_query, b_value, b_up, b_out, b_down, gain_attn, shift_attn, gain_ffn, shift_ffn)))
    valid = valid_counts(lengths)
    index = jnp.arange(SEGS, dtype=jnp.int32)
    micro = (index % MB).astype(jnp.int32)
    source = (index // MB).astype(jnp.int32)
    slot = (owners[micro, source] * MB + micro).astype(jnp.int32)
    mem_seg = memory.astype(jnp.float32)[slot]
    mem_cot = cot_memory.astype(jnp.float32)[slot]
    position = jnp.arange(ROWS, dtype=jnp.int32)

    def whole(params, token_rows, mem_rows):

        def one(item):
            tok, mem, count = item
            rows = jnp.concatenate([mem[:MEM], tok, mem[MEM:]], axis=0)
            live = ((position < MEM) | (position >= MEM + SEG_TOK) | (position - MEM < count)).astype(jnp.float32)
            result = segment_forward(params, rows, live)
            return (result[MEM:MEM + SEG_TOK], jnp.concatenate([result[:MEM], result[MEM + SEG_TOK:]], axis=0))
        return lax.map(jax.checkpoint(one), (token_rows, mem_rows, valid))
    (out_tok, out_mem), pullback = jax.vjp(whole, params, tokens.astype(jnp.float32), mem_seg)
    grad_params, grad_tok, grad_mem = pullback((cot_tokens.astype(jnp.float32), mem_cot))
    out_memory = jnp.zeros((SEGS, 2 * MEM, D), jnp.float32).at[slot].set(out_mem)
    grad_memory = jnp.zeros((SEGS, 2 * MEM, D), jnp.float32).at[slot].set(grad_mem)
    g_wq, g_wk, g_wv, g_wo, g_wu, g_wd, g_bq, g_bv, g_bu, g_bo, g_bd, g_ga, g_sa, g_gf, g_sf = grad_params
    return (out_tok.astype(jnp.bfloat16), out_memory.astype(jnp.bfloat16), grad_tok.astype(jnp.bfloat16), grad_memory.astype(jnp.bfloat16), g_wq, g_wk, g_wv, g_wo, g_wu, g_wd, g_bo, g_bd, g_ga, g_sa, g_gf, g_sf, g_bq, g_bv, g_bu)
```

```python
import functools
import math

import jax
import jax.numpy as jnp
from jax import lax
from jax.experimental import pallas as pl
from jax.experimental.pallas import tpu as pltpu
from jax.sharding import PartitionSpec as P

HEAD = 64
TOK = 512
ROWS = 544
PAIR = 128
masked_score = -1000000000.0
epsilon = 1e-05
F32, LOW = jnp.float32, jnp.bfloat16


def dot(a, b, left, right):
    return lax.dot_general(a, b, (((left,), (right,)), ((), ())), preferred_element_type=F32)


def live_at(position, count, mem):
    return (position < count) | ((position >= TOK) & (position < TOK + mem))


def project(x_ref, w_ref, bias_ref, q_ref, k_ref, v_ref, seg, half):
    width = w_ref.shape[2] // 3
    pairs = width // PAIR
    rows = x_ref[pl.ds(seg * ROWS, ROWS), :]
    lane = lax.broadcasted_iota(jnp.int32, (1, PAIR), 1)
    for kind in range(3):
        for i in range(pairs):
            at = kind * width + i * PAIR
            got = dot(rows, w_ref[half, :, at:at + PAIR], 1, 0)
            p = half * pairs + i
            if kind == 0:
                got = (got + bias_ref[half, 0:1, i * PAIR:(i + 1) * PAIR]) * (1.0 / math.sqrt(HEAD))
                q_ref[seg, p, 0] = jnp.where(lane < HEAD, got, 0.0).astype(LOW)
                q_ref[seg, p, 1] = jnp.where(lane < HEAD, 0.0, got).astype(LOW)
            elif kind == 1:
                k_ref[seg, p] = got.astype(LOW)
            else:
                v_ref[seg, p] = (got + bias_ref[half, 1:2, i * PAIR:(i + 1) * PAIR]).astype(LOW)


def attend(q_ref, k_ref, v_ref, o_ref, linv_ref, e_slot, count, mem, seg, p):
    col = lax.broadcasted_iota(jnp.int32, (1, ROWS), 1)
    lane = lax.broadcasted_iota(jnp.int32, (1, PAIR), 1)
    masking = jnp.where(live_at(col, count, mem), 0.0, masked_score)
    keys = k_ref[seg, p]
    values = jnp.concatenate([v_ref[seg, p], jnp.ones((ROWS, PAIR), LOW)], 1)
    got = []
    for j in range(2):
        scores = dot(q_ref[seg, p, j], keys, 1, 1) + masking
        peak = jnp.max(scores, -1, keepdims=True)
        e_slot[j] = jnp.exp(scores - peak).astype(LOW)
        got.append(dot(e_slot[j], values, 1, 0))
    first = lane < HEAD
    linv = 1.0 / jnp.where(first, got[0][:, PAIR:], got[1][:, PAIR:])
    linv_ref[seg, p] = linv
    o_ref[seg, p] = (jnp.where(first, got[0][:, :PAIR], got[1][:, :PAIR]) * linv).astype(LOW)


def attend_back(q_ref, k_ref, v_ref, o_ref, linv_ref, do_ref, e_slot, ds_ref, out_ref, seg, p, half, i, width):
    lane = lax.broadcasted_iota(jnp.int32, (1, PAIR), 1)
    keys, values = k_ref[seg, p], v_ref[seg, p]
    scaled = do_ref[seg, p].astype(F32) * linv_ref[seg, p]
    product = scaled * o_ref[seg, p].astype(F32)
    dq, dk, dv = [], None, None
    for j in range(2):
        mine = (lane < HEAD) if j == 0 else (lane >= HEAD)
        mine_low = jnp.where(mine, scaled, 0.0).astype(LOW)
        delta = jnp.sum(jnp.where(mine, product, 0.0), -1, keepdims=True)
        gap = dot(mine_low, values, 1, 1) - delta
        ds_ref[j] = (e_slot[j].astype(F32) * gap).astype(LOW)
        dq.append(dot(ds_ref[j], keys, 1, 0))
        one_v = dot(e_slot[j], mine_low, 0, 0)
        one_k = dot(ds_ref[j], q_ref[seg, p, j], 0, 0)
        dv = one_v if dv is None else dv + one_v
        dk = one_k if dk is None else dk + one_k
    rows = pl.ds(seg * ROWS, ROWS)
    dq = jnp.where(lane < HEAD, dq[0], dq[1]) * (1.0 / math.sqrt(HEAD))
    for kind, value in enumerate((dq, dk, dv)):
        out_ref[half, rows, pl.ds(kind * width + i * PAIR, PAIR)] = value.astype(LOW)


def normed(values):
    mean = jnp.mean(values, -1, keepdims=True)
    centered = values - mean
    inv = lax.rsqrt(jnp.mean(centered * centered, -1, keepdims=True) + epsilon)
    return centered * inv, inv


def norm_back(scaled, unit, inv):
    return inv * (scaled - jnp.mean(scaled, -1, keepdims=True) - unit * jnp.mean(scaled * unit, -1, keepdims=True))


def fold(total_ref, row, value):
    total_ref[row:row + 1, :] += jnp.sum(value, 0, keepdims=True)


def forward_kernel(mem, count_ref, x_ref, w_ref, bias_ref, q_ref, k_ref, v_ref, e_ref, o_ref, linv_ref, slots, sems):
    def copy(i, slot):
        return pltpu.make_async_copy(slots.at[slot], e_ref.at[i // 6, i % 6], sems.at[slot])

    def projected(i, carry):
        project(x_ref, w_ref, bias_ref, q_ref, k_ref, v_ref, i // 2, 0)
        project(x_ref, w_ref, bias_ref, q_ref, k_ref, v_ref, i // 2, 1)
        return carry

    for s in range(2):
        for h in range(2):
            project(x_ref, w_ref, bias_ref, q_ref, k_ref, v_ref, s, h)

    def step(i, carry):
        slot = i % 2
        seg, p = i // 6, i % 6

        @pl.when(i >= 2)
        def _():
            copy(i - 2, slot).wait()

        count = jnp.where(seg == 0, count_ref[0], count_ref[1])
        attend(q_ref, k_ref, v_ref, o_ref, linv_ref, slots.at[slot], count, mem, seg, p)
        copy(i, slot).start()
        return carry

    lax.fori_loop(0, 12, step, 0)
    copy(10, 0).wait()
    copy(11, 1).wait()


def forward(count, x, w, bias, mem):
    vm = pl.BlockSpec(memory_space=pltpu.VMEM)
    sm = pl.BlockSpec(memory_space=pltpu.SMEM)
    hb = pl.BlockSpec(memory_space=pl.ANY)
    S = jax.ShapeDtypeStruct
    return pl.pallas_call(
        functools.partial(forward_kernel, mem),
        out_shape=[S((2, 6, 2, ROWS, PAIR), LOW), S((2, 6, ROWS, PAIR), LOW), S((2, 6, ROWS, PAIR), LOW),
                   S((2, 6, 2, ROWS, ROWS), LOW), S((2, 6, ROWS, PAIR), LOW), S((2, 6, ROWS, PAIR), F32)],
        in_specs=[sm, vm, vm, vm], out_specs=[vm, vm, vm, hb, vm, vm],
        scratch_shapes=[pltpu.VMEM((2, 2, ROWS, ROWS), LOW), pltpu.SemaphoreType.DMA((2,))],
        compiler_params=pltpu.CompilerParams(vmem_limit_bytes=56 << 20),
    )(count, x, w, bias)


def middle_kernel(width, mem, tile, count_ref, x_ref, o_ref, cot_ref, vec_ref, bup_ref, wout_ref, wup_ref, wdown_ref,
                  y_ref, gdown_ref, gup_ref, gout_ref, do_ref, dh_ref, sums_ref, sup_ref,
                  x1_ref, low_ref, unit_ref, inv_ref, g_ref, d_ref, flip_ref):
    R = 2 * ROWS
    pairs = width // PAIR
    hidden = wup_ref.shape[2]
    sums_ref[...] = jnp.zeros_like(sums_ref)
    vec = {n: vec_ref[k:k + 1, :] for k, n in enumerate(("b_out", "b_down", "gain_attn", "shift_attn", "gain_ffn", "shift_ffn"))}

    def out_step(s, carry):
        rows = pl.ds(pl.multiple_of(s * ROWS, ROWS), ROWS)
        h = x_ref[rows, :].astype(F32) + vec["b_out"]
        for t in range(2):
            o = jnp.concatenate([o_ref[s, t * pairs + i] for i in range(pairs)], 1)
            h = h + dot(o, wout_ref[t, :, :width], 1, 1)
        unit, inv = normed(h)
        x1 = unit * vec["gain_attn"] + vec["shift_attn"]
        x1_ref[rows, :] = x1
        low_ref[rows, :] = x1.astype(LOW)
        unit_ref[rows, :] = unit.astype(LOW)
        inv_ref[rows, :] = inv
        return carry

    lax.fori_loop(0, 2, out_step, 0)

    steps = hidden // tile

    def up_step(k, carry):
        t, i = k // steps, k % steps
        cols = pl.ds(pl.multiple_of(i * tile, tile), tile)
        u = dot(low_ref[...], wup_ref[t, :, cols], 1, 0) + bup_ref[t, 0:1, cols]
        phi = 0.5 * (1.0 + lax.erf(u * (1.0 / math.sqrt(2.0))))
        g_ref[t, :, cols] = (u * phi).astype(LOW)
        d_ref[t, :, cols] = (phi + u * (jnp.exp(-0.5 * u * u) * (1.0 / math.sqrt(2.0 * math.pi)))).astype(LOW)
        return carry

    lax.fori_loop(0, 2 * steps, up_step, 0)

    part = R // 4

    def down_step(s, carry):
        rows = pl.ds(pl.multiple_of(s * part, part), part)
        h = x1_ref[rows, :] + vec["b_down"]
        for t in range(2):
            h = h + dot(g_ref[t, rows, :], wdown_ref[t], 1, 1)
        unit, inv = normed(h)
        count = jnp.where(s < 2, count_ref[0], count_ref[1])
        at = lax.broadcasted_iota(jnp.int32, (part, 1), 0) + (s % 2) * part
        live = jnp.where(live_at(at, count, mem), 1.0, 0.0)
        y_ref[rows, :] = ((unit * vec["gain_ffn"] + vec["shift_ffn"]) * live).astype(LOW)
        dy = cot_ref[rows, :].astype(F32) * live
        fold(sums_ref, 4, dy * unit)
        fold(sums_ref, 5, dy)
        dh = norm_back(dy * vec["gain_ffn"], unit, inv)
        fold(sums_ref, 1, dh)
        x1_ref[rows, :] = dh
        dh_ref[rows, :] = dh
        return carry

    lax.fori_loop(0, 4, down_step, 0)
    df = x1_ref[...].astype(LOW)
    flip_ref[...] = df.T
    dlow = dh_ref

    def back_step(k, carry):
        t, i = k // steps, k % steps
        cols = pl.ds(pl.multiple_of(i * tile, tile), tile)
        gdown_ref[t, :, cols] = dot(flip_ref[...], g_ref[t, :, cols], 1, 0).astype(LOW)
        du = dot(dlow[...].astype(LOW), wdown_ref[t, :, cols], 1, 0) * d_ref[t, :, cols].astype(F32)
        sup_ref[t, 0:1, cols] = jnp.sum(du, 0, keepdims=True)
        d_ref[t, :, cols] = du.astype(LOW)
        return carry

    lax.fori_loop(0, 2 * steps, back_step, 0)
    flip_ref[...] = low_ref[...].T

    def up_back(k, carry):
        t, i = k // steps, k % steps
        cols = pl.ds(pl.multiple_of(i * tile, tile), tile)
        gup_ref[t, :, cols] = dot(flip_ref[...], d_ref[t, :, cols], 1, 0).astype(LOW)
        return carry

    lax.fori_loop(0, 2 * steps, up_back, 0)

    def in_step(s, carry):
        rows = pl.ds(pl.multiple_of(s * part, part), part)
        dx = dh_ref[rows, :]
        for t in range(2):
            dx = dx + dot(d_ref[t, rows, :], wup_ref[t], 1, 1)
        unit = unit_ref[rows, :].astype(F32)
        fold(sums_ref, 2, dx * unit)
        fold(sums_ref, 3, dx)
        dh = norm_back(dx * vec["gain_attn"], unit, inv_ref[rows, :])
        fold(sums_ref, 0, dh)
        dh_ref[rows, :] = dh
        low_ref[rows, :] = dh.astype(LOW)
        return carry

    lax.fori_loop(0, 4, in_step, 0)
    flip_ref[...] = low_ref[...].T
    for t in range(2):
        for i in range(pairs):
            both = jnp.concatenate([o_ref[0, t * pairs + i], o_ref[1, t * pairs + i]], 0)
            gout_ref[t, :, i * PAIR:(i + 1) * PAIR] = dot(flip_ref[...], both, 1, 0).astype(LOW)
        for s in range(2):
            back = dot(low_ref[s * ROWS:(s + 1) * ROWS, :], wout_ref[t, :, :width], 1, 0).astype(LOW)
            for i in range(pairs):
                do_ref[s, t * pairs + i] = back[:, i * PAIR:(i + 1) * PAIR]


def middle(count, x, o, cot, vec, bup, wout, wup, wdown, width, mem, tile=512):
    vm = pl.BlockSpec(memory_space=pltpu.VMEM)
    sm = pl.BlockSpec(memory_space=pltpu.SMEM)
    S = jax.ShapeDtypeStruct
    R, D = x.shape
    H = wup.shape[2]
    return pl.pallas_call(
        functools.partial(middle_kernel, width, mem, tile),
        out_shape=[S((R, D), LOW), S((2, D, H), LOW), S((2, D, H), LOW), S((2, D, width), LOW),
                   S(o.shape, LOW), S((R, D), F32), S((8, D), F32), S((2, 8, H), F32)],
        in_specs=[sm] + [vm] * 8, out_specs=[vm] * 8,
        scratch_shapes=[pltpu.VMEM((R, D), F32), pltpu.VMEM((R, D), LOW), pltpu.VMEM((R, D), LOW), pltpu.VMEM((R, 1), F32),
                        pltpu.VMEM((2, R, H), LOW), pltpu.VMEM((2, R, H), LOW), pltpu.VMEM((D, R), LOW)],
        compiler_params=pltpu.CompilerParams(vmem_limit_bytes=63 << 20),
    )(count, x, o, cot, vec, bup, wout, wup, wdown)


def backward_kernel(x_ref, q_ref, k_ref, v_ref, e_ref, o_ref, linv_ref, do_ref, dh_ref, w_ref,
                    dx_ref, g_ref, sums_ref, slots, ds_ref, out_ref, flip_ref, sems):
    width = w_ref.shape[2] // 3
    R = 2 * ROWS

    def copy(i, slot):
        return pltpu.make_async_copy(e_ref.at[i // 6, i % 6], slots.at[slot], sems.at[slot])

    copy(0, 0).start()

    def step(i, carry):
        slot = i % 2
        seg, p = i // 6, i % 6

        @pl.when(i < 11)
        def _():
            copy(i + 1, 1 - slot).start()

        copy(i, slot).wait()
        attend_back(q_ref, k_ref, v_ref, o_ref, linv_ref, do_ref, slots.at[slot], ds_ref, out_ref, seg, p, p // 3, p % 3, width)
        return carry

    lax.fori_loop(0, 12, step, 0)
    flip_ref[...] = x_ref[...].T
    for t in range(2):
        for kind in range(3):
            cols = slice(kind * width, (kind + 1) * width)
            g_ref[t, :, cols] = dot(flip_ref[...], out_ref[t, :, cols], 1, 0).astype(LOW)
        sums_ref[t, 0:1, :] = jnp.sum(out_ref[t, :, 0:width].astype(F32), 0, keepdims=True)
        sums_ref[t, 1:2, :] = jnp.sum(out_ref[t, :, 2 * width:].astype(F32), 0, keepdims=True)
    part = R // 4

    def in_step(s, carry):
        rows = pl.ds(pl.multiple_of(s * part, part), part)
        dx = dh_ref[rows, :]
        for t in range(2):
            dx = dx + dot(out_ref[t, rows, :], w_ref[t], 1, 1)
        dx_ref[rows, :] = dx.astype(LOW)
        return carry

    lax.fori_loop(0, 4, in_step, 0)


def backward(x, q, k, v, e, o, linv, do, dh, w):
    vm = pl.BlockSpec(memory_space=pltpu.VMEM)
    hb = pl.BlockSpec(memory_space=pl.ANY)
    S = jax.ShapeDtypeStruct
    R, D = x.shape
    W = w.shape[2]
    return pl.pallas_call(
        backward_kernel,
        out_shape=[S((R, D), LOW), S((2, D, W), LOW), S((2, 8, W // 3), F32)],
        in_specs=[vm, vm, vm, vm, hb, vm, vm, vm, vm, vm], out_specs=[vm] * 3,
        scratch_shapes=[pltpu.VMEM((2, 2, ROWS, ROWS), LOW), pltpu.VMEM((2, ROWS, ROWS), LOW), pltpu.VMEM((2, R, W), LOW),
                        pltpu.VMEM((D, R), LOW), pltpu.SemaphoreType.DMA((2,))],
        compiler_params=pltpu.CompilerParams(vmem_limit_bytes=63 << 20),
    )(x, q, k, v, e, o, linv, do, dh, w)


MESH = pl.DeviceIdType.MESH
GRID = (4, 2, 2)


class Place:
    def __init__(self):
        me = lax.axis_index("dp")
        self.t = lax.axis_index("tensor")
        self.x = me % 2
        self.y = (me // 2) % 2
        self.z = me // 4
        self.px = self.at(self.z, self.y, 1 - self.x)
        self.py = self.at(self.z, 1 - self.y, self.x)
        self.zs = [(self.z + d) % 4 for d in (1, 2, 3)]
        self.zb = [(self.z + 4 - d) % 4 for d in (1, 2, 3)]
        self.pz = [self.at(z, self.y, self.x) for z in self.zs]
        self.pz1 = self.at(self.z + 1 - 2 * (self.z % 2), self.y, self.x)
        self.pz2 = self.at((self.z + 2) % 4, self.y, self.x)
        self.pc = (me, 1 - self.t)

    def at(self, z, y, x):
        return (z * 4 + y * 2 + x, self.t)


def greet(devices):
    barrier = pltpu.get_barrier_semaphore()
    for device in devices:
        pl.semaphore_signal(barrier, inc=1, device_id=device, device_id_type=MESH)
    pl.semaphore_wait(barrier, len(devices))


class Wire:
    def __init__(self, send, recv):
        self.send, self.recv, self.count, self.open = send, recv, 0, []

    def start(self, src, dst, device, landing):
        k = self.count
        self.count += 1
        copy = pltpu.make_async_remote_copy(
            src_ref=src, dst_ref=dst, send_sem=self.send.at[k], recv_sem=self.recv.at[k],
            device_id=device, device_id_type=MESH)
        copy.start()
        self.open.append(copy)
        return pltpu.make_async_remote_copy(
            src_ref=landing, dst_ref=landing, send_sem=self.send.at[k], recv_sem=self.recv.at[k],
            device_id=device, device_id_type=MESH)

    def drain(self):
        for copy in self.open:
            copy.wait_send()
        self.open = []


def first_part(width):
    return {384: 128, 512: 256, 640: 256, 768: 256, 1152: 512, 1536: 640}[width]


class Gather:
    def __init__(self, wire, place, src, out, cols, order):
        self.wire, self.p, self.src, self.out = wire, place, src, out
        self.cols, self.order, self.landed, self.crossing = cols, order, [], []

    def view(self, z, y, x, half=None):
        return self.out.at[self.p.t if half is None else half, z, y, x, :, self.cols]

    def stage(self, s):
        p, every = self.p, slice(None)
        for copy in self.landed:
            copy.wait_recv()
        self.landed = []
        own = self.src.at[:, self.cols]
        home = self.view(p.z, p.y, p.x)
        if self.order == "zxy":
            if s == 0:
                for k in range(3):
                    self.go(own, home, p.pz[k], self.view(p.zb[k], p.y, p.x))
            elif s == 1:
                self.go(self.view(every, p.y, p.x), None, p.px, self.view(every, p.y, 1 - p.x))
                self.cross(every, p.y, p.x)
            elif s == 2:
                self.go(self.view(every, p.y, every), None, p.py, self.view(every, 1 - p.y, every))
                self.cross(every, p.y, 1 - p.x)
            else:
                self.cross(every, 1 - p.y, every)
        else:
            if s == 0:
                self.go(own, home, p.py, self.view(p.z, 1 - p.y, p.x))
            elif s == 1:
                for k in range(3):
                    self.go(self.view(p.z, every, p.x), None, p.pz[k], self.view(p.zb[k], every, p.x))
                self.cross(p.z, every, p.x)
            elif s == 2:
                self.go(self.view(every, every, p.x), None, p.px, self.view(every, every, 1 - p.x))
                for k in range(3):
                    self.cross(p.zb[k], every, p.x)
            else:
                self.cross(every, every, 1 - p.x)

    def go(self, src, dst, device, landing):
        self.landed.append(self.wire.start(src, src if dst is None else dst, device, landing))

    def cross(self, z, y, x):
        mine = self.view(z, y, x)
        self.crossing.append(self.wire.start(mine, mine, self.p.pc, self.view(z, y, x, 1 - self.p.t)))

    def whole(self):
        for copy in self.crossing:
            copy.wait_recv()
        self.crossing = []


class Travel:
    def __init__(self, wire, place, keep, payload, held, landing, level_order):
        self.wire, self.p, self.keep, self.landed = wire, place, keep, None
        self.held, self.landing, self.order, self.payload = held, landing, level_order, payload

    def stage(self, s):
        p = self.p
        levels = len(self.order)
        if s > 0:
            self.landed.wait_recv()
            before = self.payload if s == 1 else self.held.at[s - 2]
            for m in range(self.payload.shape[0]):
                stay = self.keep[m, self.order[s - 1]] > 0
                mine, theirs = before[m].astype(jnp.float32), self.landing[s - 1, m].astype(jnp.float32)
                self.held[s - 1, m] = jnp.where(stay, mine, theirs).astype(self.held.dtype)
        if s < levels:
            bit = self.order[s]
            device = [p.px, p.py, p.pz1, p.pz2][bit]
            src = self.payload if s == 0 else self.held.at[s - 1]
            self.landed = self.wire.start(src, self.landing.at[s], device, self.landing.at[s])


def gather_kernel(n, *refs):
    keep, bias, payload = refs[0], refs[1], refs[2]
    ins, outs = refs[3:3 + n], refs[3 + n:3 + 2 * n]
    bias_out, mem_out = refs[3 + 2 * n:5 + 2 * n]
    held, landing, send, recv, here = refs[5 + 2 * n:]
    place = Place()
    wire = Wire(send, recv)
    greet([place.px, place.py, *place.pz, place.pc])
    parts = []
    for c in range(n):
        width = ins[c].shape[1]
        cut = first_part(width)
        parts.append([
            Gather(wire, place, ins[c], outs[c], pl.ds(0, cut), "yzx"),
            Gather(wire, place, ins[c], outs[c], pl.ds(cut, width - cut), "zxy"),
        ])
    crossing = wire.start(bias, bias_out.at[place.t], place.pc, bias_out.at[1 - place.t])
    own = pltpu.make_async_copy(bias, bias_out.at[place.t], here.at[n])
    own.start()
    travel = Travel(wire, place, keep, payload, held, landing, (3, 2, 1, 0))
    local = []
    for c in range(n):
        copy = pltpu.make_async_copy(ins[c], outs[c].at[place.t, place.z, place.y, place.x], here.at[c])
        copy.start()
        local.append(copy)
    for step in range(n + 3):
        if step < 5:
            travel.stage(step)
        for c in range(min(step, n - 1), max(step - 3, 0) - 1, -1):
            s = step - c
            if s == 1:
                local[c].wait()
            for part in parts[c]:
                part.stage(s)
    mem_out[...] = held[3]
    own.wait()
    crossing.wait_recv()
    for pair in parts:
        for part in pair:
            part.whole()
    wire.drain()


def gather(keep, bias, payload, shards, cid):
    n = len(shards)
    count = 18 * n + 5
    hbm, vmem = pl.BlockSpec(memory_space=pl.ANY), pl.BlockSpec(memory_space=pltpu.VMEM)
    outs = pl.pallas_call(
        functools.partial(gather_kernel, n),
        out_shape=[jax.ShapeDtypeStruct((2, *GRID, *s.shape), s.dtype) for s in shards]
        + [jax.ShapeDtypeStruct((2, *bias.shape), bias.dtype), jax.ShapeDtypeStruct(payload.shape, payload.dtype)],
        in_specs=[pl.BlockSpec(memory_space=pltpu.SMEM), vmem, vmem] + [hbm] * n,
        out_specs=[hbm] * n + [vmem, vmem],
        scratch_shapes=[
            pltpu.VMEM((4, *payload.shape), payload.dtype), pltpu.VMEM((4, *payload.shape), payload.dtype),
            pltpu.SemaphoreType.DMA((count,)), pltpu.SemaphoreType.DMA((count,)), pltpu.SemaphoreType.DMA((n + 1,))],
        compiler_params=pltpu.CompilerParams(collective_id=cid, has_side_effects=True, vmem_limit_bytes=16 << 20),
    )(keep, bias, payload, *shards)
    return outs[:n], outs[n], outs[n + 1]


class Scatter:
    def __init__(self, wire, place, acc, out, cols, order, landings):
        self.wire, self.p, self.acc, self.out = wire, place, acc, out
        self.cols, self.order, self.landed = cols, order, []
        self.r1, self.r2, self.r3 = landings

    def view(self, z, y, x):
        return self.acc.at[z, y, x, :, self.cols]

    def add(self, z, y, x, *terms):
        total = self.acc[z, y, x, :, self.cols].astype(jnp.float32)
        for term in terms:
            total = total + term.astype(jnp.float32)
        self.acc[z, y, x, :, self.cols] = total.astype(self.acc.dtype)

    def finish(self, *terms):
        p = self.p
        total = self.acc[p.z, p.y, p.x, :, self.cols].astype(jnp.float32)
        for term in terms:
            total = total + term.astype(jnp.float32)
        self.out[:, self.cols] = total

    def stage(self, s):
        p, everything = self.p, slice(None)
        for copy in self.landed:
            copy.wait_recv()
        self.landed = []
        r1, r2, r3 = self.r1, self.r2, self.r3
        if self.order == "yxz":
            if s == 1:
                for z in range(4):
                    for x in range(2):
                        self.add(z, p.y, x, r1[z, x])
            elif s == 2:
                for z in range(4):
                    self.add(z, p.y, p.x, r2[z])
            elif s == 3:
                self.finish(r3[0], r3[1], r3[2])
            if s == 0:
                self.go(self.view(everything, 1 - p.y, everything), r1, p.py)
            elif s == 1:
                self.go(self.view(everything, p.y, 1 - p.x), r2, p.px)
            elif s == 2:
                for k in range(3):
                    self.go(self.view(p.zs[k], p.y, p.x), r3.at[k], p.pz[k])
        else:
            if s == 1:
                for z in range(4):
                    for y in range(2):
                        self.add(z, y, p.x, r1[z, y])
            elif s == 2:
                for y in range(2):
                    self.add(p.z, y, p.x, r2[0, y], r2[1, y], r2[2, y])
            elif s == 3:
                self.finish(r3[...])
            if s == 0:
                self.go(self.view(everything, everything, 1 - p.x), r1, p.px)
            elif s == 1:
                for k in range(3):
                    self.go(self.view(p.zs[k], everything, p.x), r2.at[k], p.pz[k])
            elif s == 2:
                self.go(self.view(p.z, 1 - p.y, p.x), r3, p.py)

    def go(self, src, landing, device):
        self.landed.append(self.wire.start(src, landing, device, landing))


def scatter_shapes(rows, width, dtype):
    cut = first_part(width)
    rest = width - cut
    return [
        pltpu.VMEM((4, 2, rows, cut), dtype), pltpu.VMEM((3, 2, rows, cut), dtype), pltpu.VMEM((rows, cut), dtype),
        pltpu.VMEM((4, 2, rows, rest), dtype), pltpu.VMEM((4, rows, rest), dtype), pltpu.VMEM((3, rows, rest), dtype),
    ]


def scatter_kernel(n, *refs):
    keep, payload, y, dx, vec = refs[:5]
    ins = refs[5:5 + n]
    mem_out, y_out, dx_out, vec_out = refs[5 + n:9 + n]
    outs = refs[9 + n:9 + 2 * n]
    at = 9 + 2 * n
    accs, others = refs[at:at + n], refs[at + n:at + 2 * n]
    landings = refs[at + 2 * n:at + 8 * n]
    held, landing, vc, v0, v1, v2, vx, vy, vz, send, recv, here = refs[at + 8 * n:]
    place = Place()
    wire = Wire(send, recv)
    local, crossing = [], []
    for c in range(n):
        copy = pltpu.make_async_copy(ins[c].at[place.t], accs[c], here.at[c])
        copy.start()
        local.append(copy)
    greet([place.px, place.py, *place.pz, place.pc])
    for c in range(n):
        crossing.append(wire.start(ins[c].at[1 - place.t], others[c], place.pc, others[c]))
    ends = [wire.start(a, o.at[place.t], place.pc, o.at[1 - place.t]) for a, o in ((y, y_out), (dx, dx_out))]
    for k, (a, o) in enumerate(((y, y_out), (dx, dx_out))):
        copy = pltpu.make_async_copy(a, o.at[place.t], here.at[n + k])
        copy.start()
        local.append(copy)
    parts = []
    for c in range(n):
        width = outs[c].shape[1]
        cut = first_part(width)
        parts.append([
            Scatter(wire, place, accs[c], outs[c], slice(0, cut), "xzy", landings[6 * c:6 * c + 3]),
            Scatter(wire, place, accs[c], outs[c], slice(cut, width), "yxz", landings[6 * c + 3:6 * c + 6]),
        ])
    travel = Travel(wire, place, keep, payload, held, landing, (0, 1, 2, 3))
    total = Total(wire, place, vec, vec_out, vc, v0, v1, v2, vx, vy, vz)
    for step in range(n + 3):
        for c in range(min(step, n - 1), max(step - 3, 0) - 1, -1):
            s = step - c
            if s == 0:
                local[c].wait()
                crossing[c].wait_recv()

                def together(z, carry, c=c):
                    accs[c][z] = (accs[c][z].astype(jnp.float32) + others[c][z].astype(jnp.float32)).astype(accs[c].dtype)
                    return carry

                lax.fori_loop(0, 4, together, 0)
            for part in parts[c]:
                part.stage(s)
        if step < 5:
            travel.stage(step)
            total.stage(step)
    mem_out[place.t] = held[3]
    last = wire.start(held.at[3], mem_out.at[place.t], place.pc, mem_out.at[1 - place.t])
    for copy in [last, *ends]:
        copy.wait_recv()
    for copy in local[n:]:
        copy.wait()
    wire.drain()


class Total:
    def __init__(self, wire, place, vec, out, vc, v0, v1, v2, vx, vy, vz):
        self.wire, self.p, self.landed = wire, place, []
        self.vec, self.out, self.vc, self.v0, self.v1, self.v2 = vec, out, vc, v0, v1, v2
        self.vx, self.vy, self.vz = vx, vy, vz

    def stage(self, s):
        p = self.p
        for copy in self.landed:
            copy.wait_recv()
        self.landed = []
        if s == 0:
            self.go(self.vec, self.vc, p.pc)
        elif s == 1:
            self.v0[...] = self.vec[...] + self.vc[...]
            self.go(self.v0, self.vx, p.px)
        elif s == 2:
            self.v1[...] = self.v0[...] + self.vx[...]
            self.go(self.v1, self.vy, p.py)
        elif s == 3:
            self.v2[...] = self.v1[...] + self.vy[...]
            for k in range(3):
                self.go(self.v2, self.vz.at[k], p.pz[k])
        else:
            self.out[...] = self.v2[...] + self.vz[0] + self.vz[1] + self.vz[2]

    def go(self, src, landing, device):
        self.landed.append(self.wire.start(src, landing, device, landing))


def scatter(keep, payload, y, dx, vec, grads, cid):
    n = len(grads)
    rows = grads[0].shape[4]
    count = 11 * n + 14
    shapes = [pltpu.VMEM(g.shape[1:], g.dtype) for g in grads] * 2
    for g in grads:
        shapes += scatter_shapes(rows, g.shape[5], g.dtype)
    flat = pltpu.VMEM(vec.shape, jnp.float32)
    shapes += [pltpu.VMEM((4, *payload.shape), payload.dtype)] * 2
    shapes += [flat] * 6 + [pltpu.VMEM((3, *vec.shape), jnp.float32)]
    shapes += [pltpu.SemaphoreType.DMA((count,)), pltpu.SemaphoreType.DMA((count,)), pltpu.SemaphoreType.DMA((n + 2,))]
    hbm, vmem = pl.BlockSpec(memory_space=pl.ANY), pl.BlockSpec(memory_space=pltpu.VMEM)
    outs = pl.pallas_call(
        functools.partial(scatter_kernel, n),
        out_shape=[jax.ShapeDtypeStruct((2, *payload.shape), payload.dtype), jax.ShapeDtypeStruct((2, *y.shape), y.dtype),
                   jax.ShapeDtypeStruct((2, *dx.shape), dx.dtype), jax.ShapeDtypeStruct(vec.shape, jnp.float32)]
        + [jax.ShapeDtypeStruct((rows, g.shape[5]), jnp.float32) for g in grads],
        in_specs=[pl.BlockSpec(memory_space=pltpu.SMEM), vmem, hbm, hbm, vmem] + [hbm] * n,
        out_specs=[vmem, hbm, hbm] + [vmem] * (n + 1),
        scratch_shapes=shapes,
        compiler_params=pltpu.CompilerParams(collective_id=cid, has_side_effects=True, vmem_limit_bytes=48 << 20),
    )(keep, payload, y, dx, vec, *grads)
    return outs


def keep_flags(orders, device, levels):
    sources = jnp.arange(orders.shape[1], dtype=jnp.int32)
    holders = [jnp.full((orders.shape[0],), device, jnp.int32)]
    for bit in range(levels):
        stride = 2 ** (bit + 1)
        position = sources - sources % stride + orders % stride
        holders.append(jnp.sum(jnp.where(position == device, sources, 0), 1))
    return jnp.stack([a == b for a, b in zip(holders[:-1], holders[1:])], 1).astype(jnp.int32)


def valid_counts(lengths, index, seg_len):
    counts = (lengths + seg_len - 1) // seg_len
    place = jnp.arange(lengths.shape[0])
    ends = jnp.sum(jnp.where(place[None, :] <= place[:, None], counts[None, :], 0), 1)
    starts = ends - counts
    at = index[:, None]
    remain = lengths - (at - starts) * seg_len
    return jnp.sum(jnp.where((starts <= at) & (at < ends), jnp.minimum(remain, seg_len), 0), 1).astype(jnp.int32)


def plain_travel(keep, payload, order):
    size = lax.axis_size("dp")
    for bit in order:
        theirs = lax.ppermute(payload, "dp", [(i, i ^ 1 << bit) for i in range(size)])
        payload = jnp.where(keep[:, bit][:, None, None] > 0, payload, theirs)
    return payload


def both_cores(value):
    return lax.all_gather(value, "tensor", axis=0)


def plain_gather(keep, bias, payload, shards):
    payload = plain_travel(keep, payload, range(keep.shape[1] - 1, -1, -1))
    return [both_cores(lax.all_gather(s, "dp", axis=0, tiled=True)) for s in shards], both_cores(bias), payload


def plain_scatter(keep, payload, y, dx, vec, grads):
    payload = plain_travel(keep, payload, range(keep.shape[1]))
    parts = []
    for g in grads:
        g = lax.psum_scatter(g.astype(jnp.float32), "tensor", scatter_dimension=0)
        parts.append(lax.psum_scatter(g, "dp", scatter_dimension=0, tiled=True))
    return [both_cores(payload), both_cores(y), both_cores(dx), lax.psum(vec, ("dp", "tensor")), *parts]


def local(
    tokens, memory, lengths, owners, w_query, w_key, w_value, w_out, w_up, w_down, b_query, b_value, b_up,
    b_out, b_down, gain_attn, shift_attn, gain_ffn, shift_ffn, cot_tokens, cot_memory,
):
    micro, seg_len, depth = tokens.shape
    mem = memory.shape[1]
    size = lax.axis_size("dp")
    levels = size.bit_length() - 1
    device, t = lax.axis_index("dp"), lax.axis_index("tensor")
    mine = micro // 2
    kernels = size == math.prod(GRID)
    rows, width = w_query.shape
    hidden = w_up.shape[1]

    def own(array):
        return lax.dynamic_slice_in_dim(array, t * mine, mine, 0)

    keep = keep_flags(own(owners), device, levels)
    counts = valid_counts(lengths, device * micro + t * mine + jnp.arange(mine), seg_len)
    payload = jnp.pad(jnp.concatenate([own(memory), own(cot_memory)], 1), ((0, 0), (0, 8), (0, 0)))
    vectors = (b_out, b_down, gain_attn, shift_attn, gain_ffn, shift_ffn)
    columns = jnp.pad(jnp.stack(vectors, 1), ((0, 0), (0, 128 - len(vectors))))
    shards = [jnp.concatenate([w_query, w_key, w_value], 1), jnp.concatenate([w_out, columns], 1), w_up, w_down]
    bias = jnp.concatenate([b_query, b_value, b_up]).astype(jnp.float32)
    bias = jnp.broadcast_to(bias[None], (8, bias.shape[0]))
    if kernels:
        whole, bias, payload = gather(keep, bias, payload, shards, 1)
    else:
        whole, bias, payload = plain_gather(keep, bias, payload, shards)
    qkv, out, up, down = (w.reshape(2, -1, w.shape[-1]) for w in whole)
    vec = jnp.pad(out[0, :, width:width + 8].T.astype(jnp.float32), ((0, 0), (0, 0)))
    bias_qv = jnp.stack([bias[:, 0, :width], bias[:, 0, width:2 * width]], 1)
    bias_qv = jnp.pad(bias_qv, ((0, 0), (0, 6), (0, 0)))
    bias_up = bias[:, :, 2 * width:]

    def lay(array, ends):
        gap = jnp.zeros((mine, TOK - seg_len, depth), array.dtype)
        tail = jnp.zeros((mine, ROWS - TOK - mem, depth), array.dtype)
        return jnp.concatenate([own(array), gap, ends, tail], 1).reshape(mine * ROWS, depth)

    x = lay(tokens, payload[:, :mem])
    cot = lay(cot_tokens, payload[:, mem:2 * mem])
    q, k, v, e, o, linv = forward(counts, x, qkv, bias_qv, mem)
    y, g_down, g_up, g_out, do, dh, sums, sum_up = middle(counts, x, o, cot, vec, bias_up, out, up, down, width, mem)
    dx, g_qkv, sum_qv = backward(x, q, k, v, e, o, linv, do, dh, qkv)

    def ends_of(array):
        return array.reshape(mine, ROWS, depth)[:, TOK:TOK + mem]

    payload = jnp.pad(jnp.concatenate([ends_of(y), ends_of(dx)], 1), ((0, 0), (0, 8), (0, 0)))
    flat = jnp.concatenate([sums[:6].reshape(-1), sum_qv[:, :2].reshape(-1), sum_up[:, 0].reshape(-1)])
    flat = jnp.pad(flat, (0, -flat.shape[0] % (8 * depth))).reshape(-1, depth)
    grads = [g_down, g_up, g_out, g_qkv]
    if kernels:
        grads = [g.reshape(2, *GRID, rows, g.shape[-1]) for g in grads]
        payload, y, dx, flat, g_down, g_up, g_out, g_qkv = scatter(keep, payload, y, dx, flat, grads, 2)
    else:
        payload, y, dx, flat, g_down, g_up, g_out, g_qkv = plain_scatter(keep, payload, y, dx, flat, grads)
    payload = payload.reshape(micro, -1, depth)
    out_tokens = y.reshape(micro, ROWS, depth)[:, :seg_len]
    grad_tokens = dx.reshape(micro, ROWS, depth)[:, :seg_len]
    flat = flat.reshape(-1)
    at = 6 * depth
    vectors = lax.dynamic_slice(flat[:at].reshape(6, depth), (0, device * rows), (6, rows))
    qv = lax.dynamic_index_in_dim(flat[at:at + 4 * width].reshape(2, 2, width), t, 0, False)
    at += 4 * width
    up_sum = lax.dynamic_index_in_dim(flat[at:at + 2 * hidden].reshape(2, hidden), t, 0, False)
    return (
        out_tokens, payload[:, :mem], grad_tokens, payload[:, mem:2 * mem],
        g_qkv[:, :width], g_qkv[:, width:2 * width], g_qkv[:, 2 * width:], g_out, g_up, g_down,
        *(vectors[i] for i in range(6)), qv[0], qv[1], up_sum,
    )


def solution(mesh):
    rows, both, split, every = P("dp", None, None), P("dp", "tensor"), P("tensor"), P("dp")
    return jax.shard_map(
        local,
        mesh=mesh,
        in_specs=(rows, rows, P(), P(), *[both] * 6, *[split] * 3, *[every] * 6, rows, rows),
        out_specs=(*[rows] * 4, *[both] * 6, *[every] * 6, *[split] * 3),
        check_vma=False,
    )
```

```python
import functools
import math

import jax
import jax.numpy as jnp
from jax import lax
from jax.experimental import pallas as pl
from jax.experimental.pallas import tpu as pltpu
from jax.sharding import PartitionSpec as P

MESH = pl.DeviceIdType.MESH
GRID = (4, 2, 2)
HEAD = 64
TOK = 512
TAIL = 32
ROWS = TOK + TAIL
PAIR = 128
MEM_ROWS = 48
masked_score = -1000000000.0
epsilon = 1e-05
F32, LOW = jnp.float32, jnp.bfloat16


def dot(a, b, left, right):
    return lax.dot_general(a, b, (((left,), (right,)), ((), ())), preferred_element_type=F32)


def mat(ref, half, cols):
    got = ref[half, ..., cols]
    return got.reshape(-1, got.shape[-1])


def live_at(position, count, mem):
    return (position < count) | ((position >= TOK) & (position < TOK + mem))


def normed(values):
    mean = jnp.mean(values, -1, keepdims=True)
    centered = values - mean
    inv = lax.rsqrt(jnp.mean(centered * centered, -1, keepdims=True) + epsilon)
    return centered * inv, inv


def norm_back(scaled, unit, inv):
    return inv * (scaled - jnp.mean(scaled, -1, keepdims=True) - unit * jnp.mean(scaled * unit, -1, keepdims=True))


def fold(total_ref, row, value):
    total_ref[row:row + 1, :] += jnp.sum(value, 0, keepdims=True)


def picks(rows, cols, shift, first, count):
    r = lax.broadcasted_iota(jnp.int32, (rows, cols), 0)
    c = lax.broadcasted_iota(jnp.int32, (rows, cols), 1)
    return ((r >= first) & (r < first + count) & (c == r - first + shift)).astype(F32).astype(LOW)


def project(x_ref, w_ref, bias_ref, q_ref, k_ref, v_ref, seg, i, pairs):
    wide = 3 * PAIR
    cols = pl.ds(pl.multiple_of(i * wide, PAIR), wide)
    rows = x_ref[pl.ds(pl.multiple_of(seg * ROWS, 32), ROWS), :]
    lane = lax.broadcasted_iota(jnp.int32, (1, PAIR), 1)
    got = dot(rows, jnp.concatenate([mat(w_ref, 0, cols), mat(w_ref, 1, cols)], 1), 1, 0)
    for half in range(2):
        p = half * pairs + i
        at = half * wide
        here = pl.ds(pl.multiple_of(i * PAIR, PAIR), PAIR)
        there = pl.ds(pl.multiple_of((pairs + i) * PAIR, PAIR), PAIR)
        q = (got[:, at:at + PAIR] + bias_ref[half, 0:1, here]) * (1.0 / math.sqrt(HEAD))
        q_ref[seg, p, 0] = jnp.where(lane < HEAD, q, 0.0).astype(LOW)
        q_ref[seg, p, 1] = jnp.where(lane < HEAD, 0.0, q).astype(LOW)
        k_ref[seg, p] = got[:, at + PAIR:at + 2 * PAIR].astype(LOW)
        v_ref[seg, p] = (got[:, at + 2 * PAIR:at + 3 * PAIR] + bias_ref[half, 0:1, there]).astype(LOW)


def attend(q_ref, k_ref, v_ref, o_ref, linv_ref, e_slot, count, mem, seg, p):
    col = lax.broadcasted_iota(jnp.int32, (1, ROWS), 1)
    lane = lax.broadcasted_iota(jnp.int32, (1, PAIR), 1)
    masking = jnp.where(live_at(col, count, mem), 0.0, masked_score)
    keys = k_ref[seg, p]
    values = jnp.concatenate([v_ref[seg, p], jnp.ones((ROWS, PAIR), LOW)], 1)
    got = []
    for j in range(2):
        scores = dot(q_ref[seg, p, j], keys, 1, 1) + masking
        peak = jnp.max(scores, -1, keepdims=True)
        e_slot[j] = jnp.exp(scores - peak).astype(LOW)
        got.append(dot(e_slot[j], values, 1, 0))
    first = lane < HEAD
    linv = 1.0 / jnp.where(first, got[0][:, PAIR:], got[1][:, PAIR:])
    linv_ref[seg, p] = linv
    o_ref[seg, p] = (jnp.where(first, got[0][:, :PAIR], got[1][:, :PAIR]) * linv).astype(LOW)


def attend_back(q_ref, k_ref, v_ref, o_ref, linv_ref, do_ref, e_slot, ds_ref, out_ref, seg, p, half, i):
    lane = lax.broadcasted_iota(jnp.int32, (1, PAIR), 1)
    keys, values = k_ref[seg, p], v_ref[seg, p]
    scaled = do_ref[seg, p].astype(F32) * linv_ref[seg, p]
    product = scaled * o_ref[seg, p].astype(F32)
    dq, dk, dv = [], None, None
    for j in range(2):
        mine = (lane < HEAD) if j == 0 else (lane >= HEAD)
        mine_low = jnp.where(mine, scaled, 0.0).astype(LOW)
        delta = jnp.sum(jnp.where(mine, product, 0.0), -1, keepdims=True)
        gap = dot(mine_low, values, 1, 1) - delta
        ds_ref[j] = (e_slot[j].astype(F32) * gap).astype(LOW)
        dq.append(dot(ds_ref[j], keys, 1, 0))
        one_v = dot(e_slot[j], mine_low, 0, 0)
        one_k = dot(ds_ref[j], q_ref[seg, p, j], 0, 0)
        dv = one_v if dv is None else dv + one_v
        dk = one_k if dk is None else dk + one_k
    rows = pl.ds(pl.multiple_of(seg * ROWS, 32), ROWS)
    dq = jnp.where(lane < HEAD, dq[0], dq[1]) * (1.0 / math.sqrt(HEAD))
    for kind, value in enumerate((dq, dk, dv)):
        out_ref[half, rows, pl.ds(pl.multiple_of((3 * i + kind) * PAIR, PAIR), PAIR)] = value.astype(LOW)


class Place:
    def __init__(self):
        me = lax.axis_index("dp")
        self.t = lax.axis_index("tensor")
        self.x = me % 2
        self.y = (me // 2) % 2
        self.z = me // 4
        self.nt, self.nx, self.ny = 1 - self.t, 1 - self.x, 1 - self.y
        self.px = self.at(self.z, self.y, self.nx)
        self.py = self.at(self.z, self.ny, self.x)
        self.zs = [(self.z + d) % 4 for d in (1, 2, 3)]
        self.zb = [(self.z + 4 - d) % 4 for d in (1, 2, 3)]
        self.pz = [self.at(z, self.y, self.x) for z in self.zs]
        self.pz1 = self.at(self.z + 1 - 2 * (self.z % 2), self.y, self.x)
        self.pz2 = self.at((self.z + 2) % 4, self.y, self.x)
        self.pc = (me, self.nt)

    def at(self, z, y, x):
        return (z * 4 + y * 2 + x, self.t)

    def greet(self):
        barrier = pltpu.get_barrier_semaphore()
        devices = [self.px, self.py, *self.pz, self.pc]
        for device in devices:
            pl.semaphore_signal(barrier, inc=1, device_id=device, device_id_type=MESH)
        pl.semaphore_wait(barrier, len(devices))


class Wire:
    def __init__(self, send, recv):
        self.send, self.recv, self.count, self.open = send, recv, 0, []

    def start(self, src, dst, device, landing):
        k = self.count
        self.count += 1

        def copy(a, b):
            return pltpu.make_async_remote_copy(
                src_ref=a, dst_ref=b, send_sem=self.send.at[k], recv_sem=self.recv.at[k],
                device_id=device, device_id_type=MESH)

        copy(src(), dst()).start()
        self.open.append(lambda: copy(src(), dst()).wait_send())
        return lambda: copy(landing(), landing()).wait_recv()

    def drain(self):
        for wait in self.open:
            wait()
        self.open = []


def first_part(width):
    return {384: 128, 512: 256, 768: 256}[width]


class Gather:
    def __init__(self, wire, place, src, out, src_at, at, width, order):
        self.wire, self.p, self.src, self.out = wire, place, src, out
        self.src_cols, self.cols, self.order, self.landed, self.crossing = pl.ds(src_at, width), pl.ds(at, width), order, [], []

    def view(self, z, y, x, half=None):
        return lambda: self.out.at[self.p.t if half is None else half, z, y, x, :, self.cols]

    def own(self):
        return self.src.at[:, self.src_cols]

    def stage(self, s):
        p, every = self.p, slice(None)
        for wait in self.landed:
            wait()
        self.landed = []
        home = self.view(p.z, p.y, p.x)
        if self.order == "zxy":
            if s == 0:
                for k in range(3):
                    self.go(self.own, home, p.pz[k], self.view(p.zb[k], p.y, p.x))
            elif s == 1:
                self.go(self.view(every, p.y, p.x), None, p.px, self.view(every, p.y, p.nx))
                self.cross(every, p.y, p.x)
            elif s == 2:
                self.go(self.view(every, p.y, every), None, p.py, self.view(every, p.ny, every))
                self.cross(every, p.y, p.nx)
            else:
                self.cross(every, p.ny, every)
        else:
            if s == 0:
                self.go(self.own, home, p.py, self.view(p.z, p.ny, p.x))
            elif s == 1:
                for k in range(3):
                    self.go(self.view(p.z, every, p.x), None, p.pz[k], self.view(p.zb[k], every, p.x))
                self.cross(p.z, every, p.x)
            elif s == 2:
                self.go(self.view(every, every, p.x), None, p.px, self.view(every, every, p.nx))
                for k in range(3):
                    self.cross(p.zb[k], every, p.x)
            else:
                self.cross(every, every, p.nx)

    def go(self, src, dst, device, landing):
        self.landed.append(self.wire.start(src, src if dst is None else dst, device, landing))

    def cross(self, z, y, x):
        mine = self.view(z, y, x)
        self.crossing.append(self.wire.start(mine, mine, self.p.pc, self.view(z, y, x, self.p.nt)))

    def whole(self):
        for wait in self.crossing:
            wait()
        self.crossing = []


class Travel:
    def __init__(self, wire, place, keep, payload, held, landing, order):
        self.wire, self.p, self.keep, self.landed = wire, place, keep, None
        self.held, self.landing, self.order, self.payload = held, landing, order, payload

    def stage(self, s):
        p = self.p
        if s > 0:
            self.landed()
            before = self.payload if s == 1 else self.held.at[s - 2]
            for m in range(self.payload.shape[0]):
                stay = self.keep[m, self.order[s - 1]] > 0
                mine, theirs = before[m].astype(F32), self.landing[s - 1, m].astype(F32)
                self.held[s - 1, m] = jnp.where(stay, mine, theirs).astype(self.held.dtype)
        if s < len(self.order):
            device = [p.px, p.py, p.pz1, p.pz2][self.order[s]]
            land = lambda: self.landing.at[s]
            self.landed = self.wire.start(lambda: self.payload if s == 0 else self.held.at[s - 1], land, device, land)


CHUNKS = ((0, 0, 384), (0, 384, 384), (0, 768, 384), (1, 0, 512), (2, 0, 768), (2, 768, 768), (3, 0, 768), (3, 768, 768))


class Copies:
    def __init__(self, sems):
        self.sems, self.count = sems, 0

    def start(self, src, dst):
        k = self.count
        self.count += 1
        pltpu.make_async_copy(src(), dst(), self.sems.at[k]).start()
        return lambda: pltpu.make_async_copy(src(), dst(), self.sems.at[k]).wait()


def front_kernel(kernels, mem, width, tile, *refs):
    (count_ref, keep_ref, bias_in, payload_in, tok_in, cot_in, wqkv_in, wout_in, wup_in, wdown_in,
     x_out, wqkv_out, q_out, k_out, v_out, o_out, linv_out, e_out, do_out, dh_out, gdown_out, gup_out, gout_out,
     tails_ref, sums_ref, sup_ref,
     wqkv, wout, wup, wdown, bias_ref, held, landing, x_ref, cot_ref, vec_ref, o_ref, dh_ref, low_ref, unit_ref, inv_ref, flip_ref,
     stage_ref, send, recv, here, e_sems, g_sems) = refs
    weights_in, weights = (wqkv_in, wout_in, wup_in, wdown_in), (wqkv, wout, wup, wdown)
    R = 2 * ROWS
    pairs = width // PAIR
    D = x_ref.shape[1]
    hidden = wup.shape[-1]
    copies = Copies(here)
    loads = []
    for s in range(2):
        rows = pl.ds(s * ROWS, TOK)
        loads.append(copies.start(lambda s=s: tok_in.at[s], lambda rows=rows: x_ref.at[rows]))
        loads.append(copies.start(lambda s=s: cot_in.at[s], lambda rows=rows: cot_ref.at[rows]))
    ticks, whole = [], {}
    if kernels:
        place = Place()
        wire = Wire(send, recv)
        place.greet()
        own = [copies.start(lambda c=c: weights_in[c], lambda c=c: weights[c].at[place.t, place.z, place.y, place.x]) for c in range(4)]
        own_bias = copies.start(lambda: bias_in, lambda: bias_ref.at[place.t])
        bias_wait = wire.start(lambda: bias_in, lambda: bias_ref.at[place.t], place.pc, lambda: bias_ref.at[place.nt])
        travel = Travel(wire, place, keep_ref, payload_in, held, landing, (3, 2, 1, 0))
        parts = []
        for c, at, wide in CHUNKS:
            cut = first_part(wide)
            parts.append([
                Gather(wire, place, weights_in[c], weights[c], at, at, cut, "yzx"),
                Gather(wire, place, weights_in[c], weights[c], at + cut, at + cut, wide - cut, "zxy"),
            ])

        def tick(step):
            for c in range(min(step, len(CHUNKS) - 1), max(step - 3, 0) - 1, -1):
                for part in parts[c]:
                    part.stage(step - c)

        def ready(c):
            for part in parts[c]:
                part.whole()

        travel.stage(0)
        tick(0)
        for wait in own:
            wait()
        for step in (1, 2, 3):
            travel.stage(step)
            tick(step)
        travel.stage(4)
        own_bias()
        bias_wait()
        moved = held.at[3]
        last = len(CHUNKS) + 3
    else:
        fetched = [copies.start(lambda c=c: weights_in[c], lambda c=c: weights[c]) for c in range(4)]
        fetched.append(copies.start(lambda: bias_in, lambda: bias_ref))
        for wait in fetched:
            wait()
        moved = payload_in
        tick = ready = lambda step: None
        last = len(CHUNKS) + 3
    for wait in loads:
        wait()
    for s in range(2):
        both = dot(picks(2 * TAIL, MEM_ROWS, 0, 0, mem) + picks(2 * TAIL, MEM_ROWS, mem, TAIL, mem), moved[s], 1, 0).astype(LOW)
        x_ref[s * ROWS + TOK:(s + 1) * ROWS, :] = both[:TAIL]
        cot_ref[s * ROWS + TOK:(s + 1) * ROWS, :] = both[TAIL:]
    saves = [copies.start(lambda: x_ref, lambda: x_out)]

    def attention(q_ref, k_ref, v_ref, linv_ref, slots):
        def e_copy(seg, p, slot):
            return pltpu.make_async_copy(slots.at[slot], e_out.at[seg, p], e_sems.at[slot])

        def step(n, carry):
            i, seg = n // 2, n % 2
            project(x_ref, wqkv, bias_ref, q_ref, k_ref, v_ref, seg, i, pairs)
            count = jnp.where(seg == 0, count_ref[0], count_ref[1])
            for half in range(2):
                @pl.when(n > 0)
                def _():
                    e_copy(seg, half * pairs + i, half).wait()
                attend(q_ref, k_ref, v_ref, o_ref, linv_ref, slots.at[half], count, mem, seg, half * pairs + i)
                e_copy(seg, half * pairs + i, half).start()
                if half == 0:
                    for k in range(6):
                        @pl.when(n == k)
                        def _():
                            tick(4 + k)
            for c in range(1, pairs):
                @pl.when(n == 2 * c - 1)
                def _():
                    ready(c)
            return carry

        ready(0)
        lax.fori_loop(0, 2 * pairs, step, 0)
        done = [copies.start(lambda: a, lambda: b) for a, b in ((wqkv, wqkv_out),)]
        for a, b in ((q_ref, q_out), (k_ref, k_out), (v_ref, v_out), (o_ref, o_out), (linv_ref, linv_out)):
            done.append(copies.start(lambda a=a: a, lambda b=b: b))
        for half in range(2):
            e_copy(0, 0, half).wait()
        for wait in done:
            wait()

    six = (2, 2 * pairs, ROWS, PAIR)
    pl.run_scoped(
        attention, pltpu.VMEM((2, 2 * pairs, 2, ROWS, PAIR), LOW), pltpu.VMEM(six, LOW), pltpu.VMEM(six, LOW),
        pltpu.VMEM(six, F32), pltpu.VMEM((2, 2, ROWS, ROWS), LOW))

    tick(10)
    ready(3)
    sums_ref[...] = jnp.zeros_like(sums_ref)
    vec_ref[...] = mat(wout, 0, slice(width, width + PAIR)).astype(F32).T[:8]
    vec = {n: vec_ref[k:k + 1, :] for k, n in enumerate(("b_out", "b_down", "gain_attn", "shift_attn", "gain_ffn", "shift_ffn"))}

    def out_step(s, carry):
        rows = pl.ds(pl.multiple_of(s * ROWS, ROWS), ROWS)
        h = x_ref[rows, :].astype(F32) + vec["b_out"]
        for t in range(2):
            o = jnp.concatenate([o_ref[s, t * pairs + i] for i in range(pairs)], 1)
            h = h + dot(o, mat(wout, t, slice(0, width)), 1, 1)
        unit, inv = normed(h)
        x1 = unit * vec["gain_attn"] + vec["shift_attn"]
        dh_ref[rows, :] = x1
        low_ref[rows, :] = x1.astype(LOW)
        unit_ref[rows, :] = unit.astype(LOW)
        inv_ref[rows, :] = inv
        return carry

    lax.fori_loop(0, 2, out_step, 0)

    def ffn(g_ref, d_ref):
        steps = hidden // tile
        part = R // 4

        def columns(k):
            return k // steps, pl.ds(pl.multiple_of((k % steps) * tile, tile), tile)

        def up_cols(cols_first, count):
            def up_step(k, carry):
                t = k // count
                cols = pl.ds(pl.multiple_of(cols_first + (k % count) * tile, PAIR), tile)
                u = dot(low_ref[...], mat(wup, t, cols), 1, 0)
                u = u + bias_ref[t, 0:1, pl.ds(pl.multiple_of(2 * width + cols_first + (k % count) * tile, PAIR), tile)]
                phi = 0.5 * (1.0 + lax.erf(u * (1.0 / math.sqrt(2.0))))
                g_ref[t, :, cols] = (u * phi).astype(LOW)
                d_ref[t, :, cols] = (phi + u * (jnp.exp(-0.5 * u * u) * (1.0 / math.sqrt(2.0 * math.pi)))).astype(LOW)
                return carry

            lax.fori_loop(0, 2 * count, up_step, 0)

        ready(4)
        up_cols(0, steps // 2)
        ready(5)
        up_cols(hidden // 2, steps // 2)
        ready(6)
        ready(7)

        def down_step(s, carry):
            rows = pl.ds(pl.multiple_of(s * part, part), part)
            h = dh_ref[rows, :] + vec["b_down"]
            for t in range(2):
                h = h + dot(g_ref[t, rows, :], mat(wdown, t, slice(None)), 1, 1)
            unit, inv = normed(h)
            count = jnp.where(s < 2, count_ref[0], count_ref[1])
            at = lax.broadcasted_iota(jnp.int32, (part, 1), 0) + (s % 2) * part
            live = jnp.where(live_at(at, count, mem), 1.0, 0.0)
            x_ref[rows, :] = ((unit * vec["gain_ffn"] + vec["shift_ffn"]) * live).astype(LOW)
            dy = cot_ref[rows, :].astype(F32) * live
            fold(sums_ref, 4, dy * unit)
            fold(sums_ref, 5, dy)
            dh = norm_back(dy * vec["gain_ffn"], unit, inv)
            fold(sums_ref, 1, dh)
            dh_ref[rows, :] = dh
            cot_ref[rows, :] = dh.astype(LOW)
            return carry

        for wait in saves:
            wait()
        lax.fori_loop(0, 4, down_step, 0)
        flip_ref[...] = cot_ref[...].T

        def g_copy(slot, out, t, cols):
            return pltpu.make_async_copy(stage_ref.at[slot, :, pl.ds(0, tile)], out.at[t, :, cols], g_sems.at[slot])

        def back_step(k, carry):
            t, cols = columns(k)

            @pl.when(k >= 2)
            def _():
                g_copy(k % 2, gdown_out, t, cols).wait()

            stage_ref[k % 2, :, :tile] = dot(flip_ref[...], g_ref[t, :, cols], 1, 0).astype(LOW)
            g_copy(k % 2, gdown_out, t, cols).start()
            du = dot(cot_ref[...], mat(wdown, t, cols), 1, 0) * d_ref[t, :, cols].astype(F32)
            sup_ref[t, 0:1, cols] = jnp.sum(du, 0, keepdims=True)
            d_ref[t, :, cols] = du.astype(LOW)
            return carry

        lax.fori_loop(0, 2 * steps, back_step, 0)
        flip_ref[...] = low_ref[...].T

        def up_back(k, carry):
            t, cols = columns(k)
            g_copy(k % 2, gup_out, t, cols).wait()
            stage_ref[k % 2, :, :tile] = dot(flip_ref[...], d_ref[t, :, cols], 1, 0).astype(LOW)
            g_copy(k % 2, gup_out, t, cols).start()
            return carry

        lax.fori_loop(0, 2 * steps, up_back, 0)

        def in_step(s, carry):
            rows = pl.ds(pl.multiple_of(s * part, part), part)
            dx = dh_ref[rows, :]
            for t in range(2):
                dx = dx + dot(d_ref[t, rows, :], mat(wup, t, slice(None)), 1, 1)
            unit = unit_ref[rows, :].astype(F32)
            fold(sums_ref, 2, dx * unit)
            fold(sums_ref, 3, dx)
            dh = norm_back(dx * vec["gain_attn"], unit, inv_ref[rows, :])
            fold(sums_ref, 0, dh)
            dh_ref[rows, :] = dh
            low_ref[rows, :] = dh.astype(LOW)
            return carry

        lax.fori_loop(0, 4, in_step, 0)
        for slot in range(2):
            g_copy(slot, gup_out, 0, pl.ds(0, tile)).wait()

    pl.run_scoped(ffn, pltpu.VMEM((2, R, hidden), LOW), pltpu.VMEM((2, R, hidden), LOW))
    ends = [copies.start(lambda: dh_ref, lambda: dh_out)]
    flip_ref[...] = low_ref[...].T
    for t in range(2):
        both = jnp.concatenate([jnp.concatenate([o_ref[s, t * pairs + i] for i in range(pairs)], 1) for s in range(2)], 0)
        stage_ref[t, :, :width] = dot(flip_ref[...], both, 1, 0).astype(LOW)
        ends.append(copies.start(lambda t=t: stage_ref.at[t, :, pl.ds(0, width)], lambda t=t: gout_out.at[t]))
    for s in range(2):
        for t in range(2):
            back = dot(low_ref[s * ROWS:(s + 1) * ROWS, :], mat(wout, t, slice(0, width)), 1, 0).astype(LOW)
            for i in range(pairs):
                o_ref[s, t * pairs + i] = back[:, i * PAIR:(i + 1) * PAIR]
    ends.append(copies.start(lambda: o_ref, lambda: do_out))
    ends.append(copies.start(lambda: x_ref, lambda: tails_ref))
    for wait in ends:
        wait()
    if kernels:
        wire.drain()


def front(counts, keep, bias, payload, tok, cot, shards, width, mem, kernels, cid, tile=256):
    D = tok.shape[2]
    R = 2 * ROWS
    hidden = shards[2].shape[-1]
    pairs = width // PAIR
    S = jax.ShapeDtypeStruct
    hbm, vmem, smem = (pl.BlockSpec(memory_space=m) for m in (pl.ANY, pltpu.VMEM, pltpu.SMEM))
    full = (2, *GRID, D // math.prod(GRID)) if kernels else (2, D)
    six = (2, 2 * pairs, ROWS, PAIR)
    V = pltpu.VMEM
    count = 18 * len(CHUNKS) + 5
    params = dict(collective_id=cid, has_side_effects=True) if kernels else {}
    return pl.pallas_call(
        functools.partial(front_kernel, kernels, mem, width, tile),
        out_shape=[
            S((R, D), LOW), S((*full, 3 * width), LOW), S((2, 2 * pairs, 2, ROWS, PAIR), LOW), S(six, LOW), S(six, LOW), S(six, LOW),
            S(six, F32), S((2, 2 * pairs, 2, ROWS, ROWS), LOW), S(six, LOW), S((R, D), F32), S((2, D, hidden), LOW),
            S((2, D, hidden), LOW), S((2, D, width), LOW), S((R, D), LOW), S((8, D), F32), S((2, 8, hidden), F32)],
        in_specs=[smem, smem, vmem, vmem] + [hbm] * 6,
        out_specs=[hbm] * 14 + [vmem] * 2,
        scratch_shapes=[
            V((*full, 3 * width), LOW), V((*full, width + PAIR), LOW), V((*full, hidden), LOW), V((*full, hidden), LOW),
            V((2, 8, 2 * width + hidden), F32), V((4, *payload.shape), LOW), V((4, *payload.shape), LOW),
            V((R, D), LOW), V((R, D), LOW), V((8, D), F32), V(six, LOW), V((R, D), F32), V((R, D), LOW), V((R, D), LOW),
            V((R, 1), F32), V((D, R), LOW), V((2, D, width), LOW),
            pltpu.SemaphoreType.DMA((count,)), pltpu.SemaphoreType.DMA((count,)), pltpu.SemaphoreType.DMA((24,)),
            pltpu.SemaphoreType.DMA((2,)), pltpu.SemaphoreType.DMA((2,))],
        compiler_params=pltpu.CompilerParams(vmem_limit_bytes=63 << 20, **params),
    )(counts, keep, bias, payload, tok, cot, *shards)


def pad_kernel(t_ref, tok_ref, cot_ref, x_ref, c_ref):
    for a, b in ((tok_ref, x_ref), (cot_ref, c_ref)):
        b[0, TOK - 16:, :] = jnp.zeros((16, b.shape[2]), b.dtype)
        b[0, :a.shape[1], :] = a[0]


def padded(t, tokens, cots):
    micro, seg_len, depth = tokens.shape
    took = pl.BlockSpec((1, seg_len, depth), lambda i, t: (2 * t[0] + i, 0, 0))
    gave = pl.BlockSpec((1, TOK, depth), lambda i, t: (i, 0, 0))
    out = jax.ShapeDtypeStruct((2, TOK, depth), tokens.dtype)
    return pl.pallas_call(
        pad_kernel, out_shape=[out, out],
        grid_spec=pltpu.PrefetchScalarGridSpec(num_scalar_prefetch=1, grid=(2,), in_specs=[took, took], out_specs=[gave, gave]),
        compiler_params=pltpu.CompilerParams(vmem_limit_bytes=16 << 20),
    )(t.reshape(1), tokens, cots)


class Scatter:
    def __init__(self, wire, place, acc, out, cols, order, landings):
        self.wire, self.p, self.acc, self.out = wire, place, acc, out
        self.cols, self.order, self.landed = cols, order, []
        self.r1, self.r2, self.r3 = landings

    def view(self, z, y, x):
        return lambda: self.acc.at[z, y, x, :, self.cols]

    def sum(self, z, y, x, terms):
        total = self.acc[z, y, x, :, self.cols].astype(F32)
        for term in terms:
            total = total + term.astype(F32)
        return total

    def add(self, z, y, x, *terms):
        self.acc[z, y, x, :, self.cols] = self.sum(z, y, x, terms).astype(self.acc.dtype)

    def finish(self, *terms):
        self.out[:, self.cols] = self.sum(self.p.z, self.p.y, self.p.x, terms)

    def stage(self, s):
        p, every = self.p, slice(None)
        for wait in self.landed:
            wait()
        self.landed = []
        r1, r2, r3 = self.r1, self.r2, self.r3
        if self.order == "yxz":
            if s == 0:
                self.go(self.view(every, p.ny, every), lambda: r1, p.py)
            elif s == 1:
                for z in range(4):
                    for x in range(2):
                        self.add(z, p.y, x, r1[z, x])
                self.go(self.view(every, p.y, p.nx), lambda: r2, p.px)
            elif s == 2:
                for z in range(4):
                    self.add(z, p.y, p.x, r2[z])
                for k in range(3):
                    self.go(self.view(p.zs[k], p.y, p.x), lambda k=k: r3.at[k], p.pz[k])
            else:
                self.finish(r3[0], r3[1], r3[2])
        else:
            if s == 0:
                self.go(self.view(every, every, p.nx), lambda: r1, p.px)
            elif s == 1:
                for z in range(4):
                    for y in range(2):
                        self.add(z, y, p.x, r1[z, y])
                for k in range(3):
                    self.go(self.view(p.zs[k], every, p.x), lambda k=k: r2.at[k], p.pz[k])
            elif s == 2:
                for y in range(2):
                    self.add(p.z, y, p.x, r2[0, y], r2[1, y], r2[2, y])
                self.go(self.view(p.z, p.ny, p.x), lambda: r3, p.py)
            else:
                self.finish(r3[...])

    def go(self, src, landing, device):
        self.landed.append(self.wire.start(src, landing, device, landing))


def scatter_shapes(rows, wide):
    cut = first_part(wide)
    rest = wide - cut
    V = pltpu.VMEM
    return [V((4, 2, rows, cut), LOW), V((3, 2, rows, cut), LOW), V((rows, cut), LOW),
            V((4, 2, rows, rest), LOW), V((4, rows, rest), LOW), V((3, rows, rest), LOW)]


class Total:
    def __init__(self, wire, place, vec, out, hops, vz):
        self.wire, self.p, self.landed = wire, place, []
        self.vec, self.out, self.hops, self.vz = vec, out, hops, vz

    def stage(self, s):
        p, hops = self.p, self.hops
        for wait in self.landed:
            wait()
        self.landed = []
        if s == 0:
            self.go(lambda: self.vec, lambda: hops.at[0], p.pc)
        elif s < 4:
            hops[2 * s - 1] = (self.vec[...] if s == 1 else hops[2 * s - 3]) + hops[2 * s - 2]
            if s < 3:
                self.go(lambda: hops.at[2 * s - 1], lambda: hops.at[2 * s], (p.px, p.py)[s - 1])
            else:
                for k in range(3):
                    self.go(lambda: hops.at[5], lambda k=k: self.vz.at[k], p.pz[k])
        else:
            self.out[...] = hops[5] + self.vz[0] + self.vz[1] + self.vz[2]

    def go(self, src, landing, device):
        self.landed.append(self.wire.start(src, landing, device, landing))


SUMS = ((0, 0, 768), (0, 768, 768), (1, 0, 768), (1, 768, 768), (2, 0, 384), (3, 0, 384), (3, 384, 384), (3, 768, 384))


def back_kernel(kernels, mem, width, *refs):
    n_land = 6 * len(SUMS)
    (keep_ref, vec_in, x_in, wqkv_in, q_in, k_in, v_in, o_in, linv_in, e_in, do_in, dh_in, y_in, gdown_in, gup_in, gout_in) = refs[:16]
    (y_out, dx_out, mem_out, vec_out, late_out, down_out, up_out, out_out, qkv_out) = refs[16:25]
    (x_ref, wqkv, q_ref, k_ref, v_ref, o_ref, linv_ref, do_ref, dh_ref, slots, ds_ref, out_ref, flip_ref, late_ref,
     tail_ref, payload_ref, held, landing, hops, vz, hops2, vz2,
     acc0, acc1, acc2, acc3, oth0, oth1, oth2, oth3, away) = refs[25:56]
    landings = refs[56:56 + n_land]
    send, recv, here, e_sems = refs[56 + n_land:]
    R = 2 * ROWS
    pairs = width // PAIR
    D = x_ref.shape[1]
    copies = Copies(here)
    order = [(a, b) for a, b in ((do_in, do_ref), (linv_in, linv_ref), (o_in, o_ref), (k_in, k_ref), (v_in, v_ref), (q_in, q_ref))]
    first = [copies.start(lambda a=a: a, lambda b=b: b) for a, b in order]

    def e_copy(seg, p, slot):
        return pltpu.make_async_copy(e_in.at[seg, p], slots.at[slot], e_sems.at[slot])

    e_copy(0, 0, 0).start()
    later = [copies.start(lambda a=a: a, lambda b=b: b) for a, b in ((x_in, x_ref), (wqkv_in, wqkv), (dh_in, dh_ref))]
    tails = [copies.start(lambda s=s: y_in.at[pl.ds(s * ROWS + TOK, TAIL)], lambda s=s: tail_ref.at[s]) for s in range(2)]
    grads_in, accs, others, outs = (gdown_in, gup_in, gout_in), (acc0, acc1, acc2, acc3), (oth0, oth1, oth2, oth3), (down_out, up_out, out_out, qkv_out)
    grid_rows = (4, 2, 2, D // 16)
    if kernels:
        place = Place()
        wire = Wire(send, recv)
        place.greet()
        fetched = [copies.start(lambda c=c: grads_in[c].at[place.t], lambda c=c: accs[c]) for c in range(3)]
        crossed = []
        for c, at, wide in SUMS[:5]:
            cols = pl.ds(at, wide)
            crossed.append(wire.start(lambda c=c, cols=cols: grads_in[c].at[place.nt, :, :, :, :, cols],
                                      lambda c=c, cols=cols: others[c].at[:, :, :, :, cols], place.pc,
                                      lambda c=c, cols=cols: others[c].at[:, :, :, :, cols]))
        y_wait = wire.start(lambda: y_in, lambda: y_out.at[place.t], place.pc, lambda: y_out.at[place.nt])
        y_own = copies.start(lambda: y_in, lambda: y_out.at[place.t])
        total = Total(wire, place, vec_in, vec_out, hops, vz)
        parts = []
        for n, (c, at, wide) in enumerate(SUMS):
            cut = first_part(wide)
            parts.append([
                Scatter(wire, place, accs[c], outs[c], slice(at, at + cut), "xzy", landings[6 * n:6 * n + 3]),
                Scatter(wire, place, accs[c], outs[c], slice(at + cut, at + wide), "yxz", landings[6 * n + 3:6 * n + 6]),
            ])

        def tick(step):
            for n in range(min(step, len(SUMS) - 1), max(step - 3, 0) - 1, -1):
                if n == step:
                    c, at, wide = SUMS[n]
                    if at == 0 and c < 3:
                        fetched[c]()
                    crossed[n]()
                    cols = slice(at, at + wide)

                    def together(z, carry):
                        mine = accs[c][z, :, :, :, cols].astype(F32) + others[c][z, :, :, :, cols].astype(F32)
                        accs[c][z, :, :, :, cols] = mine.astype(LOW)
                        return carry

                    lax.fori_loop(0, 4, together, 0)
                for part in parts[n]:
                    part.stage(step - n)
            if step < 5:
                total.stage(step)
    else:
        tick = lambda step: None
        y_own = copies.start(lambda: y_in, lambda: y_out)
        vec_out[...] = vec_in[...]
    for wait in first:
        wait()

    def gradients(i):
        wide = 3 * PAIR
        cols = pl.ds(i * wide, wide)
        for t in range(2):
            got = dot(flip_ref[...], out_ref[t, :, cols], 1, 0).astype(LOW)
            if kernels:
                @pl.when(place.t == t)
                def _():
                    acc3[:, :, :, :, cols] = got.reshape(*grid_rows, wide)

                @pl.when(place.t != t)
                def _():
                    away[i] = got.reshape(*grid_rows, wide)
            else:
                qkv_out[t, :, cols] = got
            late_ref[t, i:i + 1, :] = jnp.sum(out_ref[t, :, cols].astype(F32), 0, keepdims=True)
        if kernels:
            land = lambda: oth3.at[:, :, :, :, cols]
            crossed.append(wire.start(lambda: away.at[i], land, place.pc, land))

    def step(n, carry):
        i, seg = n // 2, n % 2
        for k in range(6):
            @pl.when(n == k)
            def _():
                if k == 2:
                    later[0]()
                    flip_ref[...] = x_ref[...].T
                if k in (2, 4):
                    gradients(k // 2 - 1)
                tick(k)
        for half in range(2):
            slot = half
            e_copy(seg, half * pairs + i, slot).wait()
            if half == 0:
                e_copy(seg, pairs + i, 1).start()
            else:
                @pl.when(n < 2 * pairs - 1)
                def _():
                    e_copy((n + 1) % 2, (n + 1) // 2, 0).start()
            attend_back(q_ref, k_ref, v_ref, o_ref, linv_ref, do_ref, slots.at[slot], ds_ref, out_ref, seg, half * pairs + i, half, i)
        return carry

    late_ref[...] = jnp.zeros_like(late_ref)
    lax.fori_loop(0, 2 * pairs, step, 0)
    gradients(pairs - 1)
    if kernels:
        late = Total(wire, place, late_ref, late_out, hops2, vz2)
        late.stage(0)
    tick(6)
    for wait in later[1:] + tails:
        wait()
    part = R // 4

    def in_step(s, carry):
        rows = pl.ds(pl.multiple_of(s * part, part), part)
        dx = dh_ref[rows, :]
        for t in range(2):
            dx = dx + dot(out_ref[t, rows, :], mat(wqkv, t, slice(None)), 1, 1)
        x_ref[rows, :] = dx.astype(LOW)
        return carry

    lax.fori_loop(0, 4, in_step, 0)
    for s in range(2):
        ends = x_ref[s * ROWS + TOK:(s + 1) * ROWS, :]
        both = dot(picks(MEM_ROWS, TAIL, 0, 0, mem), tail_ref[s], 1, 0) + dot(picks(MEM_ROWS, TAIL, 0, mem, mem), ends, 1, 0)
        payload_ref[s] = both.astype(LOW)
    if kernels:
        x_wait = wire.start(lambda: x_ref, lambda: dx_out.at[place.t], place.pc, lambda: dx_out.at[place.nt])
        x_own = copies.start(lambda: x_ref, lambda: dx_out.at[place.t])
        travel = Travel(wire, place, keep_ref, payload_ref, held, landing, (0, 1, 2, 3))
        for k in range(5):
            travel.stage(k)
            if k < 4:
                tick(7 + k)
                late.stage(k + 1)
        mem_out[place.t] = held[3]
        m_wait = wire.start(lambda: held.at[3], lambda: mem_out.at[place.t], place.pc, lambda: mem_out.at[place.nt])
        for wait in (y_wait, x_wait, m_wait, x_own):
            wait()
        wire.drain()
    else:
        x_own = copies.start(lambda: x_ref, lambda: dx_out)
        x_own()
        mem_out[...] = payload_ref[...]
        late_out[...] = late_ref[...]
        for c in range(3):
            copies.start(lambda: grads_in[c], lambda: outs[c])()
    y_own()


def back(keep, vec, front_outs, width, mem, rows, kernels, cid):
    x, wqkv, q, k, v, o, linv, e, do, dh, gdown, gup, gout, y = front_outs
    R, D = x.shape
    pairs = width // PAIR
    hidden = gdown.shape[-1]
    S, V = jax.ShapeDtypeStruct, pltpu.VMEM
    hbm, vmem, smem = (pl.BlockSpec(memory_space=m) for m in (pl.ANY, pltpu.VMEM, pltpu.SMEM))
    widths = (hidden, hidden, width, 3 * width)
    grid = (*GRID, D // math.prod(GRID))
    if kernels:
        gdown, gup, gout = (g.reshape(2, *grid, g.shape[-1]) for g in (gdown, gup, gout))
        sums = [S((rows, w), F32) for w in widths]
        specs = [vmem] * 4
        two = (2,)
        params = dict(collective_id=cid, has_side_effects=True)
        accs = [V((*grid, w), LOW) for w in widths] * 2 + [V((pairs, *grid, 3 * PAIR), LOW)]
        landings = [s for _, _, wide in SUMS for s in scatter_shapes(rows, wide)]
    else:
        sums = [S((2, D, w), LOW) for w in widths]
        specs = [hbm] * 3 + [vmem]
        two = ()
        params = {}
        accs = [V((8, 128), LOW)] * 9
        landings = [V((8, 128), LOW)] * (6 * len(SUMS))
    six = (2, 2 * pairs, ROWS, PAIR)
    payload = (2, MEM_ROWS, D)
    late = (2, 8, 3 * PAIR)
    count = 11 * len(SUMS) + 20
    return pl.pallas_call(
        functools.partial(back_kernel, kernels, mem, width),
        out_shape=[S((*two, R, D), LOW), S((*two, R, D), LOW), S((*two, *payload), LOW), S(vec.shape, F32), S(late, F32), *sums],
        in_specs=[smem, vmem] + [hbm] * 14,
        out_specs=[hbm, hbm, vmem, vmem, vmem, *specs],
        scratch_shapes=[
            V((R, D), LOW), V(wqkv.shape, LOW), V((2, 2 * pairs, 2, ROWS, PAIR), LOW), V(six, LOW), V(six, LOW), V(six, LOW), V(six, F32),
            V(six, LOW), V((R, D), F32), V((2, 2, ROWS, ROWS), LOW), V((2, ROWS, ROWS), LOW), V((2, R, 3 * width), LOW), V((D, R), LOW),
            V(late, F32), V((2, TAIL, D), LOW), V(payload, LOW), V((4, *payload), LOW), V((4, *payload), LOW),
            V((6, *vec.shape), F32), V((3, *vec.shape), F32), V((6, *late), F32), V((3, *late), F32),
            *accs, *landings,
            pltpu.SemaphoreType.DMA((count,)), pltpu.SemaphoreType.DMA((count,)), pltpu.SemaphoreType.DMA((24,)), pltpu.SemaphoreType.DMA((2,))],
        compiler_params=pltpu.CompilerParams(vmem_limit_bytes=63 << 20, **params),
    )(keep, vec, x, wqkv, q, k, v, o, linv, e, do, dh, y, gdown, gup, gout)


def keep_flags(orders, device, levels):
    sources = jnp.arange(orders.shape[1], dtype=jnp.int32)
    holders = [jnp.full((orders.shape[0],), device, jnp.int32)]
    for bit in range(levels):
        stride = 2 ** (bit + 1)
        position = sources - sources % stride + orders % stride
        holders.append(jnp.sum(jnp.where(position == device, sources, 0), 1))
    return jnp.stack([a == b for a, b in zip(holders[:-1], holders[1:])], 1).astype(jnp.int32)


def valid_counts(lengths, index, seg_len):
    counts = (lengths + seg_len - 1) // seg_len
    place = jnp.arange(lengths.shape[0])
    ends = jnp.sum(jnp.where(place[None, :] <= place[:, None], counts[None, :], 0), 1)
    starts = ends - counts
    at = index[:, None]
    remain = lengths - (at - starts) * seg_len
    return jnp.sum(jnp.where((starts <= at) & (at < ends), jnp.minimum(remain, seg_len), 0), 1).astype(jnp.int32)


def plain_travel(keep, payload, order):
    size = lax.axis_size("dp")
    for bit in order:
        theirs = lax.ppermute(payload, "dp", [(i, i ^ 1 << bit) for i in range(size)])
        payload = jnp.where(keep[:, bit][:, None, None] > 0, payload, theirs)
    return payload


def both_cores(value):
    return lax.all_gather(value, "tensor", axis=0)


def plain_gather(keep, bias, payload, shards):
    payload = plain_travel(keep, payload, range(keep.shape[1] - 1, -1, -1))
    return [both_cores(lax.all_gather(s, "dp", axis=0, tiled=True)) for s in shards], both_cores(bias), payload


def plain_scatter(keep, outs):
    y, dx, payload, vec, late, *grads = outs
    payload = plain_travel(keep, payload, range(keep.shape[1]))
    parts = []
    for g in grads:
        g = lax.psum_scatter(g.astype(F32), "tensor", scatter_dimension=0)
        parts.append(lax.psum_scatter(g, "dp", scatter_dimension=0, tiled=True))
    everywhere = ("dp", "tensor")
    return [both_cores(y), both_cores(dx), both_cores(payload), lax.psum(vec, everywhere), lax.psum(late, everywhere), *parts]


def local(
    tokens, memory, lengths, owners, w_query, w_key, w_value, w_out, w_up, w_down, b_query, b_value, b_up,
    b_out, b_down, gain_attn, shift_attn, gain_ffn, shift_ffn, cot_tokens, cot_memory,
):
    micro, seg_len, depth = tokens.shape
    mem = memory.shape[1]
    size = lax.axis_size("dp")
    levels = size.bit_length() - 1
    device, t = lax.axis_index("dp"), lax.axis_index("tensor")
    mine = micro // 2
    kernels = size == math.prod(GRID)
    rows, width = w_query.shape
    hidden = w_up.shape[1]

    def own(array):
        return lax.dynamic_slice_in_dim(array, t * mine, mine, 0)

    keep = keep_flags(own(owners), device, levels)
    counts = valid_counts(lengths, device * micro + t * mine + jnp.arange(mine), seg_len)
    payload = jnp.pad(jnp.concatenate([own(memory), own(cot_memory)], 1), ((0, 0), (0, MEM_ROWS - 2 * mem), (0, 0)))
    vectors = (b_out, b_down, gain_attn, shift_attn, gain_ffn, shift_ffn)
    columns = jnp.pad(jnp.stack(vectors, 1), ((0, 0), (0, PAIR - len(vectors))))
    pairs = width // PAIR
    by_pair = jnp.concatenate([w[:, i * PAIR:(i + 1) * PAIR] for i in range(pairs) for w in (w_query, w_key, w_value)], 1)
    shards = [by_pair, jnp.concatenate([w_out, columns], 1), w_up, w_down]
    bias = jnp.concatenate([b_query, b_value, b_up]).astype(F32)
    bias = jnp.broadcast_to(bias[None], (8, bias.shape[0]))
    if not kernels:
        shards, bias, payload = plain_gather(keep, bias, payload, shards)
    tok, cot = padded(t, tokens, cot_tokens)
    *kept, sums, sum_up = front(counts, keep, bias, payload, tok, cot, shards, width, mem, kernels, 1)
    flat = jnp.concatenate([sums[:6].reshape(-1), sum_up[:, 0].reshape(-1)])
    flat = jnp.pad(flat, (0, -flat.shape[0] % (8 * depth))).reshape(-1, depth)
    outs = back(keep, flat, kept, width, mem, rows, kernels, 2)
    if not kernels:
        outs = plain_scatter(keep, outs)
    y, dx, payload, flat, late, g_down, g_up, g_out, g_qkv = outs
    payload = payload.reshape(micro, -1, depth)
    out_tokens = y.reshape(micro, ROWS, depth)[:, :seg_len]
    grad_tokens = dx.reshape(micro, ROWS, depth)[:, :seg_len]
    flat = flat.reshape(-1)
    at = 6 * depth
    vectors = lax.dynamic_slice(flat[:at].reshape(6, depth), (0, device * rows), (6, rows))
    up_sum = lax.dynamic_index_in_dim(flat[at:at + 2 * hidden].reshape(2, hidden), t, 0, False)
    late = lax.dynamic_index_in_dim(late, t, 0, False)[:pairs].reshape(pairs, 3, PAIR)
    g_qkv = g_qkv.reshape(rows, pairs, 3, PAIR)
    return (
        out_tokens, payload[:, :mem], grad_tokens, payload[:, mem:2 * mem],
        *(g_qkv[:, :, k].reshape(rows, width) for k in range(3)), g_out, g_up, g_down,
        *(vectors[i] for i in range(6)), late[:, 0].reshape(width), late[:, 2].reshape(width), up_sum,
    )


def solution(mesh):
    rows, both, split, every = P("dp", None, None), P("dp", "tensor"), P("tensor"), P("dp")
    return jax.shard_map(
        local,
        mesh=mesh,
        in_specs=(rows, rows, P(), P(), *[both] * 6, *[split] * 3, *[every] * 6, rows, rows),
        out_specs=(*[rows] * 4, *[both] * 6, *[every] * 6, *[split] * 3),
        check_vma=False,
    )
```

```python
import functools
import math

import jax
import jax.numpy as jnp
from jax import lax
from jax.experimental import pallas as pl
from jax.experimental.pallas import tpu as pltpu
from jax.sharding import PartitionSpec as P

MESH = pl.DeviceIdType.MESH
GRID = (4, 2, 2)
HEAD = 64
TOK = 512
TAIL = 32
ROWS = TOK + TAIL
PAIR = 128
MEM_ROWS = 48
masked_score = -1000000000.0
epsilon = 1e-05
F32, LOW = jnp.float32, jnp.bfloat16


def dot(a, b, left, right):
    return lax.dot_general(a, b, (((left,), (right,)), ((), ())), preferred_element_type=F32)


def mat(ref, half, cols):
    got = ref[half, ..., cols]
    return got.reshape(-1, got.shape[-1])


def live_at(position, count, mem):
    return (position < count) | ((position >= TOK) & (position < TOK + mem))


def normed(values):
    mean = jnp.mean(values, -1, keepdims=True)
    centered = values - mean
    inv = lax.rsqrt(jnp.mean(centered * centered, -1, keepdims=True) + epsilon)
    return centered * inv, inv


def norm_back(scaled, unit, inv):
    return inv * (scaled - jnp.mean(scaled, -1, keepdims=True) - unit * jnp.mean(scaled * unit, -1, keepdims=True))


def fold(total_ref, row, value):
    total_ref[row:row + 1, :] += jnp.sum(value, 0, keepdims=True)


def picks(rows, cols, shift, first, count):
    r = lax.broadcasted_iota(jnp.int32, (rows, cols), 0)
    c = lax.broadcasted_iota(jnp.int32, (rows, cols), 1)
    return ((r >= first) & (r < first + count) & (c == r - first + shift)).astype(F32).astype(LOW)


def project(x_ref, w_ref, bias_ref, q_ref, k_ref, v_ref, seg, i, pairs):
    wide = 3 * PAIR
    cols = pl.ds(pl.multiple_of(i * wide, PAIR), wide)
    rows = x_ref[pl.ds(pl.multiple_of(seg * ROWS, 32), ROWS), :]
    lane = lax.broadcasted_iota(jnp.int32, (1, PAIR), 1)
    got = dot(rows, jnp.concatenate([mat(w_ref, 0, cols), mat(w_ref, 1, cols)], 1), 1, 0)
    for half in range(2):
        p = half * pairs + i
        at = half * wide
        here = pl.ds(pl.multiple_of(i * PAIR, PAIR), PAIR)
        there = pl.ds(pl.multiple_of((pairs + i) * PAIR, PAIR), PAIR)
        q = (got[:, at:at + PAIR] + bias_ref[half, 0:1, here]) * (1.0 / math.sqrt(HEAD))
        q_ref[seg, p, 0] = jnp.where(lane < HEAD, q, 0.0).astype(LOW)
        q_ref[seg, p, 1] = jnp.where(lane < HEAD, 0.0, q).astype(LOW)
        k_ref[seg, p] = got[:, at + PAIR:at + 2 * PAIR].astype(LOW)
        v_ref[seg, p] = (got[:, at + 2 * PAIR:at + 3 * PAIR] + bias_ref[half, 0:1, there]).astype(LOW)


def attend(q_ref, k_ref, v_ref, o_ref, linv_ref, e_slot, count, mem, seg, p):
    col = lax.broadcasted_iota(jnp.int32, (1, ROWS), 1)
    lane = lax.broadcasted_iota(jnp.int32, (1, PAIR), 1)
    masking = jnp.where(live_at(col, count, mem), 0.0, masked_score)
    keys = k_ref[seg, p]
    values = jnp.concatenate([v_ref[seg, p], jnp.ones((ROWS, PAIR), LOW)], 1)
    got = []
    for j in range(2):
        scores = dot(q_ref[seg, p, j], keys, 1, 1) + masking
        peak = jnp.max(scores, -1, keepdims=True)
        e_slot[j] = jnp.exp(scores - peak).astype(LOW)
        got.append(dot(e_slot[j], values, 1, 0))
    first = lane < HEAD
    linv = 1.0 / jnp.where(first, got[0][:, PAIR:], got[1][:, PAIR:])
    linv_ref[seg, p] = linv
    o_ref[seg, p] = (jnp.where(first, got[0][:, :PAIR], got[1][:, :PAIR]) * linv).astype(LOW)


def attend_back(q_ref, k_ref, v_ref, o_ref, linv_ref, do_ref, e_slot, ds_ref, out_ref, seg, p, half, i):
    lane = lax.broadcasted_iota(jnp.int32, (1, PAIR), 1)
    keys, values = k_ref[...], v_ref[...]
    scaled = do_ref[seg, p].astype(F32) * linv_ref[...]
    product = scaled * o_ref[...].astype(F32)
    dq, dk, dv = [], None, None
    for j in range(2):
        mine = (lane < HEAD) if j == 0 else (lane >= HEAD)
        mine_low = jnp.where(mine, scaled, 0.0).astype(LOW)
        delta = jnp.sum(jnp.where(mine, product, 0.0), -1, keepdims=True)
        gap = dot(mine_low, values, 1, 1) - delta
        ds_ref[j] = (e_slot[j].astype(F32) * gap).astype(LOW)
        dq.append(dot(ds_ref[j], keys, 1, 0))
        one_v = dot(e_slot[j], mine_low, 0, 0)
        one_k = dot(ds_ref[j], q_ref[j], 0, 0)
        dv = one_v if dv is None else dv + one_v
        dk = one_k if dk is None else dk + one_k
    rows = pl.ds(pl.multiple_of(seg * ROWS, 32), ROWS)
    dq = jnp.where(lane < HEAD, dq[0], dq[1]) * (1.0 / math.sqrt(HEAD))
    for kind, value in enumerate((dq, dk, dv)):
        out_ref[half, rows, pl.ds(pl.multiple_of((3 * i + kind) * PAIR, PAIR), PAIR)] = value.astype(LOW)


class Place:
    def __init__(self):
        me = lax.axis_index("dp")
        self.t = lax.axis_index("tensor")
        self.x = me % 2
        self.y = (me // 2) % 2
        self.z = me // 4
        self.nt, self.nx, self.ny = 1 - self.t, 1 - self.x, 1 - self.y
        self.px = self.at(self.z, self.y, self.nx)
        self.py = self.at(self.z, self.ny, self.x)
        self.zs = [(self.z + d) % 4 for d in (1, 2, 3)]
        self.zb = [(self.z + 4 - d) % 4 for d in (1, 2, 3)]
        self.pz = [self.at(z, self.y, self.x) for z in self.zs]
        self.pz1 = self.at(self.z + 1 - 2 * (self.z % 2), self.y, self.x)
        self.pz2 = self.at((self.z + 2) % 4, self.y, self.x)
        self.pc = (me, self.nt)

    def at(self, z, y, x):
        return (z * 4 + y * 2 + x, self.t)

    def greet(self):
        barrier = pltpu.get_barrier_semaphore()
        devices = [self.px, self.py, *self.pz, self.pc]
        for device in devices:
            pl.semaphore_signal(barrier, inc=1, device_id=device, device_id_type=MESH)
        pl.semaphore_wait(barrier, len(devices))


class Wire:
    def __init__(self, send, recv):
        self.send, self.recv, self.count, self.open = send, recv, 0, {}

    def start(self, src, dst, device, landing):
        k = self.count
        self.count += 1

        def copy(a, b):
            return pltpu.make_async_remote_copy(
                src_ref=a, dst_ref=b, send_sem=self.send.at[k], recv_sem=self.recv.at[k],
                device_id=device, device_id_type=MESH)

        copy(src(), dst()).start()
        self.open[k] = lambda: copy(src(), dst()).wait_send()
        return lambda: copy(landing(), landing()).wait_recv()

    def sent(self, k):
        self.open.pop(k)()

    def drain(self):
        for k in list(self.open):
            self.sent(k)


class Gather:
    def __init__(self, wire, place, out, at, width, order):
        self.wire, self.p, self.out = wire, place, out
        self.cols, self.order, self.landed, self.crossing = pl.ds(at, width), order, [], []

    def view(self, z, y, x, half=None):
        return lambda: self.out.at[self.p.t if half is None else half, z, y, x, :, self.cols]

    def stage(self, s):
        p, every = self.p, slice(None)
        for wait in self.landed:
            wait()
        self.landed = []
        home = self.view(p.z, p.y, p.x)
        if self.order == "zxy":
            if s == 0:
                for k in range(3):
                    self.go(home, None, p.pz[k], self.view(p.zb[k], p.y, p.x))
            elif s == 1:
                self.go(self.view(every, p.y, p.x), None, p.px, self.view(every, p.y, p.nx))
                self.cross(every, p.y, p.x)
            elif s == 2:
                self.go(self.view(every, p.y, every), None, p.py, self.view(every, p.ny, every))
                self.cross(every, p.y, p.nx)
            else:
                self.cross(every, p.ny, every)
        else:
            if s == 0:
                self.go(home, None, p.py, self.view(p.z, p.ny, p.x))
            elif s == 1:
                for k in range(3):
                    self.go(self.view(p.z, every, p.x), None, p.pz[k], self.view(p.zb[k], every, p.x))
                self.cross(p.z, every, p.x)
            elif s == 2:
                self.go(self.view(every, every, p.x), None, p.px, self.view(every, every, p.nx))
                for k in range(3):
                    self.cross(p.zb[k], every, p.x)
            else:
                self.cross(every, every, p.nx)

    def go(self, src, dst, device, landing):
        self.landed.append(self.wire.start(src, src if dst is None else dst, device, landing))

    def cross(self, z, y, x):
        mine = self.view(z, y, x)
        self.crossing.append(self.wire.start(mine, mine, self.p.pc, self.view(z, y, x, self.p.nt)))

    def whole(self):
        for wait in self.crossing:
            wait()
        self.crossing = []


class Travel:
    def __init__(self, wire, place, keep, payload, held, landing, order):
        self.wire, self.p, self.keep, self.landed = wire, place, keep, None
        self.held, self.landing, self.order, self.payload = held, landing, order, payload

    def stage(self, s):
        p = self.p
        if s > 0:
            self.landed()
            before = self.payload if s == 1 else self.held.at[s - 2]
            for m in range(self.payload.shape[0]):
                stay = self.keep[m][self.order[s - 1]]
                mine, theirs = before[m].astype(F32), self.landing[s - 1, m].astype(F32)
                self.held[s - 1, m] = jnp.where(stay, mine, theirs).astype(self.held.dtype)
        if s < len(self.order):
            device = [p.px, p.py, p.pz1, p.pz2][self.order[s]]
            land = lambda: self.landing.at[s]
            self.landed = self.wire.start(lambda: self.payload if s == 0 else self.held.at[s - 1], land, device, land)


def keep_flags(owners_ref, row, device, levels):
    holders = [device]
    for bit in range(levels):
        stride = 2 ** (bit + 1)
        found = device * 0
        for source in range(owners_ref.shape[1]):
            position = source - source % stride + lax.rem(owners_ref[row, source], stride)
            found = found + jnp.where(position == device, source, 0)
        holders.append(found)
    return [a == b for a, b in zip(holders[:-1], holders[1:])]


def valid_count(lengths_ref, index, seg_len):
    start, valid = index * 0, index * 0
    for j in range(lengths_ref.shape[0]):
        length = lengths_ref[j]
        count = lax.div(length + (seg_len - 1), seg_len)
        inside = (start <= index) & (index < start + count)
        valid = valid + jnp.where(inside, jnp.minimum(length - (index - start) * seg_len, seg_len), 0)
        start = start + count
    return valid


G384 = (('yzx', 0, 128), ('zxy', 128, 256))
G512 = (('yzx', 0, 128), ('zxy', 128, 384))
G768 = (('yzx', 0, 128), ('zxy', 128, 256), ('yzx', 384, 128), ('zxy', 512, 256))
CHUNKS = ((0, 0, G384), (0, 384, G384), (0, 768, G384), (1, 0, G512), (2, 0, G768), (2, 768, G768), (3, 0, G768), (3, 768, G768))
GATHER = (
    ((0, 0, 0), (0, 1, 0), (1, 0, 0), (1, 1, 0), (0, 0, 1), (0, 1, 1), (2, 0, 0), (2, 1, 0), (1, 0, 1), (1, 1, 1), (0, 0, 2), (0, 1, 2), (3, 0, 0), (3, 1, 0), (2, 0, 1), (2, 1, 1), (1, 0, 2), (1, 1, 2), (0, 0, 3), (0, 1, 3)),
    (),
    ((4, 0, 0), (4, 1, 0), (3, 0, 1), (3, 1, 1), (2, 0, 2), (2, 1, 2), (1, 0, 3), (1, 1, 3)),
    (),
    ((4, 2, 0), (4, 3, 0), (4, 0, 1), (4, 1, 1), (3, 0, 2), (3, 1, 2), (2, 0, 3), (2, 1, 3)),
    (),
    ((5, 0, 0), (5, 1, 0), (4, 2, 1), (4, 3, 1), (4, 0, 2), (4, 1, 2), (3, 0, 3), (3, 1, 3)),
    (),
    ((5, 2, 0), (5, 3, 0), (5, 0, 1), (5, 1, 1), (4, 2, 2), (4, 3, 2), (4, 0, 3), (4, 1, 3)),
    (),
    ((6, 0, 0), (6, 1, 0), (5, 2, 1), (5, 3, 1), (5, 0, 2), (5, 1, 2), (4, 2, 3), (4, 3, 3)),
    (),
    ((6, 2, 0), (6, 3, 0), (6, 0, 1), (6, 1, 1), (5, 2, 2), (5, 3, 2), (5, 0, 3), (5, 1, 3)),
    ((7, 0, 0), (7, 1, 0), (6, 2, 1), (6, 3, 1), (6, 0, 2), (6, 1, 2), (5, 2, 3), (5, 3, 3)),
    ((7, 2, 0), (7, 3, 0), (7, 0, 1), (7, 1, 1), (6, 2, 2), (6, 3, 2), (6, 0, 3), (6, 1, 3)),
    (),
    (),
    (),
    ((7, 2, 1), (7, 3, 1), (7, 0, 2), (7, 1, 2), (6, 2, 3), (6, 3, 3)),
    (),
    ((7, 2, 2), (7, 3, 2), (7, 0, 3), (7, 1, 3)),
    (),
    ((7, 2, 3), (7, 3, 3)),
    (),
    (),
    (),
    (),
    (),
    (),
)


class Copies:
    def __init__(self, sems):
        self.sems, self.count = sems, 0

    def start(self, src, dst):
        k = self.count
        self.count += 1
        pltpu.make_async_copy(src(), dst(), self.sems.at[k]).start()
        return lambda: pltpu.make_async_copy(src(), dst(), self.sems.at[k]).wait()


def front_kernel(kernels, mem, seg_len, width, *refs):
    n_in = 14 if kernels else 11
    lengths_ref, owners_ref, bias_in, mem_a, mem_b, tok_in, cot_in = refs[:7]
    weights_in = refs[7:n_in]
    (wqkv_out, wout_out, wup_out, wdown_out, q_out, k_out, v_out, o_out, linv_out, e_out, xt_out, x1t_out, unit_out, inv_out,
     dh_out, df_out, dft_out, g_out, d_out, y_out, sums_ref) = refs[n_in:n_in + 21]
    (wqkv, wout, wup, wdown, bias_ref, payload, held, landing, tok_ref, x_ref, cot_ref, vec_ref, o_ref, dh_ref, low_ref, unit_ref,
     inv_ref, flip_ref, send, recv, here, e_sems) = refs[-22:]
    weights = (wqkv, wout, wup, wdown)
    R = 2 * ROWS
    pairs = width // PAIR
    D = x_ref.shape[1]
    hidden = wup.shape[-1]
    copies = Copies(here)
    t = lax.axis_index("tensor")
    device = lax.axis_index("dp")
    loads = []
    for k, (a, s) in enumerate(((tok_in, 0), (tok_in, 1), (cot_in, 0), (cot_in, 1))):
        loads.append(copies.start(lambda a=a, s=s: a.at[2 * t + s], lambda k=k: tok_ref.at[k]))
    if kernels:
        place = Place()
        wire = Wire(send, recv)

        def mine(c, cols):
            return lambda: weights[c].at[place.t, place.z, place.y, place.x, :, cols]

        own = []
        for i in range(pairs):
            for kind in range(3):
                cols = pl.ds(i * PAIR, PAIR)
                own.append(copies.start(lambda kind=kind, cols=cols: weights_in[kind].at[:, cols], mine(0, pl.ds((3 * i + kind) * PAIR, PAIR))))
        own.append(copies.start(lambda: weights_in[3], mine(1, pl.ds(0, width))))
        own.append(copies.start(lambda: weights_in[6], mine(1, pl.ds(width, PAIR))))
        own.append(copies.start(lambda: weights_in[4], mine(2, pl.ds(0, hidden))))
        own.append(copies.start(lambda: weights_in[5], mine(3, pl.ds(0, hidden))))
        own_bias = copies.start(lambda: bias_in, lambda: bias_ref.at[place.t])
        for m in range(2):
            both = dot(picks(MEM_ROWS, mem, 0, 0, mem), mem_a[2 * t + m], 1, 0) + dot(picks(MEM_ROWS, mem, 0, mem, mem), mem_b[2 * t + m], 1, 0)
            payload[m] = both.astype(LOW)
        place.greet()
        keep = [keep_flags(owners_ref, 2 * t + m, device, 4) for m in range(2)]
        travel = Travel(wire, place, keep, payload, held, landing, (3, 2, 1, 0))
        parts = []
        for c, at, cuts in CHUNKS:
            parts.append([Gather(wire, place, weights[c], at + first, wide, order) for order, first, wide in cuts])

        def tick(point):
            for c, part, s in GATHER[point]:
                parts[c][part].stage(s)

        def ready(c):
            for part in parts[c]:
                part.whole()

        travel.stage(0)
        for wait in own:
            wait()
        bias_wait = wire.start(lambda: bias_in, lambda: bias_ref.at[place.t], place.pc, lambda: bias_ref.at[place.nt])
        for k, (c, part, s) in enumerate(GATHER[0]):
            parts[c][part].stage(s)
            if k in (1, 5, 11, 19):
                travel.stage((1, 5, 11, 19).index(k) + 1)
        own_bias()
        bias_wait()
        moved = held.at[3]
    else:
        fetched = [copies.start(lambda c=c: weights_in[c], lambda c=c: weights[c]) for c in range(4)]
        fetched.append(copies.start(lambda: bias_in, lambda: bias_ref))
        for wait in fetched:
            wait()
        moved = mem_a
        tick = ready = lambda step: None
    counts = [valid_count(lengths_ref, device * 4 + 2 * t + s, seg_len) for s in range(2)]
    for wait in loads:
        wait()
    for s in range(2):
        both = dot(picks(2 * TAIL, MEM_ROWS, 0, 0, mem) + picks(2 * TAIL, MEM_ROWS, mem, TAIL, mem), moved[s], 1, 0).astype(LOW)
        for k, ref in enumerate((x_ref, cot_ref)):
            ref[s * ROWS + TOK - 16:s * ROWS + TOK, :] = jnp.zeros((16, D), LOW)
            ref[s * ROWS:s * ROWS + seg_len, :] = tok_ref[2 * k + s]
            ref[s * ROWS + TOK:(s + 1) * ROWS, :] = both[k * TAIL:(k + 1) * TAIL]
    flip_ref[...] = x_ref[...].T
    saves = [copies.start(lambda: flip_ref, lambda: xt_out)]

    def attention(q_ref, k_ref, v_ref, linv_ref, slots):
        def e_copy(seg, p, slot):
            return pltpu.make_async_copy(slots.at[slot], e_out.at[seg, p], e_sems.at[slot])

        def step(n, carry):
            i, seg, half = n // 4, (n // 2) % 2, n % 2
            for k in range(12):
                @pl.when(n == k)
                def _():
                    tick(1 + k)
                    if k in (4, 8):
                        ready(k // 4)

            @pl.when(half == 0)
            def _():
                project(x_ref, wqkv, bias_ref, q_ref, k_ref, v_ref, seg, i, pairs)

            count = jnp.where(seg == 0, counts[0], counts[1])

            @pl.when(n > 1)
            def _():
                e_copy(seg, half * pairs + i, half).wait()

            attend(q_ref, k_ref, v_ref, o_ref, linv_ref, slots.at[half], count, mem, seg, half * pairs + i)
            e_copy(seg, half * pairs + i, half).start()
            return carry

        ready(0)
        lax.fori_loop(0, 4 * pairs, step, 0)
        done = []
        for a, b in ((q_ref, q_out), (k_ref, k_out), (v_ref, v_out), (o_ref, o_out), (linv_ref, linv_out), (wqkv, wqkv_out)):
            done.append(copies.start(lambda a=a: a, lambda b=b: b))
        tick(13)
        ready(3)
        done.append(copies.start(lambda: wout, lambda: wout_out))
        for half in range(2):
            e_copy(0, 0, half).wait()
        for wait in done:
            wait()

    six = (2, 2 * pairs, ROWS, PAIR)
    pl.run_scoped(
        attention, pltpu.VMEM((2, 2 * pairs, 2, ROWS, PAIR), LOW), pltpu.VMEM(six, LOW), pltpu.VMEM(six, LOW),
        pltpu.VMEM(six, F32), pltpu.VMEM((2, 2, ROWS, ROWS), LOW))

    sums_ref[...] = jnp.zeros_like(sums_ref)
    vec_ref[...] = mat(wout, 0, slice(width, width + PAIR)).astype(F32).T[:8]
    vec = {n: vec_ref[k:k + 1, :] for k, n in enumerate(("b_out", "b_down", "gain_attn", "shift_attn", "gain_ffn", "shift_ffn"))}

    def out_step(s, carry):
        rows = pl.ds(pl.multiple_of(s * ROWS, ROWS), ROWS)
        h = x_ref[rows, :].astype(F32) + vec["b_out"]
        for t in range(2):
            o = jnp.concatenate([o_ref[s, t * pairs + i] for i in range(pairs)], 1)
            h = h + dot(o, mat(wout, t, slice(0, width)), 1, 1)
        unit, inv = normed(h)
        x1 = unit * vec["gain_attn"] + vec["shift_attn"]
        dh_ref[rows, :] = x1
        low_ref[rows, :] = x1.astype(LOW)
        unit_ref[rows, :] = unit.astype(LOW)
        inv_ref[rows, :] = inv
        return carry

    lax.fori_loop(0, 2, out_step, 0)
    tick(14)
    tick(15)
    for wait in saves:
        wait()
    flip_ref[...] = low_ref[...].T
    saves = [copies.start(lambda a=a: a, lambda b=b: b) for a, b in ((flip_ref, x1t_out), (unit_ref, unit_out), (inv_ref, inv_out))]

    def ffn(g_ref, d_ref):
        tile = min(hidden // 2, 256)
        part = R // 4

        def up_cols(first, count, base):
            def up_step(k, carry):
                t = k % 2
                at = first + (k // 2) * tile
                for n in range(2 * count):
                    @pl.when(k == n)
                    def _():
                        tick(base + n)
                        if n == 0:
                            ready(4 + (base - 16) // 6)
                cols = pl.ds(pl.multiple_of(at, PAIR), tile)
                u = dot(low_ref[...], mat(wup, t, cols), 1, 0)
                u = u + bias_ref[t, 0:1, pl.ds(pl.multiple_of(2 * width + at, PAIR), tile)]
                phi = 0.5 * (1.0 + lax.erf(u * (1.0 / math.sqrt(2.0))))
                g_ref[t, :, cols] = (u * phi).astype(LOW)
                d_ref[t, :, cols] = (phi + u * (jnp.exp(-0.5 * u * u) * (1.0 / math.sqrt(2.0 * math.pi)))).astype(LOW)
                return carry

            lax.fori_loop(0, 2 * count, up_step, 0)

        up_cols(0, hidden // 2 // tile, 16)
        up_cols(hidden // 2, hidden // 2 // tile, 22)
        done = [copies.start(lambda a=a: a, lambda b=b: b) for a, b in ((wup, wup_out), (g_ref, g_out), (d_ref, d_out))]
        tick(28)
        ready(6)
        ready(7)
        done.append(copies.start(lambda: wdown, lambda: wdown_out))

        def down_step(s, carry):
            rows = pl.ds(pl.multiple_of(s * part, part), part)
            h = dh_ref[rows, :] + vec["b_down"]
            for t in range(2):
                h = h + dot(g_ref[t, rows, :], mat(wdown, t, slice(None)), 1, 1)
            unit, inv = normed(h)
            count = jnp.where(s < 2, counts[0], counts[1])
            at = lax.broadcasted_iota(jnp.int32, (part, 1), 0) + (s % 2) * part
            live = jnp.where(live_at(at, count, mem), 1.0, 0.0)
            x_ref[rows, :] = ((unit * vec["gain_ffn"] + vec["shift_ffn"]) * live).astype(LOW)
            dy = cot_ref[rows, :].astype(F32) * live
            fold(sums_ref, 4, dy * unit)
            fold(sums_ref, 5, dy)
            dh = norm_back(dy * vec["gain_ffn"], unit, inv)
            fold(sums_ref, 1, dh)
            dh_ref[rows, :] = dh
            cot_ref[rows, :] = dh.astype(LOW)
            return carry

        lax.fori_loop(0, 4, down_step, 0)
        for wait in done:
            wait()

    pl.run_scoped(ffn, pltpu.VMEM((2, R, hidden), LOW), pltpu.VMEM((2, R, hidden), LOW))
    ends = [copies.start(lambda a=a: a, lambda b=b: b) for a, b in ((dh_ref, dh_out), (cot_ref, df_out), (x_ref, y_out))]
    for wait in saves:
        wait()
    flip_ref[...] = cot_ref[...].T
    ends.append(copies.start(lambda: flip_ref, lambda: dft_out))
    for wait in ends:
        wait()
    if kernels:
        wire.drain()


def front(lengths, owners, bias, mem_a, mem_b, tokens, cots, weights, width, hidden, mem, kernels, cid):
    seg_len, D = tokens.shape[1:]
    R = 2 * ROWS
    pairs = width // PAIR
    S, V = jax.ShapeDtypeStruct, pltpu.VMEM
    hbm, vmem, smem = (pl.BlockSpec(memory_space=m) for m in (pl.ANY, pltpu.VMEM, pltpu.SMEM))
    full = (2, *GRID, D // math.prod(GRID)) if kernels else (2, D)
    six = (2, 2 * pairs, ROWS, PAIR)
    payload = (2, MEM_ROWS, D)
    count = 5 + sum(8 if part[0] == "zxy" else 10 for _, _, cuts in CHUNKS for part in cuts)
    shapes = [(*full, w) for w in (3 * width, width + PAIR, hidden, hidden)]
    params = dict(collective_id=cid, has_side_effects=True) if kernels else {}
    return pl.pallas_call(
        functools.partial(front_kernel, kernels, mem, seg_len, width),
        out_shape=[
            *(S(s, LOW) for s in shapes), S((2, 2 * pairs, 2, ROWS, PAIR), LOW), S(six, LOW), S(six, LOW), S(six, LOW), S(six, F32),
            S((2, 2 * pairs, 2, ROWS, ROWS), LOW), S((D, R), LOW), S((D, R), LOW), S((R, D), LOW), S((R, 1), F32), S((R, D), F32),
            S((R, D), LOW), S((D, R), LOW), S((2, R, hidden), LOW), S((2, R, hidden), LOW), S((R, D), LOW), S((8, D), F32)],
        in_specs=[smem, smem, vmem, vmem, vmem] + [hbm] * (2 + len(weights)),
        out_specs=[hbm] * 20 + [vmem],
        scratch_shapes=[
            *(V(s, LOW) for s in shapes), V((2, 1, 2 * width + hidden), F32), V(payload, LOW), V((4, *payload), LOW), V((4, *payload), LOW),
            V((4, seg_len, D), LOW), V((R, D), LOW), V((R, D), LOW), V((8, D), F32), V(six, LOW), V((R, D), F32), V((R, D), LOW),
            V((R, D), LOW), V((R, 1), F32), V((D, R), LOW),
            pltpu.SemaphoreType.DMA((count,)), pltpu.SemaphoreType.DMA((count,)), pltpu.SemaphoreType.DMA((40,)),
            pltpu.SemaphoreType.DMA((2,))],
        compiler_params=pltpu.CompilerParams(vmem_limit_bytes=63 << 20, **params),
    )(lengths, owners, bias, mem_a, mem_b, tokens, cots, *weights)


class Scatter:
    def __init__(self, wire, place, acc, sink, cols, order, landings):
        self.wire, self.p, self.acc, self.sink = wire, place, acc, sink
        self.cols, self.order, self.landed = cols, order, []
        self.r1, self.r2, self.r3 = landings

    def view(self, z, y, x):
        return lambda: self.acc.at[z, y, x, :, self.cols]

    def sum(self, z, y, x, terms):
        total = self.acc[z, y, x, :, self.cols].astype(F32)
        for term in terms:
            total = total + term.astype(F32)
        return total

    def add(self, z, y, x, *terms):
        self.acc[z, y, x, :, self.cols] = self.sum(z, y, x, terms).astype(self.acc.dtype)

    def finish(self, *terms):
        self.sink(self.sum(self.p.z, self.p.y, self.p.x, terms))

    def stage(self, s):
        p, every = self.p, slice(None)
        for wait in self.landed:
            wait()
        self.landed = []
        r1, r2, r3 = self.r1, self.r2, self.r3
        if self.order == "yxz":
            if s == 0:
                self.go(self.view(every, p.ny, every), lambda: r1, p.py)
            elif s == 1:
                for z in range(4):
                    for x in range(2):
                        self.add(z, p.y, x, r1[z, x])
                self.go(self.view(every, p.y, p.nx), lambda: r2, p.px)
            elif s == 2:
                for z in range(4):
                    self.add(z, p.y, p.x, r2[z])
                for k in range(3):
                    self.go(self.view(p.zs[k], p.y, p.x), lambda k=k: r3.at[k], p.pz[k])
            else:
                self.finish(r3[0], r3[1], r3[2])
        else:
            if s == 0:
                self.go(self.view(every, every, p.nx), lambda: r1, p.px)
            elif s == 1:
                for z in range(4):
                    for y in range(2):
                        self.add(z, y, p.x, r1[z, y])
                for k in range(3):
                    self.go(self.view(p.zs[k], every, p.x), lambda k=k: r2.at[k], p.pz[k])
            elif s == 2:
                for y in range(2):
                    self.add(p.z, y, p.x, r2[0, y], r2[1, y], r2[2, y])
                self.go(self.view(p.z, p.ny, p.x), lambda: r3, p.py)
            else:
                self.finish(r3[...])

    def go(self, src, landing, device):
        self.landed.append(self.wire.start(src, landing, device, landing))


def scatter_shapes(rows, order, wide):
    V = pltpu.VMEM
    if order == "xzy":
        return [V((4, 2, rows, wide), LOW), V((3, 2, rows, wide), LOW), V((rows, wide), LOW)]
    return [V((4, 2, rows, wide), LOW), V((4, rows, wide), LOW), V((3, rows, wide), LOW)]


class Total:
    def __init__(self, wire, place, vec, out, hops, vz):
        self.wire, self.p, self.landed = wire, place, []
        self.vec, self.out, self.hops, self.vz = vec, out, hops, vz

    def stage(self, s):
        p, hops = self.p, self.hops
        for wait in self.landed:
            wait()
        self.landed = []
        if s == 0:
            self.go(lambda: self.vec, lambda: hops.at[0], p.pc)
        elif s < 4:
            hops[2 * s - 1] = (self.vec[...] if s == 1 else hops[2 * s - 3]) + hops[2 * s - 2]
            if s < 3:
                self.go(lambda: hops.at[2 * s - 1], lambda: hops.at[2 * s], (p.px, p.py)[s - 1])
            else:
                for k in range(3):
                    self.go(lambda: hops.at[5], lambda k=k: self.vz.at[k], p.pz[k])
        else:
            self.out[...] = hops[5] + self.vz[0] + self.vz[1] + self.vz[2]

    def go(self, src, landing, device):
        self.landed.append(self.wire.start(src, landing, device, landing))


S384 = (('xzy', 0, 128), ('yxz', 128, 256))
S768 = (('xzy', 0, 128), ('yxz', 128, 256), ('xzy', 384, 128), ('yxz', 512, 256))
SUMS = ((0, 0, 768, S768), (0, 768, 768, S768), (1, 0, 768, S768), (1, 768, 768, S768), (2, 0, 384, S384), (3, 0, 384, S384), (3, 384, 384, S384), (3, 768, 384, S384))
SCATTER = (
    ((0, 2, 0), (0, 3, 0), (0, 0, 0), (0, 1, 0)),
    ((1, 2, 0), (1, 3, 0), (1, 0, 0), (1, 1, 0)),
    (),
    ((0, 2, 1), (0, 3, 1), (0, 0, 1), (0, 1, 1)),
    ((2, 2, 0), (2, 3, 0), (2, 0, 0), (2, 1, 0)),
    ((1, 2, 1), (1, 3, 1), (1, 0, 1), (1, 1, 1), (0, 2, 2), (0, 3, 2), (0, 0, 2), (0, 1, 2)),
    ((1, 0, 2), (1, 1, 2), (0, 2, 3), (0, 3, 3), (0, 0, 3), (0, 1, 3)),
    ((1, 2, 2), (1, 3, 2)),
    ((3, 2, 0), (3, 3, 0), (3, 0, 0), (3, 1, 0), (2, 2, 1), (2, 3, 1), (2, 0, 1), (2, 1, 1), (1, 2, 3), (1, 3, 3), (1, 0, 3), (1, 1, 3)),
    (),
    ((2, 2, 2), (2, 3, 2), (2, 0, 2), (2, 1, 2)),
    ((4, 0, 0), (4, 1, 0)),
    ((2, 2, 3), (2, 3, 3), (2, 0, 3), (2, 1, 3)),
    (),
    (),
    (),
    ((3, 2, 1), (3, 3, 1), (3, 0, 1), (3, 1, 1)),
    ((4, 0, 1), (4, 1, 1)),
    ((5, 0, 0), (5, 1, 0), (3, 2, 2), (3, 3, 2), (3, 0, 2), (3, 1, 2)),
    (),
    (),
    ((4, 0, 2), (4, 1, 2), (3, 2, 3), (3, 3, 3), (3, 0, 3), (3, 1, 3)),
    ((6, 0, 0), (6, 1, 0), (5, 0, 1), (5, 1, 1)),
    (),
    ((4, 0, 3), (4, 1, 3)),
    ((5, 0, 2), (5, 1, 2)),
    ((7, 0, 0), (7, 1, 0)),
    ((6, 0, 1), (6, 1, 1), (5, 0, 3), (5, 1, 3)),
    (),
    ((6, 0, 2), (6, 1, 2), (7, 0, 1), (7, 1, 1), (6, 0, 3), (6, 1, 3), (7, 0, 2), (7, 1, 2), (7, 0, 3), (7, 1, 3)),
)
TOTAL = (13, 16, 19, 22, 25)
PART = 768
SUB = 256


def back_kernel(kernels, mem, width, hidden, *refs):
    n_land = 3 * sum(len(cuts) for _, _, _, cuts in SUMS)
    (owners_ref, sums_in, wqkv_in, wout_in, wup_in, wdown_in, q_in, k_in, v_in, o_in, linv_in, e_in, xt_in, x1t_in, unit_in, inv_in,
     dh_in, df_in, dft_in, g_in, d_in, y_in) = refs[:22]
    (y_out, dx_out, mem_out, vec_out, late_out, gq_out, gk_out, gv_out, out_out, up_out, down_out) = refs[22:33]
    (tot_ref, late_ref, o_ref, do_ref, dh_ref, low_ref, unit_ref, inv_ref, flip_ref, wout, tail_ref, payload, held, landing,
     hops, vz, hops2, vz2, acc0, acc1, acc2, acc3, oth0, oth1, oth2, oth3, away0, away1, away2, away3) = refs[33:63]
    landings = refs[63:63 + n_land]
    send, recv, here, pair_sems = refs[63 + n_land:]
    R = 2 * ROWS
    pairs = width // PAIR
    D = dh_ref.shape[1]
    grid_rows = (4, 2, 2, D // 16)
    wide_qkv = 3 * PAIR
    steps = hidden // PART
    copies = Copies(here)
    accs, others, aways = (acc0, acc1, acc2, acc3), (oth0, oth1, oth2, oth3), (away0, away1, away2, away3)
    place = Place()
    halves = (place.nt, place.t) if kernels else (0, 1)
    if kernels:
        wire = Wire(send, recv)

        def sink(c, at, first, wide):
            if c < 3:
                out = (down_out, up_out, out_out)[c]

                def put(total):
                    out[:, at + first:at + first + wide] = total

                return put
            cols = slice(at // 3, at // 3 + PAIR)

            def put_q(total):
                gq_out[:, cols] = total

            def put_kv(total):
                gk_out[:, cols] = total[:, :PAIR]
                gv_out[:, cols] = total[:, PAIR:]

            return put_kv if first else put_q

        parts, crossed = [], {}
        taken = 0
        for c, at, _, cuts in SUMS:
            parts.append([])
            for order, first, wide in cuts:
                cols = slice(at + first, at + first + wide)
                parts[-1].append(Scatter(wire, place, accs[c], sink(c, at, first, wide), cols, order, landings[taken:taken + 3]))
                taken += 3
        total = Total(wire, place, tot_ref, vec_out, hops, vz)

    def point(p):
        if not kernels:
            return
        for event in SCATTER[p]:
            run(event)
        if p in TOTAL:
            total.stage(TOTAL.index(p))

    def run(event):
        n, part, s = event
        if n in crossed:
            c, at, wide, _ = SUMS[n]
            crossed.pop(n)()
            cols = slice(at, at + wide)

            def together(z, carry):
                both = accs[c][z, :, :, :, cols].astype(F32) + others[c][z, :, :, :, cols].astype(F32)
                accs[c][z, :, :, :, cols] = both.astype(LOW)
                return carry

            lax.fori_loop(0, 4, together, 0)
        parts[n][part].stage(s)

    away_open = {}

    def away_of(n):
        c, at, wide, _ = SUMS[n]
        return aways[c].at[at // wide] if c == 3 else aways[c]

    def fresh(n):
        c = SUMS[n][0]
        if kernels and c in away_open:
            wire.sent(away_open.pop(c))

    def emit(n, h, at, value):
        c, first, wide, _ = SUMS[n]
        size = value.shape[1]
        value = value.astype(LOW)
        if not kernels:
            away_of(n)[:, :, :, :, pl.ds(at, size)] = value.reshape(*grid_rows, size)
        elif h == 0:
            away_of(n)[:, :, :, :, pl.ds(at, size)] = value.reshape(*grid_rows, size)
        else:
            cols = pl.ds(first + at, size) if isinstance(at, int) else pl.ds(pl.multiple_of(first + at, PAIR), size)
            accs[c][:, :, :, :, cols] = value.reshape(*grid_rows, size)

    def emitted(n, h):
        c, at, wide, _ = SUMS[n]
        if kernels:
            if h == 0:
                land = lambda: others[c].at[:, :, :, :, pl.ds(at, wide)]
                away_open[c if c < 3 else (c, n)] = wire.count
                crossed[n] = wire.start(lambda: away_of(n), land, place.pc, land)
        elif c < 3:
            out = (down_out, up_out, out_out)[c]
            copies.start(lambda: away_of(n), lambda: out.at[h, :, :, :, :, pl.ds(at, wide)])()
        else:
            for kind, out in enumerate((gq_out, gk_out, gv_out)):
                copies.start(lambda: away_of(n).at[:, :, :, :, pl.ds(kind * PAIR, PAIR)],
                             lambda: out.at[h, :, :, :, :, pl.ds(at // 3, PAIR)])()

    tot_ref[...] = jnp.zeros_like(tot_ref)
    tot_ref[0:8, :] = sums_in[...]
    late_ref[...] = jnp.zeros_like(late_ref)
    load_flip = copies.start(lambda: dft_in, lambda: flip_ref)

    def tile_cols(j):
        return pl.ds(j * PART, PART)

    def ffn(df_ref, x1t_ref, g_slot, d_slot, du_slot, wd_slot, wu_slot):
        def load(a, slot, h, j, weight):
            half = halves[h]
            if weight and kernels:
                return copies.start(lambda: a.at[half, :, :, :, :, tile_cols(j)], lambda: slot.at[h])
            return copies.start(lambda: a.at[half, :, tile_cols(j)], lambda: slot.at[h])

        waits = {}

        def fetch(j, kinds):
            for kind in kinds:
                a, slot, weight = {"g": (g_in, g_slot, 0), "d": (d_in, d_slot, 0), "wd": (wdown_in, wd_slot, 1), "wu": (wup_in, wu_slot, 1)}[kind]
                for h in range(2):
                    waits[kind, h, j] = load(a, slot, h, j, weight)

        fetch(0, ["g"])
        load_df = copies.start(lambda: df_in, lambda: df_ref)
        fetch(0, ["wd", "d"])
        load_x1t = copies.start(lambda: x1t_in, lambda: x1t_ref)
        fetch(0, ["wu"])
        load_dh = copies.start(lambda: dh_in, lambda: dh_ref)
        later = [copies.start(lambda a=a: a, lambda b=b: b) for a, b in ((unit_in, unit_ref), (inv_in, inv_ref), (o_in, o_ref), (wout_in, wout))]
        later += [copies.start(lambda s=s: y_in.at[pl.ds(s * ROWS + TOK, TAIL)], lambda s=s: tail_ref.at[s]) for s in range(2)]
        load_y = copies.start(lambda: y_in, lambda: low_ref)
        y_waits = []
        if kernels:
            place.greet()
        load_flip()
        part = R // 4
        for j in range(steps):
            fresh(j)
            for h in range(2):
                waits["g", h, j]()

                def down(k, carry):
                    cols = pl.ds(pl.multiple_of(k * SUB, SUB), SUB)
                    emit(j, h, k * SUB, dot(flip_ref[...], g_slot[h, :, cols], 1, 0))
                    return carry

                lax.fori_loop(0, PART // SUB, down, 0)
                emitted(j, h)
                if j + 1 < steps:
                    waits["g", h, j + 1] = load(g_in, g_slot, h, j + 1, 0)
            point(j)
        load_df()
        load_x1t()
        load_y()
        if kernels:
            y_sent = wire.count
            y_waits.append(wire.start(lambda: low_ref, lambda: y_out.at[place.t], place.pc, lambda: y_out.at[place.nt]))
            y_waits.append(copies.start(lambda: low_ref, lambda: y_out.at[place.t]))
        else:
            y_waits.append(copies.start(lambda: low_ref, lambda: y_out))
        for j in range(steps):
            fresh(2 + j)
            for h in range(2):
                waits["wd", h, j]()
                waits["d", h, j]()

                def up(k, carry):
                    cols = pl.ds(pl.multiple_of(k * SUB, SUB), SUB)
                    weight = wd_slot[h, ..., cols].reshape(D, SUB)
                    du = dot(df_ref[...], weight, 1, 0) * d_slot[h, :, cols].astype(F32)
                    tot_ref[pl.ds(8 + 2 * halves[h] + j, 1), cols] = jnp.sum(du, 0, keepdims=True)
                    du_slot[:, cols] = du.astype(LOW)
                    emit(2 + j, h, k * SUB, dot(x1t_ref[...], du_slot[:, cols], 1, 0))
                    return carry

                lax.fori_loop(0, PART // SUB, up, 0)
                emitted(2 + j, h)
                point(2 + 4 * j + 2 * h)
                waits["wu", h, j]()
                if j == 0 and h == 0:
                    load_dh()

                def inward(s, carry):
                    rows = pl.ds(pl.multiple_of(s * part, part), part)
                    dh_ref[rows, :] += dot(du_slot[rows, :], wu_slot[h].reshape(D, PART), 1, 1)
                    return carry

                lax.fori_loop(0, 4, inward, 0)
                if j + 1 < steps:
                    for kind, a, slot, weight in (("wd", wdown_in, wd_slot, 1), ("d", d_in, d_slot, 0), ("wu", wup_in, wu_slot, 1)):
                        waits[kind, h, j + 1] = load(a, slot, h, j + 1, weight)
                point(3 + 4 * j + 2 * h)
        for wait in later:
            wait()
        for wait in y_waits:
            wait()
        if kernels:
            wire.sent(y_sent)

    V = pltpu.VMEM
    weight_tile = (*grid_rows, PART) if kernels else (D, PART)
    pl.run_scoped(ffn, V((R, D), LOW), V((D, R), LOW), V((2, R, PART), LOW), V((2, R, PART), LOW), V((R, PART), LOW),
                  V((2, *weight_tile), LOW), V((2, *weight_tile), LOW))

    vec_gain = mat(wout, 0, slice(width, width + PAIR)).astype(F32).T[2:3]
    quarter = R // 4

    def norm_step(s, carry):
        rows = pl.ds(pl.multiple_of(s * quarter, quarter), quarter)
        dx = dh_ref[rows, :]
        unit = unit_ref[rows, :].astype(F32)
        fold(tot_ref, 2, dx * unit)
        fold(tot_ref, 3, dx)
        dh = norm_back(dx * vec_gain, unit, inv_ref[rows, :])
        fold(tot_ref, 0, dh)
        dh_ref[rows, :] = dh
        low_ref[rows, :] = dh.astype(LOW)
        return carry

    lax.fori_loop(0, 4, norm_step, 0)
    point(10)
    flip_ref[...] = low_ref[...].T
    for h in range(2):
        both = jnp.concatenate([jnp.concatenate([o_ref[s, halves[h] * pairs + i] for i in range(pairs)], 1) for s in range(2)], 0)
        emit(4, h, 0, dot(flip_ref[...], both, 1, 0))
        emitted(4, h)
    load_xt = copies.start(lambda: xt_in, lambda: flip_ref)

    def out_back(s, carry):
        rows = pl.ds(pl.multiple_of(s * ROWS, ROWS), ROWS)
        for t in range(2):
            got = dot(low_ref[rows, :], mat(wout, t, slice(0, width)), 1, 0).astype(LOW)
            for i in range(pairs):
                do_ref[s, t * pairs + i] = got[:, i * PAIR:(i + 1) * PAIR]
        return carry

    def attention(q_s, k_s, v_s, o_s, linv_s, e_s, ds_ref, out_ref, wqkv):
        def place_of(n):
            return n // 4, (n // 2) % 2, n % 2

        def slot_copies(n):
            i, seg, half = place_of(n)
            p, slot = half * pairs + i, n % 2
            table = ((q_in, q_s), (k_in, k_s), (v_in, v_s), (o_in, o_s), (linv_in, linv_s), (e_in, e_s))
            return [pltpu.make_async_copy(a.at[seg, p], b.at[slot], pair_sems.at[slot, k]) for k, (a, b) in enumerate(table)]

        for copy in slot_copies(0):
            copy.start()
        load_w = copies.start(lambda: wqkv_in, lambda: wqkv)
        point(11)
        lax.fori_loop(0, 2, out_back, 0)
        point(12)
        load_xt()

        def gradients(i):
            cols = pl.ds(i * wide_qkv, wide_qkv)
            for h in range(2):
                emit(5 + i, h, 0, dot(flip_ref[...], out_ref[halves[h], :, cols], 1, 0))
                emitted(5 + i, h)
                late_ref[halves[h], i:i + 1, :] = jnp.sum(out_ref[halves[h], :, cols].astype(F32), 0, keepdims=True)

        def step(n, carry):
            i, seg, half = place_of(n)
            slot = n % 2

            @pl.when(n < 4 * pairs - 1)
            def _():
                for copy in slot_copies(n + 1):
                    copy.start()

            for k in range(12):
                @pl.when(n == k)
                def _():
                    if k in (4, 8):
                        gradients(k // 4 - 1)
                    point(13 + k)
            for copy in slot_copies(n):
                copy.wait()
            attend_back(q_s.at[slot], k_s.at[slot], v_s.at[slot], o_s.at[slot], linv_s.at[slot], do_ref, e_s.at[slot], ds_ref, out_ref,
                        seg, half * pairs + i, half, i)
            return carry

        lax.fori_loop(0, 4 * pairs, step, 0)
        gradients(pairs - 1)
        if kernels:
            late = Total(wire, place, late_ref, late_out, hops2, vz2)
            late.stage(0)
        late_stage = late.stage if kernels else (lambda s: None)
        point(25)
        load_w()

        def in_step(s, carry):
            rows = pl.ds(pl.multiple_of(s * quarter, quarter), quarter)
            dx = dh_ref[rows, :]
            for t in range(2):
                dx = dx + dot(out_ref[t, rows, :], mat(wqkv, t, slice(None)), 1, 1)
            low_ref[rows, :] = dx.astype(LOW)
            return carry

        point(26)
        lax.fori_loop(0, 2, in_step, 0)
        point(27)
        late_stage(1)
        lax.fori_loop(2, 4, in_step, 0)
        point(28)
        late_stage(2)
        for s in range(2):
            ends = low_ref[s * ROWS + TOK:(s + 1) * ROWS, :]
            both = dot(picks(MEM_ROWS, TAIL, 0, 0, mem), tail_ref[s], 1, 0) + dot(picks(MEM_ROWS, TAIL, 0, mem, mem), ends, 1, 0)
            payload[s] = both.astype(LOW)
        if kernels:
            x_wait = wire.start(lambda: low_ref, lambda: dx_out.at[place.t], place.pc, lambda: dx_out.at[place.nt])
            x_own = copies.start(lambda: low_ref, lambda: dx_out.at[place.t])
            keep = [keep_flags(owners_ref, 2 * place.t + m, lax.axis_index("dp"), 4) for m in range(2)]
            travel = Travel(wire, place, keep, payload, held, landing, (0, 1, 2, 3))
            rest = SCATTER[29]
            for k in range(5):
                travel.stage(k)
                if k in (1, 3):
                    late.stage(3 + k // 2)
                for event in rest[k * len(rest) // 5:(k + 1) * len(rest) // 5]:
                    run(event)
            mem_out[place.t] = held[3]
            m_wait = wire.start(lambda: held.at[3], lambda: mem_out.at[place.t], place.pc, lambda: mem_out.at[place.nt])
            for wait in (x_wait, m_wait, x_own):
                wait()
            wire.drain()
        else:
            copies.start(lambda: low_ref, lambda: dx_out)()
            mem_out[...] = payload[...]
            late_out[...] = late_ref[...]
            vec_out[...] = tot_ref[...]

    slot_shapes = [V((2, 2, ROWS, PAIR), LOW)] + [V((2, ROWS, PAIR), LOW)] * 3 + [V((2, ROWS, PAIR), F32)]
    full = (2, *grid_rows, 3 * width) if kernels else (2, D, 3 * width)
    pl.run_scoped(attention, *slot_shapes, V((2, 2, ROWS, ROWS), LOW), V((2, ROWS, ROWS), LOW), V((2, R, 3 * width), LOW), V(full, LOW))


def back(owners, sums, front_outs, width, hidden, mem, rows, kernels, cid):
    dh = front_outs[14]
    R, D = dh.shape
    pairs = width // PAIR
    S, V = jax.ShapeDtypeStruct, pltpu.VMEM
    hbm, vmem, smem = (pl.BlockSpec(memory_space=m) for m in (pl.ANY, pltpu.VMEM, pltpu.SMEM))
    widths = (hidden, hidden, width, 3 * width)
    grid = (*GRID, D // math.prod(GRID))
    if kernels:
        sums_out = [S((rows, w), F32) for w in (width, width, width, width, hidden, hidden)]
        specs = [vmem] * 6
        two = (2,)
        params = dict(collective_id=cid, has_side_effects=True)
        accs = [V((*grid, w), LOW) for w in widths] * 2
        landings = [s for _, _, _, cuts in SUMS for order, _, wide in cuts for s in scatter_shapes(rows, order, wide)]
    else:
        sums_out = [S((2, *grid, w), LOW) for w in (width, width, width, width, hidden, hidden)]
        specs = [hbm] * 6
        two = ()
        params = {}
        accs = [V((8, 128), LOW)] * 8
        landings = [V((8, 128), LOW)] * (3 * sum(len(cuts) for _, _, _, cuts in SUMS))
    aways = [V((*grid, PART), LOW), V((*grid, PART), LOW), V((*grid, width), LOW), V((pairs, *grid, 3 * PAIR), LOW)]
    payload = (2, MEM_ROWS, D)
    late = (2, 8, 3 * PAIR)
    six = (2, 2 * pairs, ROWS, PAIR)
    count = 28 + 5 * sum(len(cuts) for _, _, _, cuts in SUMS)
    return pl.pallas_call(
        functools.partial(back_kernel, kernels, mem, width, hidden),
        out_shape=[S((*two, R, D), LOW), S((*two, R, D), LOW), S((*two, *payload), LOW), S((16, D), F32), S(late, F32), *sums_out],
        in_specs=[smem, vmem] + [hbm] * 20,
        out_specs=[hbm, hbm, vmem, vmem, vmem, *specs],
        scratch_shapes=[
            V((16, D), F32), V(late, F32), V(six, LOW), V(six, LOW), V((R, D), F32), V((R, D), LOW), V((R, D), LOW), V((R, 1), F32), V((D, R), LOW),
            V(front_outs[1].shape, LOW), V((2, TAIL, D), LOW), V(payload, LOW), V((4, *payload), LOW), V((4, *payload), LOW),
            V((6, 16, D), F32), V((3, 16, D), F32), V((6, *late), F32), V((3, *late), F32),
            *accs, *aways, *landings,
            pltpu.SemaphoreType.DMA((count,)), pltpu.SemaphoreType.DMA((count,)), pltpu.SemaphoreType.DMA((64,)), pltpu.SemaphoreType.DMA((2, 6))],
        compiler_params=pltpu.CompilerParams(vmem_limit_bytes=63 << 20, **params),
    )(owners, sums, *front_outs)


def last_kernel(mem, seg_len, *refs):
    y_ref, dx_ref, ends_ref, *grads_in = refs[:9]
    out_tok, out_mem, grad_tok, grad_mem, *grads_out = refs[9:]
    out_tok[0] = y_ref[0, :seg_len, :]
    grad_tok[0] = dx_ref[0, :seg_len, :]
    ends = ends_ref[0]
    out_mem[0] = dot(picks(mem, MEM_ROWS, 0, 0, mem), ends, 1, 0).astype(LOW)
    grad_mem[0] = dot(picks(mem, MEM_ROWS, mem, 0, mem), ends, 1, 0).astype(LOW)

    @pl.when(pl.program_id(0) == 0)
    def _():
        for a, b in zip(grads_in, grads_out):
            b[...] = a[...]


def last(y, dx, ends, grads, seg_len, mem):
    micro, _, D = y.shape
    S = jax.ShapeDtypeStruct

    def block(n):
        return pl.BlockSpec((1, n, D), lambda i: (i, 0, 0))

    whole = [pl.BlockSpec(g.shape, lambda i: (0, 0)) for g in grads]
    return pl.pallas_call(
        functools.partial(last_kernel, mem, seg_len), grid=(micro,),
        out_shape=[S((micro, n, D), LOW) for n in (seg_len, mem, seg_len, mem)] + [S(g.shape, F32) for g in grads],
        in_specs=[block(TOK), block(TOK), block(MEM_ROWS)] + whole,
        out_specs=[block(n) for n in (seg_len, mem, seg_len, mem)] + whole,
        compiler_params=pltpu.CompilerParams(vmem_limit_bytes=32 << 20),
    )(y, dx, ends, *grads)


def plain_keep(orders, device, levels):
    sources = jnp.arange(orders.shape[1], dtype=jnp.int32)
    holders = [jnp.full((orders.shape[0],), device, jnp.int32)]
    for bit in range(levels):
        stride = 2 ** (bit + 1)
        position = sources - sources % stride + orders % stride
        holders.append(jnp.sum(jnp.where(position == device, sources, 0), 1))
    return jnp.stack([a == b for a, b in zip(holders[:-1], holders[1:])], 1)


def plain_travel(keep, payload, order):
    size = lax.axis_size("dp")
    for bit in order:
        theirs = lax.ppermute(payload, "dp", [(i, i ^ 1 << bit) for i in range(size)])
        payload = jnp.where(keep[:, bit][:, None, None], payload, theirs)
    return payload


def both_cores(value):
    return lax.all_gather(value, "tensor", axis=0)


def plain_scatter(keep, outs):
    y, dx, payload, vec, late, *grads = outs
    payload = plain_travel(keep, payload, range(keep.shape[1]))
    parts = []
    for g in grads:
        g = lax.psum_scatter(g.reshape(2, -1, g.shape[-1]).astype(F32), "tensor", scatter_dimension=0)
        parts.append(lax.psum_scatter(g, "dp", scatter_dimension=0, tiled=True))
    everywhere = ("dp", "tensor")
    return [both_cores(y), both_cores(dx), both_cores(payload), lax.psum(vec, everywhere), lax.psum(late, everywhere), *parts]


def local(
    tokens, memory, lengths, owners, w_query, w_key, w_value, w_out, w_up, w_down, b_query, b_value, b_up,
    b_out, b_down, gain_attn, shift_attn, gain_ffn, shift_ffn, cot_tokens, cot_memory,
):
    micro, seg_len, depth = tokens.shape
    mem = memory.shape[1]
    size = lax.axis_size("dp")
    device, t = lax.axis_index("dp"), lax.axis_index("tensor")
    kernels = size == math.prod(GRID)
    rows, width = w_query.shape
    hidden = w_up.shape[1]
    pairs = width // PAIR
    vectors = (b_out, b_down, gain_attn, shift_attn, gain_ffn, shift_ffn)
    columns = jnp.pad(jnp.stack(vectors, 1), ((0, 0), (0, PAIR - len(vectors))))
    bias = jnp.concatenate([b_query, b_value, b_up]).astype(F32)[None]
    if kernels:
        weights = [w_query, w_key, w_value, w_out, w_up, w_down, columns]
        mem_a, mem_b = memory, cot_memory
    else:
        mine = micro // 2
        own = lambda array: lax.dynamic_slice_in_dim(array, t * mine, mine, 0)
        keep = plain_keep(own(owners), device, size.bit_length() - 1)
        payload = jnp.pad(jnp.concatenate([own(memory), own(cot_memory)], 1), ((0, 0), (0, MEM_ROWS - 2 * mem), (0, 0)))
        mem_a = mem_b = plain_travel(keep, payload, range(keep.shape[1] - 1, -1, -1))
        by_pair = jnp.concatenate([w[:, i * PAIR:(i + 1) * PAIR] for i in range(pairs) for w in (w_query, w_key, w_value)], 1)
        shards = [by_pair, jnp.concatenate([w_out, columns], 1), w_up, w_down]
        weights = [both_cores(lax.all_gather(s, "dp", axis=0, tiled=True)) for s in shards]
        bias = both_cores(bias)
    *kept, sums = front(lengths, owners, bias, mem_a, mem_b, tokens, cot_tokens, weights, width, hidden, mem, kernels, 1)
    outs = back(owners, sums, kept, width, hidden, mem, rows, kernels, 2)
    if not kernels:
        outs = plain_scatter(keep, outs)
    y, dx, ends, vec, late, *grads = outs
    out_tok, out_mem, grad_tok, grad_mem, *grads = last(
        y.reshape(micro, ROWS, depth), dx.reshape(micro, ROWS, depth), ends.reshape(micro, MEM_ROWS, depth), grads, seg_len, mem)
    lines = lax.dynamic_slice(vec[:6], (0, device * rows), (6, rows))
    up_sum = lax.dynamic_slice_in_dim(vec, 8 + 2 * t, 2, 0).reshape(hidden)
    late = lax.dynamic_index_in_dim(late, t, 0, False)[:pairs].reshape(pairs, 3, PAIR)
    return (
        out_tok, out_mem, grad_tok, grad_mem, *grads,
        *(lines[i] for i in range(6)), late[:, 0].reshape(width), late[:, 2].reshape(width), up_sum,
    )


def solution(mesh):
    rows, both, split, every = P("dp", None, None), P("dp", "tensor"), P("tensor"), P("dp")
    return jax.shard_map(
        local,
        mesh=mesh,
        in_specs=(rows, rows, P(), P(), *[both] * 6, *[split] * 3, *[every] * 6, rows, rows),
        out_specs=(*[rows] * 4, *[both] * 6, *[every] * 6, *[split] * 3),
        check_vma=False,
    )
```

```python
import functools
import math

import jax
import jax.numpy as jnp
from jax import lax
from jax.experimental import pallas as pl
from jax.experimental.pallas import tpu as pltpu
from jax.sharding import PartitionSpec as P

MESH = pl.DeviceIdType.MESH
GRID = (4, 2, 2)
HEAD = 64
TOK = 512
TAIL = 32
ROWS = TOK + TAIL
PAIR = 128
masked_score = -1000000000.0
epsilon = 1e-05
F32, LOW = jnp.float32, jnp.bfloat16


def dot(a, b, left, right):
    return lax.dot_general(a, b, (((left,), (right,)), ((), ())), preferred_element_type=F32)


def mat(ref, half, cols):
    got = ref[half, ..., cols]
    return got.reshape(-1, got.shape[-1])


def live_at(position, count, mem):
    return (position < count) | ((position >= TOK) & (position < TOK + mem))


def normed(values):
    mean = jnp.mean(values, -1, keepdims=True)
    centered = values - mean
    inv = lax.rsqrt(jnp.mean(centered * centered, -1, keepdims=True) + epsilon)
    return centered * inv, inv


def norm_back(scaled, unit, inv):
    return inv * (scaled - jnp.mean(scaled, -1, keepdims=True) - unit * jnp.mean(scaled * unit, -1, keepdims=True))


def fold(total_ref, row, value):
    total_ref[row:row + 1, :] += jnp.sum(value, 0, keepdims=True)


def project(x_ref, w_ref, bias_ref, q_ref, k_ref, v_ref, seg, i, pairs):
    wide = 3 * PAIR
    cols = pl.ds(pl.multiple_of(i * wide, PAIR), wide)
    rows = x_ref[pl.ds(pl.multiple_of(seg * ROWS, 32), ROWS), :]
    lane = lax.broadcasted_iota(jnp.int32, (1, PAIR), 1)
    got = dot(rows, jnp.concatenate([mat(w_ref, 0, cols), mat(w_ref, 1, cols)], 1), 1, 0)
    for half in range(2):
        p = half * pairs + i
        at = half * wide
        here = pl.ds(pl.multiple_of(i * PAIR, PAIR), PAIR)
        there = pl.ds(pl.multiple_of((pairs + i) * PAIR, PAIR), PAIR)
        q = (got[:, at:at + PAIR] + bias_ref[half, 0:1, here]) * (1.0 / math.sqrt(HEAD))
        q_ref[seg, p, 0] = jnp.where(lane < HEAD, q, 0.0).astype(LOW)
        q_ref[seg, p, 1] = jnp.where(lane < HEAD, 0.0, q).astype(LOW)
        k_ref[seg, p] = got[:, at + PAIR:at + 2 * PAIR].astype(LOW)
        v_ref[seg, p] = (got[:, at + 2 * PAIR:at + 3 * PAIR] + bias_ref[half, 0:1, there]).astype(LOW)


def attend(q_ref, k_ref, v_ref, o_ref, linv_ref, e_slot, count, mem, seg, p):
    col = lax.broadcasted_iota(jnp.int32, (1, ROWS), 1)
    lane = lax.broadcasted_iota(jnp.int32, (1, PAIR), 1)
    masking = jnp.where(live_at(col, count, mem), 0.0, masked_score)
    keys = k_ref[seg, p]
    values = jnp.concatenate([v_ref[seg, p], jnp.ones((ROWS, PAIR), LOW)], 1)
    got = []
    for j in range(2):
        scores = dot(q_ref[seg, p, j], keys, 1, 1) + masking
        peak = jnp.max(scores, -1, keepdims=True)
        e_slot[j] = jnp.exp(scores - peak).astype(LOW)
        got.append(dot(e_slot[j], values, 1, 0))
    first = lane < HEAD
    linv = 1.0 / jnp.where(first, got[0][:, PAIR:], got[1][:, PAIR:])
    linv_ref[seg, p] = linv
    o_ref[seg, p] = (jnp.where(first, got[0][:, :PAIR], got[1][:, :PAIR]) * linv).astype(LOW)


def attend_back(q_ref, k_ref, v_ref, o_ref, linv_ref, do_ref, e_slot, ds_ref, out_ref, seg, p, half, i):
    lane = lax.broadcasted_iota(jnp.int32, (1, PAIR), 1)
    keys, values = k_ref[...], v_ref[...]
    scaled = do_ref[seg, p].astype(F32) * linv_ref[...]
    product = scaled * o_ref[...].astype(F32)
    dq, dk, dv = [], None, None
    for j in range(2):
        mine = (lane < HEAD) if j == 0 else (lane >= HEAD)
        mine_low = jnp.where(mine, scaled, 0.0).astype(LOW)
        delta = jnp.sum(jnp.where(mine, product, 0.0), -1, keepdims=True)
        gap = dot(mine_low, values, 1, 1) - delta
        ds_ref[j] = (e_slot[j].astype(F32) * gap).astype(LOW)
        dq.append(dot(ds_ref[j], keys, 1, 0))
        one_v = dot(e_slot[j], mine_low, 0, 0)
        one_k = dot(ds_ref[j], q_ref[j], 0, 0)
        dv = one_v if dv is None else dv + one_v
        dk = one_k if dk is None else dk + one_k
    rows = pl.ds(pl.multiple_of(seg * ROWS, 32), ROWS)
    dq = jnp.where(lane < HEAD, dq[0], dq[1]) * (1.0 / math.sqrt(HEAD))
    for kind, value in enumerate((dq, dk, dv)):
        out_ref[half, rows, pl.ds(pl.multiple_of((3 * i + kind) * PAIR, PAIR), PAIR)] = value.astype(LOW)


class Place:
    def __init__(self):
        me = lax.axis_index("dp")
        self.t = lax.axis_index("tensor")
        self.x = me % 2
        self.y = (me // 2) % 2
        self.z = me // 4
        self.nt, self.nx, self.ny = 1 - self.t, 1 - self.x, 1 - self.y
        self.px = self.at(self.z, self.y, self.nx)
        self.py = self.at(self.z, self.ny, self.x)
        self.zs = [(self.z + d) % 4 for d in (1, 2, 3)]
        self.zb = [(self.z + 4 - d) % 4 for d in (1, 2, 3)]
        self.pz = [self.at(z, self.y, self.x) for z in self.zs]
        self.pz1 = self.at(self.z + 1 - 2 * (self.z % 2), self.y, self.x)
        self.pz2 = self.at((self.z + 2) % 4, self.y, self.x)
        self.pc = (me, self.nt)

    def at(self, z, y, x):
        return (z * 4 + y * 2 + x, self.t)

    def greet(self):
        barrier = pltpu.get_barrier_semaphore()
        devices = [self.px, self.py, *self.pz, self.pc]
        for device in devices:
            pl.semaphore_signal(barrier, inc=1, device_id=device, device_id_type=MESH)
        pl.semaphore_wait(barrier, len(devices))


class Wire:
    def __init__(self, send, recv):
        self.send, self.recv, self.count, self.open = send, recv, 0, {}

    def start(self, src, dst, device, landing):
        k = self.count
        self.count += 1

        def copy(a, b):
            return pltpu.make_async_remote_copy(
                src_ref=a, dst_ref=b, send_sem=self.send.at[k], recv_sem=self.recv.at[k],
                device_id=device, device_id_type=MESH)

        copy(src(), dst()).start()
        self.open[k] = lambda: copy(src(), dst()).wait_send()
        return lambda: copy(landing(), landing()).wait_recv()

    def sent(self, k):
        self.open.pop(k)()

    def drain(self):
        for k in list(self.open):
            self.sent(k)


class Gather:
    def __init__(self, wire, place, out, at, width, order):
        self.wire, self.p, self.out = wire, place, out
        self.cols, self.order, self.landed, self.crossing = pl.ds(at, width), order, [], []

    def view(self, z, y, x, half=None):
        return lambda: self.out.at[self.p.t if half is None else half, z, y, x, :, self.cols]

    def stage(self, s):
        p, every = self.p, slice(None)
        for wait in self.landed:
            wait()
        self.landed = []
        home = self.view(p.z, p.y, p.x)
        if self.order == "zxy":
            if s == 0:
                for k in range(3):
                    self.go(home, None, p.pz[k], self.view(p.zb[k], p.y, p.x))
            elif s == 1:
                self.go(self.view(every, p.y, p.x), None, p.px, self.view(every, p.y, p.nx))
                self.cross(every, p.y, p.x)
            elif s == 2:
                self.go(self.view(every, p.y, every), None, p.py, self.view(every, p.ny, every))
                self.cross(every, p.y, p.nx)
            else:
                self.cross(every, p.ny, every)
        else:
            if s == 0:
                self.go(home, None, p.py, self.view(p.z, p.ny, p.x))
            elif s == 1:
                for k in range(3):
                    self.go(self.view(p.z, every, p.x), None, p.pz[k], self.view(p.zb[k], every, p.x))
                self.cross(p.z, every, p.x)
            elif s == 2:
                self.go(self.view(every, every, p.x), None, p.px, self.view(every, every, p.nx))
                for k in range(3):
                    self.cross(p.zb[k], every, p.x)
            else:
                self.cross(every, every, p.nx)

    def go(self, src, dst, device, landing):
        self.landed.append(self.wire.start(src, src if dst is None else dst, device, landing))

    def cross(self, z, y, x):
        mine = self.view(z, y, x)
        self.crossing.append(self.wire.start(mine, mine, self.p.pc, self.view(z, y, x, self.p.nt)))

    def whole(self):
        for wait in self.crossing:
            wait()
        self.crossing = []


class Travel:
    def __init__(self, wire, place, keep, payload, held, landing, order):
        self.wire, self.p, self.keep, self.landed = wire, place, keep, None
        self.held, self.landing, self.order, self.payload = held, landing, order, payload

    def stage(self, s):
        p = self.p
        if s > 0:
            self.landed()
            before = self.payload if s == 1 else self.held.at[s - 2]
            for m in range(self.payload.shape[0]):
                stay = self.keep[m][self.order[s - 1]]
                mine, theirs = before[m].astype(F32), self.landing[s - 1, m].astype(F32)
                self.held[s - 1, m] = jnp.where(stay, mine, theirs).astype(self.held.dtype)
        if s < len(self.order):
            device = [p.px, p.py, p.pz1, p.pz2][self.order[s]]
            land = lambda: self.landing.at[s]
            self.landed = self.wire.start(lambda: self.payload if s == 0 else self.held.at[s - 1], land, device, land)


def keep_flags(owners_ref, row, device, levels):
    holders = [device]
    for bit in range(levels):
        stride = 2 ** (bit + 1)
        found = device * 0
        for source in range(owners_ref.shape[1]):
            position = source - source % stride + lax.rem(owners_ref[row, source], stride)
            found = found + jnp.where(position == device, source, 0)
        holders.append(found)
    return [a == b for a, b in zip(holders[:-1], holders[1:])]


def valid_count(lengths_ref, index, seg_len):
    start, valid = index * 0, index * 0
    for j in range(lengths_ref.shape[0]):
        length = lengths_ref[j]
        count = lax.div(length + (seg_len - 1), seg_len)
        inside = (start <= index) & (index < start + count)
        valid = valid + jnp.where(inside, jnp.minimum(length - (index - start) * seg_len, seg_len), 0)
        start = start + count
    return valid


G384 = (('yzx', 0, 128), ('zxy', 128, 256))
G512 = (('yzx', 0, 128), ('zxy', 128, 384))
G768 = (('yzx', 0, 128), ('zxy', 128, 256), ('yzx', 384, 128), ('zxy', 512, 256))
CHUNKS = ((0, 0, G384), (0, 384, G384), (0, 768, G384), (1, 0, G512), (2, 0, G768), (2, 768, G768), (3, 0, G768), (3, 768, G768))
GATHER = (
    ((0, 0, 0), (0, 1, 0), (1, 0, 0), (1, 1, 0), (0, 0, 1), (0, 1, 1), (2, 0, 0), (2, 1, 0), (1, 0, 1), (1, 1, 1), (0, 0, 2), (0, 1, 2), (3, 0, 0), (3, 1, 0), (2, 0, 1), (2, 1, 1), (1, 0, 2), (1, 1, 2), (0, 0, 3), (0, 1, 3)),
    (),
    ((4, 0, 0), (4, 1, 0), (3, 0, 1), (3, 1, 1), (2, 0, 2), (2, 1, 2), (1, 0, 3), (1, 1, 3)),
    (),
    ((4, 2, 0), (4, 3, 0), (4, 0, 1), (4, 1, 1), (3, 0, 2), (3, 1, 2), (2, 0, 3), (2, 1, 3)),
    (),
    ((5, 0, 0), (5, 1, 0), (4, 2, 1), (4, 3, 1), (4, 0, 2), (4, 1, 2), (3, 0, 3), (3, 1, 3)),
    (),
    ((5, 2, 0), (5, 3, 0), (5, 0, 1), (5, 1, 1), (4, 2, 2), (4, 3, 2), (4, 0, 3), (4, 1, 3)),
    (),
    ((6, 0, 0), (6, 1, 0), (5, 2, 1), (5, 3, 1), (5, 0, 2), (5, 1, 2), (4, 2, 3), (4, 3, 3)),
    (),
    ((6, 2, 0), (6, 3, 0), (6, 0, 1), (6, 1, 1), (5, 2, 2), (5, 3, 2), (5, 0, 3), (5, 1, 3)),
    ((7, 0, 0), (7, 1, 0), (6, 2, 1), (6, 3, 1), (6, 0, 2), (6, 1, 2), (5, 2, 3), (5, 3, 3)),
    ((7, 2, 0), (7, 3, 0), (7, 0, 1), (7, 1, 1), (6, 2, 2), (6, 3, 2), (6, 0, 3), (6, 1, 3)),
    (),
    (),
    (),
    ((7, 2, 1), (7, 3, 1), (7, 0, 2), (7, 1, 2), (6, 2, 3), (6, 3, 3)),
    (),
    ((7, 2, 2), (7, 3, 2), (7, 0, 3), (7, 1, 3)),
    (),
    ((7, 2, 3), (7, 3, 3)),
    (),
    (),
    (),
    (),
    (),
    (),
)


class Copies:
    def __init__(self, sems):
        self.sems, self.count = sems, 0

    def start(self, src, dst):
        k = self.count
        self.count += 1
        pltpu.make_async_copy(src(), dst(), self.sems.at[k]).start()
        return lambda: pltpu.make_async_copy(src(), dst(), self.sems.at[k]).wait()


def front_kernel(kernels, mem, seg_len, width, *refs):
    n_in = 14 if kernels else 11
    lengths_ref, owners_ref, bias_in, mem_a, mem_b, tok_in, cot_in = refs[:7]
    weights_in = refs[7:n_in]
    (wqkv_out, wout_out, wup_out, wdown_out, q_out, k_out, v_out, o_out, linv_out, e_out, xt_out, x1t_out, unit_out, inv_out,
     dh_out, df_out, dft_out, g_out, d_out, y_out, sums_ref, tail_ref) = refs[n_in:n_in + 22]
    (wqkv, wout, wup, wdown, bias_ref, payload, held, landing, tok_ref, x_ref, cot_ref, vec_ref, o_ref, dh_ref, low_ref, unit_ref,
     inv_ref, flip_ref, send, recv, here, e_sems) = refs[-22:]
    weights = (wqkv, wout, wup, wdown)
    R = 2 * ROWS
    pairs = width // PAIR
    D = x_ref.shape[1]
    hidden = wup.shape[-1]
    copies = Copies(here)
    t = lax.axis_index("tensor")
    device = lax.axis_index("dp")
    loads = []
    for k, (a, s) in enumerate(((tok_in, 0), (tok_in, 1), (cot_in, 0), (cot_in, 1))):
        loads.append(copies.start(lambda a=a, s=s: a.at[2 * t + s], lambda k=k: tok_ref.at[k]))
    if kernels:
        place = Place()
        wire = Wire(send, recv)

        def mine(c, cols):
            return lambda: weights[c].at[place.t, place.z, place.y, place.x, :, cols]

        own = []
        for i in range(pairs):
            for kind in range(3):
                cols = pl.ds(i * PAIR, PAIR)
                own.append(copies.start(lambda kind=kind, cols=cols: weights_in[kind].at[:, cols], mine(0, pl.ds((3 * i + kind) * PAIR, PAIR))))
        own.append(copies.start(lambda: weights_in[3], mine(1, pl.ds(0, width))))
        own.append(copies.start(lambda: weights_in[6], mine(1, pl.ds(width, PAIR))))
        own.append(copies.start(lambda: weights_in[4], mine(2, pl.ds(0, hidden))))
        own.append(copies.start(lambda: weights_in[5], mine(3, pl.ds(0, hidden))))
        own_bias = copies.start(lambda: bias_in, lambda: bias_ref.at[place.t])
        for m in range(2):
            payload[0, m] = mem_a[2 * t + m]
            payload[1, m] = mem_b[2 * t + m]
        place.greet()
        keep = [keep_flags(owners_ref, 2 * t + m, device, 4) for m in range(2)]
        travel = Travel(wire, place, keep, payload.at[0], held.at[0], landing.at[0], (3, 2, 1, 0))
        second = Travel(wire, place, keep, payload.at[1], held.at[1], landing.at[1], (3, 2, 1, 0))
        parts = []
        for c, at, cuts in CHUNKS:
            parts.append([Gather(wire, place, weights[c], at + first, wide, order) for order, first, wide in cuts])

        def tick(point):
            for c, part, s in GATHER[point]:
                parts[c][part].stage(s)

        def ready(c):
            for part in parts[c]:
                part.whole()

        travel.stage(0)
        for wait in own:
            wait()
        bias_wait = wire.start(lambda: bias_in, lambda: bias_ref.at[place.t], place.pc, lambda: bias_ref.at[place.nt])
        for k, (c, part, s) in enumerate(GATHER[0]):
            parts[c][part].stage(s)
            if k in (1, 5, 11, 19):
                travel.stage((1, 5, 11, 19).index(k) + 1)
        own_bias()
        bias_wait()
        moved, moved_cot = held.at[0, 3], held.at[1, 3]
        later = second.stage
    else:
        fetched = [copies.start(lambda c=c: weights_in[c], lambda c=c: weights[c]) for c in range(4)]
        fetched.append(copies.start(lambda: bias_in, lambda: bias_ref))
        for wait in fetched:
            wait()
        moved, moved_cot = mem_a, mem_b
        tick = ready = later = lambda step: None
    counts = [valid_count(lengths_ref, device * 4 + 2 * t + s, seg_len) for s in range(2)]
    for wait in loads:
        wait()
    for s in range(2):
        for k, ref in enumerate((x_ref, cot_ref)):
            ref[s * ROWS + TOK - 16:(s + 1) * ROWS, :] = jnp.zeros((16 + TAIL, D), LOW)
            ref[s * ROWS:s * ROWS + seg_len, :] = tok_ref[2 * k + s]
        x_ref[s * ROWS + TOK:s * ROWS + TOK + mem, :] = moved[s]
    flip_ref[...] = x_ref[...].T
    saves = [copies.start(lambda: flip_ref, lambda: xt_out)]

    def attention(q_ref, k_ref, v_ref, linv_ref, slots):
        def e_copy(seg, p, slot):
            return pltpu.make_async_copy(slots.at[slot], e_out.at[seg, p], e_sems.at[slot])

        def step(n, carry):
            i, seg, half = n // 4, (n // 2) % 2, n % 2
            for k in range(12):
                @pl.when(n == k)
                def _():
                    tick(1 + k)
                    if k in (1, 3, 5, 7, 9):
                        later(k // 2)
                    if k in (4, 8):
                        ready(k // 4)

            @pl.when(half == 0)
            def _():
                project(x_ref, wqkv, bias_ref, q_ref, k_ref, v_ref, seg, i, pairs)

            count = jnp.where(seg == 0, counts[0], counts[1])

            @pl.when(n > 1)
            def _():
                e_copy(seg, half * pairs + i, half).wait()

            attend(q_ref, k_ref, v_ref, o_ref, linv_ref, slots.at[half], count, mem, seg, half * pairs + i)
            e_copy(seg, half * pairs + i, half).start()
            return carry

        ready(0)
        lax.fori_loop(0, 4 * pairs, step, 0)
        done = []
        for a, b in ((q_ref, q_out), (k_ref, k_out), (v_ref, v_out), (o_ref, o_out), (linv_ref, linv_out), (wqkv, wqkv_out)):
            done.append(copies.start(lambda a=a: a, lambda b=b: b))
        tick(13)
        ready(3)
        done.append(copies.start(lambda: wout, lambda: wout_out))
        for half in range(2):
            e_copy(0, 0, half).wait()
        for wait in done:
            wait()

    six = (2, 2 * pairs, ROWS, PAIR)
    pl.run_scoped(
        attention, pltpu.VMEM((2, 2 * pairs, 2, ROWS, PAIR), LOW), pltpu.VMEM(six, LOW), pltpu.VMEM(six, LOW),
        pltpu.VMEM(six, F32), pltpu.VMEM((2, 2, ROWS, ROWS), LOW))

    sums_ref[...] = jnp.zeros_like(sums_ref)
    vec_ref[...] = mat(wout, 0, slice(width, width + PAIR)).astype(F32).T[:8]
    vec = {n: vec_ref[k:k + 1, :] for k, n in enumerate(("b_out", "b_down", "gain_attn", "shift_attn", "gain_ffn", "shift_ffn"))}

    def out_step(s, carry):
        rows = pl.ds(pl.multiple_of(s * ROWS, ROWS), ROWS)
        h = x_ref[rows, :].astype(F32) + vec["b_out"]
        for t in range(2):
            o = jnp.concatenate([o_ref[s, t * pairs + i] for i in range(pairs)], 1)
            h = h + dot(o, mat(wout, t, slice(0, width)), 1, 1)
        unit, inv = normed(h)
        x1 = unit * vec["gain_attn"] + vec["shift_attn"]
        dh_ref[rows, :] = x1
        low_ref[rows, :] = x1.astype(LOW)
        unit_ref[rows, :] = unit.astype(LOW)
        inv_ref[rows, :] = inv
        return carry

    lax.fori_loop(0, 2, out_step, 0)
    tick(14)
    tick(15)
    for wait in saves:
        wait()
    flip_ref[...] = low_ref[...].T
    saves = [copies.start(lambda a=a: a, lambda b=b: b) for a, b in ((flip_ref, x1t_out), (unit_ref, unit_out), (inv_ref, inv_out))]

    def ffn(g_ref, d_ref):
        for s in range(2):
            cot_ref[s * ROWS + TOK:s * ROWS + TOK + mem, :] = moved_cot[s]
        tile = min(hidden // 2, 256)
        part = R // 4

        def up_cols(first, count, base):
            def up_step(k, carry):
                t = k % 2
                at = first + (k // 2) * tile
                for n in range(2 * count):
                    @pl.when(k == n)
                    def _():
                        tick(base + n)
                        if n == 0:
                            ready(4 + (base - 16) // 6)
                cols = pl.ds(pl.multiple_of(at, PAIR), tile)
                u = dot(low_ref[...], mat(wup, t, cols), 1, 0)
                u = u + bias_ref[t, 0:1, pl.ds(pl.multiple_of(2 * width + at, PAIR), tile)]
                phi = 0.5 * (1.0 + lax.erf(u * (1.0 / math.sqrt(2.0))))
                g_ref[t, :, cols] = (u * phi).astype(LOW)
                d_ref[t, :, cols] = (phi + u * (jnp.exp(-0.5 * u * u) * (1.0 / math.sqrt(2.0 * math.pi)))).astype(LOW)
                return carry

            lax.fori_loop(0, 2 * count, up_step, 0)

        up_cols(0, hidden // 2 // tile, 16)
        up_cols(hidden // 2, hidden // 2 // tile, 22)
        done = [copies.start(lambda a=a: a, lambda b=b: b) for a, b in ((wup, wup_out), (g_ref, g_out), (d_ref, d_out))]
        tick(28)
        ready(6)
        ready(7)
        done.append(copies.start(lambda: wdown, lambda: wdown_out))

        def down_step(s, carry):
            rows = pl.ds(pl.multiple_of(s * part, part), part)
            h = dh_ref[rows, :] + vec["b_down"]
            for t in range(2):
                h = h + dot(g_ref[t, rows, :], mat(wdown, t, slice(None)), 1, 1)
            unit, inv = normed(h)
            count = jnp.where(s < 2, counts[0], counts[1])
            at = lax.broadcasted_iota(jnp.int32, (part, 1), 0) + (s % 2) * part
            live = jnp.where(live_at(at, count, mem), 1.0, 0.0)
            x_ref[rows, :] = ((unit * vec["gain_ffn"] + vec["shift_ffn"]) * live).astype(LOW)
            dy = cot_ref[rows, :].astype(F32) * live
            fold(sums_ref, 4, dy * unit)
            fold(sums_ref, 5, dy)
            dh = norm_back(dy * vec["gain_ffn"], unit, inv)
            fold(sums_ref, 1, dh)
            dh_ref[rows, :] = dh
            cot_ref[rows, :] = dh.astype(LOW)
            return carry

        lax.fori_loop(0, 4, down_step, 0)
        for wait in done:
            wait()

    pl.run_scoped(ffn, pltpu.VMEM((2, R, hidden), LOW), pltpu.VMEM((2, R, hidden), LOW))
    for s in range(2):
        tok_ref[s] = x_ref[s * ROWS:s * ROWS + seg_len, :]
        tail_ref[s] = x_ref[s * ROWS + TOK:s * ROWS + TOK + mem, :]
    ends = [copies.start(lambda a=a: a, lambda b=b: b) for a, b in ((dh_ref, dh_out), (cot_ref, df_out))]
    ends.append(copies.start(lambda: tok_ref.at[pl.ds(0, 2)], lambda: y_out))
    for wait in saves:
        wait()
    flip_ref[...] = cot_ref[...].T
    ends.append(copies.start(lambda: flip_ref, lambda: dft_out))
    for wait in ends:
        wait()
    if kernels:
        wire.drain()


def front(lengths, owners, bias, mem_a, mem_b, tokens, cots, weights, width, hidden, mem, kernels, cid):
    seg_len, D = tokens.shape[1:]
    R = 2 * ROWS
    pairs = width // PAIR
    S, V = jax.ShapeDtypeStruct, pltpu.VMEM
    hbm, vmem, smem = (pl.BlockSpec(memory_space=m) for m in (pl.ANY, pltpu.VMEM, pltpu.SMEM))
    full = (2, *GRID, D // math.prod(GRID)) if kernels else (2, D)
    six = (2, 2 * pairs, ROWS, PAIR)
    payload = (2, mem, D)
    count = 9 + sum(8 if part[0] == "zxy" else 10 for _, _, cuts in CHUNKS for part in cuts)
    shapes = [(*full, w) for w in (3 * width, width + PAIR, hidden, hidden)]
    params = dict(collective_id=cid, has_side_effects=True) if kernels else {}
    return pl.pallas_call(
        functools.partial(front_kernel, kernels, mem, seg_len, width),
        out_shape=[
            *(S(s, LOW) for s in shapes), S((2, 2 * pairs, 2, ROWS, PAIR), LOW), S(six, LOW), S(six, LOW), S(six, LOW), S(six, F32),
            S((2, 2 * pairs, 2, ROWS, ROWS), LOW), S((D, R), LOW), S((D, R), LOW), S((R, D), LOW), S((R, 1), F32), S((R, D), F32),
            S((R, D), LOW), S((D, R), LOW), S((2, R, hidden), LOW), S((2, R, hidden), LOW), S((2, seg_len, D), LOW), S((8, D), F32), S(payload, LOW)],
        in_specs=[smem, smem, vmem, vmem, vmem] + [hbm] * (2 + len(weights)),
        out_specs=[hbm] * 20 + [vmem] * 2,
        scratch_shapes=[
            *(V(s, LOW) for s in shapes), V((2, 1, 2 * width + hidden), F32), V((2, *payload), LOW), V((2, 4, *payload), LOW), V((2, 4, *payload), LOW),
            V((4, seg_len, D), LOW), V((R, D), LOW), V((R, D), LOW), V((8, D), F32), V(six, LOW), V((R, D), F32), V((R, D), LOW),
            V((R, D), LOW), V((R, 1), F32), V((D, R), LOW),
            pltpu.SemaphoreType.DMA((count,)), pltpu.SemaphoreType.DMA((count,)), pltpu.SemaphoreType.DMA((40,)),
            pltpu.SemaphoreType.DMA((2,))],
        compiler_params=pltpu.CompilerParams(vmem_limit_bytes=63 << 20, **params),
    )(lengths, owners, bias, mem_a, mem_b, tokens, cots, *weights)


class Scatter:
    def __init__(self, wire, place, acc, sink, cols, order, landings):
        self.wire, self.p, self.acc, self.sink = wire, place, acc, sink
        self.cols, self.order, self.landed = cols, order, []
        self.r1, self.r2, self.r3 = landings

    def view(self, z, y, x):
        return lambda: self.acc.at[z, y, x, :, self.cols]

    def sum(self, z, y, x, terms):
        total = self.acc[z, y, x, :, self.cols].astype(F32)
        for term in terms:
            total = total + term.astype(F32)
        return total

    def add(self, z, y, x, *terms):
        if len(terms) == 1:
            self.acc[z, y, x, :, self.cols] = self.acc[z, y, x, :, self.cols] + terms[0]
            return
        self.acc[z, y, x, :, self.cols] = self.sum(z, y, x, terms).astype(self.acc.dtype)

    def finish(self, *terms):
        self.sink(self.sum(self.p.z, self.p.y, self.p.x, terms))

    def stage(self, s):
        p, every = self.p, slice(None)
        for wait in self.landed:
            wait()
        self.landed = []
        r1, r2, r3 = self.r1, self.r2, self.r3
        if self.order == "yxz":
            if s == 0:
                self.go(self.view(every, p.ny, every), lambda: r1, p.py)
            elif s == 1:
                for z in range(4):
                    for x in range(2):
                        self.add(z, p.y, x, r1[z, x])
                self.go(self.view(every, p.y, p.nx), lambda: r2, p.px)
            elif s == 2:
                for z in range(4):
                    self.add(z, p.y, p.x, r2[z])
                for k in range(3):
                    self.go(self.view(p.zs[k], p.y, p.x), lambda k=k: r3.at[k], p.pz[k])
            else:
                self.finish(r3[0], r3[1], r3[2])
        else:
            if s == 0:
                self.go(self.view(every, every, p.nx), lambda: r1, p.px)
            elif s == 1:
                for z in range(4):
                    for y in range(2):
                        self.add(z, y, p.x, r1[z, y])
                for k in range(3):
                    self.go(self.view(p.zs[k], every, p.x), lambda k=k: r2.at[k], p.pz[k])
            elif s == 2:
                for y in range(2):
                    self.add(p.z, y, p.x, r2[0, y], r2[1, y], r2[2, y])
                self.go(self.view(p.z, p.ny, p.x), lambda: r3, p.py)
            else:
                self.finish(r3[...])

    def go(self, src, landing, device):
        self.landed.append(self.wire.start(src, landing, device, landing))


def scatter_shapes(rows, order, wide):
    V = pltpu.VMEM
    if order == "xzy":
        return [V((4, 2, rows, wide), LOW), V((3, 2, rows, wide), LOW), V((rows, wide), LOW)]
    return [V((4, 2, rows, wide), LOW), V((4, rows, wide), LOW), V((3, rows, wide), LOW)]


class Total:
    def __init__(self, wire, place, vec, out, hops, vz):
        self.wire, self.p, self.landed = wire, place, []
        self.vec, self.out, self.hops, self.vz = vec, out, hops, vz

    def stage(self, s):
        p, hops = self.p, self.hops
        for wait in self.landed:
            wait()
        self.landed = []
        if s == 0:
            self.go(lambda: self.vec, lambda: hops.at[0], p.pc)
        elif s < 4:
            hops[2 * s - 1] = (self.vec[...] if s == 1 else hops[2 * s - 3]) + hops[2 * s - 2]
            if s < 3:
                self.go(lambda: hops.at[2 * s - 1], lambda: hops.at[2 * s], (p.px, p.py)[s - 1])
            else:
                for k in range(3):
                    self.go(lambda: hops.at[5], lambda k=k: self.vz.at[k], p.pz[k])
        else:
            self.out[...] = hops[5] + self.vz[0] + self.vz[1] + self.vz[2]

    def go(self, src, landing, device):
        self.landed.append(self.wire.start(src, landing, device, landing))


S384 = (('xzy', 0, 128), ('yxz', 128, 256))
S768 = (('xzy', 0, 128), ('yxz', 128, 256), ('xzy', 384, 128), ('yxz', 512, 256))
SUMS = ((0, 0, 768, S768), (0, 768, 768, S768), (1, 0, 768, S768), (1, 768, 768, S768), (2, 0, 384, S384), (3, 0, 384, S384), (3, 384, 384, S384), (3, 768, 384, S384))
SCATTER = (
    ((0, 2, 0), (0, 3, 0), (0, 0, 0), (0, 1, 0)),
    ((1, 2, 0), (1, 3, 0), (1, 0, 0), (1, 1, 0)),
    (),
    ((0, 2, 1), (0, 3, 1), (0, 0, 1), (0, 1, 1)),
    ((2, 2, 0), (2, 3, 0), (2, 0, 0), (2, 1, 0)),
    ((1, 2, 1), (1, 3, 1), (1, 0, 1), (1, 1, 1), (0, 2, 2), (0, 3, 2), (0, 0, 2), (0, 1, 2)),
    ((1, 0, 2), (1, 1, 2), (0, 2, 3), (0, 3, 3), (0, 0, 3), (0, 1, 3)),
    ((1, 2, 2), (1, 3, 2)),
    ((3, 2, 0), (3, 3, 0), (3, 0, 0), (3, 1, 0), (2, 2, 1), (2, 3, 1), (2, 0, 1), (2, 1, 1), (1, 2, 3), (1, 3, 3), (1, 0, 3), (1, 1, 3)),
    (),
    ((2, 2, 2), (2, 3, 2), (2, 0, 2), (2, 1, 2)),
    ((4, 0, 0), (4, 1, 0)),
    ((2, 2, 3), (2, 3, 3), (2, 0, 3), (2, 1, 3)),
    (),
    (),
    (),
    ((3, 2, 1), (3, 3, 1), (3, 0, 1), (3, 1, 1)),
    ((4, 0, 1), (4, 1, 1)),
    ((5, 0, 0), (5, 1, 0), (3, 2, 2), (3, 3, 2), (3, 0, 2), (3, 1, 2)),
    (),
    (),
    ((4, 0, 2), (4, 1, 2), (3, 2, 3), (3, 3, 3), (3, 0, 3), (3, 1, 3)),
    ((6, 0, 0), (6, 1, 0), (5, 0, 1), (5, 1, 1)),
    (),
    ((4, 0, 3), (4, 1, 3)),
    ((5, 0, 2), (5, 1, 2)),
    ((7, 0, 0), (7, 1, 0)),
    ((6, 0, 1), (6, 1, 1), (5, 0, 3), (5, 1, 3)),
    (),
    ((6, 0, 2), (6, 1, 2), (7, 0, 1), (7, 1, 1), (6, 0, 3), (6, 1, 3), (7, 0, 2), (7, 1, 2), (7, 0, 3), (7, 1, 3)),
)
TOTAL = (13, 16, 19, 22, 25)
PART = 768
SUB = 256


def back_kernel(kernels, mem, seg_len, width, hidden, *refs):
    n_land = 3 * sum(len(cuts) for _, _, _, cuts in SUMS)
    (owners_ref, sums_in, wqkv_in, wout_in, wup_in, wdown_in, q_in, k_in, v_in, o_in, linv_in, e_in, xt_in, x1t_in, unit_in, inv_in,
     dh_in, df_in, dft_in, g_in, d_in, y_in, tail_in) = refs[:23]
    (y_out, dx_out, om_out, gm_out, vec_out, late_out, gq_out, gk_out, gv_out, out_out, up_out, down_out) = refs[23:35]
    (tot_ref, late_ref, o_ref, do_ref, dh_ref, low_ref, unit_ref, inv_ref, flip_ref, wout, payload, held, landing,
     hops, vz, hops2, vz2, acc0, acc1, acc2, acc3, oth0, oth1, oth2, oth3, away0, away1, away2, away3) = refs[35:64]
    landings = refs[64:64 + n_land]
    send, recv, here, pair_sems = refs[64 + n_land:]
    R = 2 * ROWS
    pairs = width // PAIR
    D = dh_ref.shape[1]
    grid_rows = (4, 2, 2, D // 16)
    wide_qkv = 3 * PAIR
    steps = hidden // PART
    copies = Copies(here)
    accs, others, aways = (acc0, acc1, acc2, acc3), (oth0, oth1, oth2, oth3), (away0, away1, away2, away3)
    place = Place()
    halves = (place.nt, place.t) if kernels else (0, 1)
    if kernels:
        wire = Wire(send, recv)

        def sink(c, at, first, wide):
            if c < 3:
                out = (down_out, up_out, out_out)[c]

                def put(total):
                    out[:, at + first:at + first + wide] = total

                return put
            cols = slice(at // 3, at // 3 + PAIR)

            def put_q(total):
                gq_out[:, cols] = total

            def put_kv(total):
                gk_out[:, cols] = total[:, :PAIR]
                gv_out[:, cols] = total[:, PAIR:]

            return put_kv if first else put_q

        parts, crossed = [], {}
        taken = 0
        for c, at, _, cuts in SUMS:
            parts.append([])
            for order, first, wide in cuts:
                cols = slice(at + first, at + first + wide)
                parts[-1].append(Scatter(wire, place, accs[c], sink(c, at, first, wide), cols, order, landings[taken:taken + 3]))
                taken += 3
        total = Total(wire, place, tot_ref, vec_out, hops, vz)

    def point(p):
        if not kernels:
            return
        for event in SCATTER[p]:
            run(event)
        if p in TOTAL:
            total.stage(TOTAL.index(p))

    def run(event):
        n, part, s = event
        if n in crossed:
            c, at, wide, _ = SUMS[n]
            crossed.pop(n)()
            cols = slice(at, at + wide)

            def together(z, carry):
                accs[c][z, :, :, :, cols] = accs[c][z, :, :, :, cols] + others[c][z, :, :, :, cols]
                return carry

            lax.fori_loop(0, 4, together, 0)
        parts[n][part].stage(s)

    away_open = {}

    def away_of(n):
        c, at, wide, _ = SUMS[n]
        return aways[c].at[at // wide] if c == 3 else aways[c]

    def fresh(n):
        c = SUMS[n][0]
        if kernels and c in away_open:
            wire.sent(away_open.pop(c))

    def emit(n, h, at, value):
        c, first, wide, _ = SUMS[n]
        size = value.shape[1]
        value = value.astype(LOW)
        if not kernels:
            away_of(n)[:, :, :, :, pl.ds(at, size)] = value.reshape(*grid_rows, size)
        elif h == 0:
            away_of(n)[:, :, :, :, pl.ds(at, size)] = value.reshape(*grid_rows, size)
        else:
            cols = pl.ds(first + at, size) if isinstance(at, int) else pl.ds(pl.multiple_of(first + at, PAIR), size)
            accs[c][:, :, :, :, cols] = value.reshape(*grid_rows, size)

    def emitted(n, h):
        c, at, wide, _ = SUMS[n]
        if kernels:
            if h == 0:
                land = lambda: others[c].at[:, :, :, :, pl.ds(at, wide)]
                away_open[c if c < 3 else (c, n)] = wire.count
                crossed[n] = wire.start(lambda: away_of(n), land, place.pc, land)
        elif c < 3:
            out = (down_out, up_out, out_out)[c]
            copies.start(lambda: away_of(n), lambda: out.at[h, :, :, :, :, pl.ds(at, wide)])()
        else:
            for kind, out in enumerate((gq_out, gk_out, gv_out)):
                copies.start(lambda: away_of(n).at[:, :, :, :, pl.ds(kind * PAIR, PAIR)],
                             lambda: out.at[h, :, :, :, :, pl.ds(at // 3, PAIR)])()

    tot_ref[...] = jnp.zeros_like(tot_ref)
    tot_ref[0:8, :] = sums_in[...]
    late_ref[...] = jnp.zeros_like(late_ref)
    load_flip = copies.start(lambda: dft_in, lambda: flip_ref)

    def both_of(ref, half):
        return ref.at[pl.ds(2 * half, 2)]

    def tile_cols(j):
        return pl.ds(j * PART, PART)

    def ffn(tok_ref, df_ref, x1t_ref, g_slot, d_slot, du_slot, wd_slot, wu_slot):
        def load(a, slot, h, j, weight):
            half = halves[h]
            if weight and kernels:
                return copies.start(lambda: a.at[half, :, :, :, :, tile_cols(j)], lambda: slot.at[h])
            return copies.start(lambda: a.at[half, :, tile_cols(j)], lambda: slot.at[h])

        waits = {}

        def fetch(j, kinds):
            for kind in kinds:
                a, slot, weight = {"g": (g_in, g_slot, 0), "d": (d_in, d_slot, 0), "wd": (wdown_in, wd_slot, 1), "wu": (wup_in, wu_slot, 1)}[kind]
                for h in range(2):
                    waits[kind, h, j] = load(a, slot, h, j, weight)

        fetch(0, ["g"])
        load_df = copies.start(lambda: df_in, lambda: df_ref)
        fetch(0, ["wd", "d"])
        load_x1t = copies.start(lambda: x1t_in, lambda: x1t_ref)
        fetch(0, ["wu"])
        load_dh = copies.start(lambda: dh_in, lambda: dh_ref)
        later = [copies.start(lambda a=a: a, lambda b=b: b) for a, b in ((unit_in, unit_ref), (inv_in, inv_ref), (o_in, o_ref), (wout_in, wout))]
        load_y = copies.start(lambda: y_in, lambda: tok_ref)
        y_waits = []
        if kernels:
            place.greet()
        load_flip()
        part = R // 4
        for j in range(steps):
            fresh(j)
            for h in range(2):
                waits["g", h, j]()

                def down(k, carry):
                    cols = pl.ds(pl.multiple_of(k * SUB, SUB), SUB)
                    emit(j, h, k * SUB, dot(flip_ref[...], g_slot[h, :, cols], 1, 0))
                    return carry

                lax.fori_loop(0, PART // SUB, down, 0)
                emitted(j, h)
                if j + 1 < steps:
                    waits["g", h, j + 1] = load(g_in, g_slot, h, j + 1, 0)
            point(j)
        load_df()
        load_x1t()
        load_y()
        if kernels:
            y_sent = wire.count
            y_waits.append(wire.start(lambda: tok_ref, lambda: both_of(y_out, place.t), place.pc, lambda: both_of(y_out, place.nt)))
            y_waits.append(copies.start(lambda: tok_ref, lambda: both_of(y_out, place.t)))
        else:
            y_waits.append(copies.start(lambda: tok_ref, lambda: y_out))
        for j in range(steps):
            fresh(2 + j)
            for h in range(2):
                waits["wd", h, j]()
                waits["d", h, j]()

                def up(k, carry):
                    cols = pl.ds(pl.multiple_of(k * SUB, SUB), SUB)
                    weight = wd_slot[h, ..., cols].reshape(D, SUB)
                    du = dot(df_ref[...], weight, 1, 0) * d_slot[h, :, cols].astype(F32)
                    tot_ref[pl.ds(8 + 2 * halves[h] + j, 1), cols] = jnp.sum(du, 0, keepdims=True)
                    du_slot[:, cols] = du.astype(LOW)
                    emit(2 + j, h, k * SUB, dot(x1t_ref[...], du_slot[:, cols], 1, 0))
                    return carry

                lax.fori_loop(0, PART // SUB, up, 0)
                emitted(2 + j, h)
                point(2 + 4 * j + 2 * h)
                waits["wu", h, j]()
                if j == 0 and h == 0:
                    load_dh()

                def inward(s, carry):
                    rows = pl.ds(pl.multiple_of(s * part, part), part)
                    dh_ref[rows, :] += dot(du_slot[rows, :], wu_slot[h].reshape(D, PART), 1, 1)
                    return carry

                lax.fori_loop(0, 4, inward, 0)
                if j + 1 < steps:
                    for kind, a, slot, weight in (("wd", wdown_in, wd_slot, 1), ("d", d_in, d_slot, 0), ("wu", wup_in, wu_slot, 1)):
                        waits[kind, h, j + 1] = load(a, slot, h, j + 1, weight)
                point(3 + 4 * j + 2 * h)
        for wait in later:
            wait()
        for wait in y_waits:
            wait()
        if kernels:
            wire.sent(y_sent)

    V = pltpu.VMEM
    weight_tile = (*grid_rows, PART) if kernels else (D, PART)
    pl.run_scoped(ffn, V((2, seg_len, D), LOW), V((R, D), LOW), V((D, R), LOW), V((2, R, PART), LOW), V((2, R, PART), LOW), V((R, PART), LOW),
                  V((2, *weight_tile), LOW), V((2, *weight_tile), LOW))

    vec_gain = mat(wout, 0, slice(width, width + PAIR)).astype(F32).T[2:3]
    quarter = R // 4

    def norm_step(s, carry):
        rows = pl.ds(pl.multiple_of(s * quarter, quarter), quarter)
        dx = dh_ref[rows, :]
        unit = unit_ref[rows, :].astype(F32)
        fold(tot_ref, 2, dx * unit)
        fold(tot_ref, 3, dx)
        dh = norm_back(dx * vec_gain, unit, inv_ref[rows, :])
        fold(tot_ref, 0, dh)
        dh_ref[rows, :] = dh
        low_ref[rows, :] = dh.astype(LOW)
        return carry

    lax.fori_loop(0, 4, norm_step, 0)
    point(10)
    flip_ref[...] = low_ref[...].T
    for h in range(2):
        both = jnp.concatenate([jnp.concatenate([o_ref[s, halves[h] * pairs + i] for i in range(pairs)], 1) for s in range(2)], 0)
        emit(4, h, 0, dot(flip_ref[...], both, 1, 0))
        emitted(4, h)
    load_xt = copies.start(lambda: xt_in, lambda: flip_ref)

    def out_back(s, carry):
        rows = pl.ds(pl.multiple_of(s * ROWS, ROWS), ROWS)
        for t in range(2):
            got = dot(low_ref[rows, :], mat(wout, t, slice(0, width)), 1, 0).astype(LOW)
            for i in range(pairs):
                do_ref[s, t * pairs + i] = got[:, i * PAIR:(i + 1) * PAIR]
        return carry

    def attention(tok_ref, q_s, k_s, v_s, o_s, linv_s, e_s, ds_ref, out_ref, wqkv):
        def place_of(n):
            return n // 4, (n // 2) % 2, n % 2

        def slot_copies(n):
            i, seg, half = place_of(n)
            p, slot = half * pairs + i, n % 2
            table = ((q_in, q_s), (k_in, k_s), (v_in, v_s), (o_in, o_s), (linv_in, linv_s), (e_in, e_s))
            return [pltpu.make_async_copy(a.at[seg, p], b.at[slot], pair_sems.at[slot, k]) for k, (a, b) in enumerate(table)]

        if kernels:
            device = lax.axis_index("dp")
            keep = [keep_flags(owners_ref, 2 * place.t + m, device, 4) for m in range(2)]
            payload[0] = tail_in[...]
            first = Travel(wire, place, keep, payload.at[0], held.at[0], landing.at[0], (0, 1, 2, 3)).stage
            second = Travel(wire, place, keep, payload.at[1], held.at[1], landing.at[1], (0, 1, 2, 3)).stage
        else:
            first = second = lambda s: None
        for copy in slot_copies(0):
            copy.start()
        load_w = copies.start(lambda: wqkv_in, lambda: wqkv)
        point(11)
        lax.fori_loop(0, 2, out_back, 0)
        point(12)
        load_xt()

        def gradients(i):
            cols = pl.ds(i * wide_qkv, wide_qkv)
            for h in range(2):
                emit(5 + i, h, 0, dot(flip_ref[...], out_ref[halves[h], :, cols], 1, 0))
                emitted(5 + i, h)
                late_ref[halves[h], i:i + 1, :] = jnp.sum(out_ref[halves[h], :, cols].astype(F32), 0, keepdims=True)

        def step(n, carry):
            i, seg, half = place_of(n)
            slot = n % 2

            @pl.when(n < 4 * pairs - 1)
            def _():
                for copy in slot_copies(n + 1):
                    copy.start()

            for k in range(12):
                @pl.when(n == k)
                def _():
                    if k in (4, 8):
                        gradients(k // 4 - 1)
                    point(13 + k)
                    if k in (1, 3, 5, 7, 10):
                        first((1, 3, 5, 7, 10).index(k))
            for copy in slot_copies(n):
                copy.wait()
            attend_back(q_s.at[slot], k_s.at[slot], v_s.at[slot], o_s.at[slot], linv_s.at[slot], do_ref, e_s.at[slot], ds_ref, out_ref,
                        seg, half * pairs + i, half, i)
            return carry

        lax.fori_loop(0, 4 * pairs, step, 0)
        gradients(pairs - 1)
        late = Total(wire, place, late_ref, late_out, hops2, vz2).stage if kernels else (lambda s: None)
        late(0)
        point(25)
        load_w()
        ends = [low_ref.at[pl.ds(s * ROWS + TOK, TAIL)] for s in range(2)]

        def inputs(rows):
            dx = dh_ref[rows, :]
            for t in range(2):
                dx = dx + dot(out_ref[t, rows, :], mat(wqkv, t, slice(None)), 1, 1)
            return dx.astype(LOW)

        for s in range(2):
            payload[1, s] = inputs(pl.ds(s * ROWS + TOK, TAIL))[:mem]
        second(0)
        point(26)
        half = ROWS // 2

        def in_step(s, carry):
            rows = pl.ds(pl.multiple_of(s * half, half), half)
            low_ref[rows, :] = inputs(rows)
            return carry

        lax.fori_loop(0, 2, in_step, 0)
        second(1)
        late(1)
        point(27)
        lax.fori_loop(2, 4, in_step, 0)
        second(2)
        late(2)
        for s in range(2):
            tok_ref[s] = low_ref[s * ROWS:s * ROWS + seg_len, :]
        point(28)
        if kernels:
            x_wait = wire.start(lambda: tok_ref, lambda: both_of(dx_out, place.t), place.pc, lambda: both_of(dx_out, place.nt))
            x_own = copies.start(lambda: tok_ref, lambda: both_of(dx_out, place.t))
            om_out[place.t] = held[0, 3]
            waits = [x_wait, x_own, wire.start(lambda: held.at[0, 3], lambda: om_out.at[place.t], place.pc, lambda: om_out.at[place.nt])]
            rest = SCATTER[29]
            for k in range(2):
                for event in rest[k * len(rest) // 2:(k + 1) * len(rest) // 2]:
                    run(event)
                second(3 + k)
                late(3 + k)
            gm_out[place.t] = held[1, 3]
            waits.append(wire.start(lambda: held.at[1, 3], lambda: gm_out.at[place.t], place.pc, lambda: gm_out.at[place.nt]))
            for wait in waits:
                wait()
            wire.drain()
        else:
            copies.start(lambda: tok_ref, lambda: dx_out)()
            om_out[...] = tail_in[...]
            gm_out[...] = payload[1]
            late_out[...] = late_ref[...]
            vec_out[...] = tot_ref[...]

    slot_shapes = [V((2, 2, ROWS, PAIR), LOW)] + [V((2, ROWS, PAIR), LOW)] * 3 + [V((2, ROWS, PAIR), F32)]
    full = (2, *grid_rows, 3 * width) if kernels else (2, D, 3 * width)
    pl.run_scoped(attention, V((2, seg_len, D), LOW), *slot_shapes, V((2, 2, ROWS, ROWS), LOW), V((2, ROWS, ROWS), LOW), V((2, R, 3 * width), LOW), V(full, LOW))


def back(owners, sums, tails, front_outs, width, hidden, mem, rows, kernels, cid):
    dh = front_outs[14]
    R, D = dh.shape
    pairs = width // PAIR
    S, V = jax.ShapeDtypeStruct, pltpu.VMEM
    hbm, vmem, smem = (pl.BlockSpec(memory_space=m) for m in (pl.ANY, pltpu.VMEM, pltpu.SMEM))
    widths = (hidden, hidden, width, 3 * width)
    grid = (*GRID, D // math.prod(GRID))
    if kernels:
        sums_out = [S((rows, w), F32) for w in (width, width, width, width, hidden, hidden)]
        specs = [vmem] * 6
        two, all_of = (2,), 2
        params = dict(collective_id=cid, has_side_effects=True)
        accs = [V((*grid, w), LOW) for w in widths] * 2
        landings = [s for _, _, _, cuts in SUMS for order, _, wide in cuts for s in scatter_shapes(rows, order, wide)]
    else:
        sums_out = [S((2, *grid, w), LOW) for w in (width, width, width, width, hidden, hidden)]
        specs = [hbm] * 6
        two, all_of = (), 1
        params = {}
        accs = [V((8, 128), LOW)] * 8
        landings = [V((8, 128), LOW)] * (3 * sum(len(cuts) for _, _, _, cuts in SUMS))
    aways = [V((*grid, PART), LOW), V((*grid, PART), LOW), V((*grid, width), LOW), V((pairs, *grid, 3 * PAIR), LOW)]
    seg_len = front_outs[19].shape[1]
    payload = (2, mem, D)
    late = (2, 8, 3 * PAIR)
    six = (2, 2 * pairs, ROWS, PAIR)
    count = 33 + 5 * sum(len(cuts) for _, _, _, cuts in SUMS)
    return pl.pallas_call(
        functools.partial(back_kernel, kernels, mem, seg_len, width, hidden),
        out_shape=[S((2 * all_of, seg_len, D), LOW)] * 2 + [S((*two, *payload), LOW)] * 2 + [S((16, D), F32), S(late, F32), *sums_out],
        in_specs=[smem, vmem] + [hbm] * 20 + [vmem],
        out_specs=[hbm, hbm, vmem, vmem, vmem, vmem, *specs],
        scratch_shapes=[
            V((16, D), F32), V(late, F32), V(six, LOW), V(six, LOW), V((R, D), F32), V((R, D), LOW), V((R, D), LOW), V((R, 1), F32), V((D, R), LOW),
            V(front_outs[1].shape, LOW), V((2, *payload), LOW), V((2, 4, *payload), LOW), V((2, 4, *payload), LOW),
            V((6, 16, D), F32), V((3, 16, D), F32), V((6, *late), F32), V((3, *late), F32),
            *accs, *aways, *landings,
            pltpu.SemaphoreType.DMA((count,)), pltpu.SemaphoreType.DMA((count,)), pltpu.SemaphoreType.DMA((64,)), pltpu.SemaphoreType.DMA((2, 6))],
        compiler_params=pltpu.CompilerParams(vmem_limit_bytes=63 << 20, **params),
    )(owners, sums, *front_outs, tails)


def last_kernel(*refs):
    n = len(refs) // 2
    for a, b in zip(refs[:n], refs[n:]):
        b[...] = a[...]


def last(arrays):
    vmem = pl.BlockSpec(memory_space=pltpu.VMEM)
    return pl.pallas_call(
        last_kernel, out_shape=[jax.ShapeDtypeStruct(a.shape, a.dtype) for a in arrays],
        in_specs=[vmem] * len(arrays), out_specs=[vmem] * len(arrays),
    )(*arrays)


def plain_keep(orders, device, levels):
    sources = jnp.arange(orders.shape[1], dtype=jnp.int32)
    holders = [jnp.full((orders.shape[0],), device, jnp.int32)]
    for bit in range(levels):
        stride = 2 ** (bit + 1)
        position = sources - sources % stride + orders % stride
        holders.append(jnp.sum(jnp.where(position == device, sources, 0), 1))
    return jnp.stack([a == b for a, b in zip(holders[:-1], holders[1:])], 1)


def plain_travel(keep, payload, order):
    size = lax.axis_size("dp")
    for bit in order:
        theirs = lax.ppermute(payload, "dp", [(i, i ^ 1 << bit) for i in range(size)])
        payload = jnp.where(keep[:, bit][:, None, None], payload, theirs)
    return payload


def both_cores(value):
    return lax.all_gather(value, "tensor", axis=0)


def plain_scatter(keep, outs):
    y, dx, mem_y, mem_dx, vec, late, *grads = outs
    mem_y, mem_dx = (both_cores(plain_travel(keep, m, range(keep.shape[1]))) for m in (mem_y, mem_dx))
    parts = []
    for g in grads:
        g = lax.psum_scatter(g.reshape(2, -1, g.shape[-1]).astype(F32), "tensor", scatter_dimension=0)
        parts.append(lax.psum_scatter(g, "dp", scatter_dimension=0, tiled=True))
    everywhere = ("dp", "tensor")
    return [both_cores(y), both_cores(dx), mem_y, mem_dx, lax.psum(vec, everywhere), lax.psum(late, everywhere), *parts]


def local(
    tokens, memory, lengths, owners, w_query, w_key, w_value, w_out, w_up, w_down, b_query, b_value, b_up,
    b_out, b_down, gain_attn, shift_attn, gain_ffn, shift_ffn, cot_tokens, cot_memory,
):
    micro, seg_len, depth = tokens.shape
    mem = memory.shape[1]
    size = lax.axis_size("dp")
    device, t = lax.axis_index("dp"), lax.axis_index("tensor")
    kernels = size == math.prod(GRID)
    rows, width = w_query.shape
    hidden = w_up.shape[1]
    pairs = width // PAIR
    vectors = (b_out, b_down, gain_attn, shift_attn, gain_ffn, shift_ffn)
    columns = jnp.pad(jnp.stack(vectors, 1), ((0, 0), (0, PAIR - len(vectors))))
    bias = jnp.concatenate([b_query, b_value, b_up]).astype(F32)[None]
    if kernels:
        weights = [w_query, w_key, w_value, w_out, w_up, w_down, columns]
        mem_a, mem_b = memory, cot_memory
    else:
        mine = micro // 2
        own = lambda array: lax.dynamic_slice_in_dim(array, t * mine, mine, 0)
        keep = plain_keep(own(owners), device, size.bit_length() - 1)
        mem_a, mem_b = (plain_travel(keep, own(m), range(keep.shape[1] - 1, -1, -1)) for m in (memory, cot_memory))
        by_pair = jnp.concatenate([w[:, i * PAIR:(i + 1) * PAIR] for i in range(pairs) for w in (w_query, w_key, w_value)], 1)
        shards = [by_pair, jnp.concatenate([w_out, columns], 1), w_up, w_down]
        weights = [both_cores(lax.all_gather(s, "dp", axis=0, tiled=True)) for s in shards]
        bias = both_cores(bias)
    *kept, sums, tails = front(lengths, owners, bias, mem_a, mem_b, tokens, cot_tokens, weights, width, hidden, mem, kernels, 1)
    outs = back(owners, sums, tails, kept, width, hidden, mem, rows, kernels, 2)
    if not kernels:
        outs = plain_scatter(keep, outs)
    y, dx, mem_y, mem_dx, vec, late, *grads = outs
    out_tok, grad_tok = (a.reshape(micro, seg_len, depth) for a in (y, dx))
    out_mem, grad_mem, *grads = last([mem_y.reshape(micro, mem, depth), mem_dx.reshape(micro, mem, depth), *grads])
    lines = lax.dynamic_slice(vec[:6], (0, device * rows), (6, rows))
    up_sum = lax.dynamic_slice_in_dim(vec, 8 + 2 * t, 2, 0).reshape(hidden)
    late = lax.dynamic_index_in_dim(late, t, 0, False)[:pairs].reshape(pairs, 3, PAIR)
    return (
        out_tok, out_mem, grad_tok, grad_mem, *grads,
        *(lines[i] for i in range(6)), late[:, 0].reshape(width), late[:, 2].reshape(width), up_sum,
    )


def solution(mesh):
    rows, both, split, every = P("dp", None, None), P("dp", "tensor"), P("tensor"), P("dp")
    return jax.shard_map(
        local,
        mesh=mesh,
        in_specs=(rows, rows, P(), P(), *[both] * 6, *[split] * 3, *[every] * 6, rows, rows),
        out_specs=(*[rows] * 4, *[both] * 6, *[every] * 6, *[split] * 3),
        check_vma=False,
    )
```

```python
import functools
import math

import jax
import jax.numpy as jnp
from jax import lax
from jax.experimental import pallas as pl
from jax.experimental.pallas import tpu as pltpu
from jax.sharding import PartitionSpec as P

MESH = pl.DeviceIdType.MESH
GRID = (4, 2, 2)
HEAD = 64
TOK = 512
TAIL = 32
ROWS = TOK + TAIL
PAIR = 128
masked_score = -1000000000.0
epsilon = 1e-05
F32, LOW = jnp.float32, jnp.bfloat16


def dot(a, b, left, right):
    return lax.dot_general(a, b, (((left,), (right,)), ((), ())), preferred_element_type=F32)


def mat(ref, half, cols):
    got = ref[half, ..., cols]
    return got.reshape(-1, got.shape[-1])


def live_at(position, count, mem):
    return (position < count) | ((position >= TOK) & (position < TOK + mem))


def normed(values):
    mean = jnp.mean(values, -1, keepdims=True)
    centered = values - mean
    inv = lax.rsqrt(jnp.mean(centered * centered, -1, keepdims=True) + epsilon)
    return centered * inv, inv


def norm_back(scaled, unit, inv):
    return inv * (scaled - jnp.mean(scaled, -1, keepdims=True) - unit * jnp.mean(scaled * unit, -1, keepdims=True))


def fold(total_ref, row, value):
    total_ref[row:row + 1, :] += jnp.sum(value, 0, keepdims=True)


def project(x_ref, w_ref, bias_ref, q_ref, k_ref, v_ref, seg, i, pairs):
    wide = 3 * PAIR
    cols = pl.ds(pl.multiple_of(i * wide, PAIR), wide)
    rows = x_ref[pl.ds(pl.multiple_of(seg * ROWS, 32), ROWS), :]
    lane = lax.broadcasted_iota(jnp.int32, (1, PAIR), 1)
    got = dot(rows, jnp.concatenate([mat(w_ref, 0, cols), mat(w_ref, 1, cols)], 1), 1, 0)
    for half in range(2):
        p = half * pairs + i
        at = half * wide
        here = pl.ds(pl.multiple_of(i * PAIR, PAIR), PAIR)
        there = pl.ds(pl.multiple_of((pairs + i) * PAIR, PAIR), PAIR)
        q = (got[:, at:at + PAIR] + bias_ref[half, 0:1, here]) * (1.0 / math.sqrt(HEAD))
        q_ref[seg, p, 0] = jnp.where(lane < HEAD, q, 0.0).astype(LOW)
        q_ref[seg, p, 1] = jnp.where(lane < HEAD, 0.0, q).astype(LOW)
        k_ref[seg, p] = got[:, at + PAIR:at + 2 * PAIR].astype(LOW)
        v_ref[seg, p] = (got[:, at + 2 * PAIR:at + 3 * PAIR] + bias_ref[half, 0:1, there]).astype(LOW)


def attend(q_ref, k_ref, v_ref, o_ref, linv_ref, e_slot, count, mem, seg, p):
    col = lax.broadcasted_iota(jnp.int32, (1, ROWS), 1)
    lane = lax.broadcasted_iota(jnp.int32, (1, PAIR), 1)
    masking = jnp.where(live_at(col, count, mem), 0.0, masked_score)
    keys = k_ref[seg, p]
    values = jnp.concatenate([v_ref[seg, p], jnp.ones((ROWS, PAIR), LOW)], 1)
    got = []
    for j in range(2):
        scores = dot(q_ref[seg, p, j], keys, 1, 1) + masking
        peak = jnp.max(scores, -1, keepdims=True)
        e_slot[j] = jnp.exp(scores - peak).astype(LOW)
        got.append(dot(e_slot[j], values, 1, 0))
    first = lane < HEAD
    linv = 1.0 / jnp.where(first, got[0][:, PAIR:], got[1][:, PAIR:])
    linv_ref[seg, p] = linv
    o_ref[seg, p] = (jnp.where(first, got[0][:, :PAIR], got[1][:, :PAIR]) * linv).astype(LOW)


def attend_back(q_ref, k_ref, v_ref, o_ref, linv_ref, do_ref, e_slot, ds_ref, out_ref, seg, p, half, i):
    lane = lax.broadcasted_iota(jnp.int32, (1, PAIR), 1)
    keys, values = k_ref[...], v_ref[...]
    scaled = do_ref[seg, p].astype(F32) * linv_ref[...]
    product = scaled * o_ref[...].astype(F32)
    dq, dk, dv = [], None, None
    for j in range(2):
        mine = (lane < HEAD) if j == 0 else (lane >= HEAD)
        mine_low = jnp.where(mine, scaled, 0.0).astype(LOW)
        delta = jnp.sum(jnp.where(mine, product, 0.0), -1, keepdims=True)
        gap = dot(mine_low, values, 1, 1) - delta
        ds_ref[j] = (e_slot[j].astype(F32) * gap).astype(LOW)
        dq.append(dot(ds_ref[j], keys, 1, 0))
        one_v = dot(e_slot[j], mine_low, 0, 0)
        one_k = dot(ds_ref[j], q_ref[j], 0, 0)
        dv = one_v if dv is None else dv + one_v
        dk = one_k if dk is None else dk + one_k
    rows = pl.ds(pl.multiple_of(seg * ROWS, 32), ROWS)
    dq = jnp.where(lane < HEAD, dq[0], dq[1]) * (1.0 / math.sqrt(HEAD))
    for kind, value in enumerate((dq, dk, dv)):
        out_ref[half, rows, pl.ds(pl.multiple_of((3 * i + kind) * PAIR, PAIR), PAIR)] = value.astype(LOW)


class Place:
    def __init__(self):
        me = lax.axis_index("dp")
        self.t = lax.axis_index("tensor")
        self.x = me % 2
        self.y = (me // 2) % 2
        self.z = me // 4
        self.nt, self.nx, self.ny = 1 - self.t, 1 - self.x, 1 - self.y
        self.px = self.at(self.z, self.y, self.nx)
        self.py = self.at(self.z, self.ny, self.x)
        self.zs = [(self.z + d) % 4 for d in (1, 2, 3)]
        self.zb = [(self.z + 4 - d) % 4 for d in (1, 2, 3)]
        self.pz = [self.at(z, self.y, self.x) for z in self.zs]
        self.pz1 = self.at(self.z + 1 - 2 * (self.z % 2), self.y, self.x)
        self.pz2 = self.at((self.z + 2) % 4, self.y, self.x)
        self.pc = (me, self.nt)

    def at(self, z, y, x):
        return (z * 4 + y * 2 + x, self.t)

    def greet(self):
        barrier = pltpu.get_barrier_semaphore()
        devices = [self.px, self.py, *self.pz, self.pc]
        for device in devices:
            pl.semaphore_signal(barrier, inc=1, device_id=device, device_id_type=MESH)
        pl.semaphore_wait(barrier, len(devices))


class Wire:
    def __init__(self, send, recv):
        self.send, self.recv, self.count, self.open = send, recv, 0, {}

    def start(self, src, dst, device, landing):
        k = self.count
        self.count += 1

        def copy(a, b):
            return pltpu.make_async_remote_copy(
                src_ref=a, dst_ref=b, send_sem=self.send.at[k], recv_sem=self.recv.at[k],
                device_id=device, device_id_type=MESH)

        copy(src(), dst()).start()
        self.open[k] = lambda: copy(src(), dst()).wait_send()
        return lambda: copy(landing(), landing()).wait_recv()

    def sent(self, k):
        self.open.pop(k)()

    def drain(self):
        for k in list(self.open):
            self.sent(k)


class Gather:
    def __init__(self, wire, place, out, at, width, order):
        self.wire, self.p, self.out = wire, place, out
        self.cols, self.order, self.landed, self.crossing = pl.ds(at, width), order, [], []

    def view(self, z, y, x, half=None):
        return lambda: self.out.at[self.p.t if half is None else half, z, y, x, :, self.cols]

    def stage(self, s):
        p, every = self.p, slice(None)
        for wait in self.landed:
            wait()
        self.landed = []
        home = self.view(p.z, p.y, p.x)
        if self.order == "zxy":
            if s == 0:
                for k in range(3):
                    self.go(home, None, p.pz[k], self.view(p.zb[k], p.y, p.x))
            elif s == 1:
                self.go(self.view(every, p.y, p.x), None, p.px, self.view(every, p.y, p.nx))
                self.cross(every, p.y, p.x)
            elif s == 2:
                self.go(self.view(every, p.y, every), None, p.py, self.view(every, p.ny, every))
                self.cross(every, p.y, p.nx)
            else:
                self.cross(every, p.ny, every)
        else:
            if s == 0:
                self.go(home, None, p.py, self.view(p.z, p.ny, p.x))
            elif s == 1:
                for k in range(3):
                    self.go(self.view(p.z, every, p.x), None, p.pz[k], self.view(p.zb[k], every, p.x))
                self.cross(p.z, every, p.x)
            elif s == 2:
                self.go(self.view(every, every, p.x), None, p.px, self.view(every, every, p.nx))
                for k in range(3):
                    self.cross(p.zb[k], every, p.x)
            else:
                self.cross(every, every, p.nx)

    def go(self, src, dst, device, landing):
        self.landed.append(self.wire.start(src, src if dst is None else dst, device, landing))

    def cross(self, z, y, x):
        mine = self.view(z, y, x)
        self.crossing.append(self.wire.start(mine, mine, self.p.pc, self.view(z, y, x, self.p.nt)))

    def whole(self):
        for wait in self.crossing:
            wait()
        self.crossing = []


class Travel:
    def __init__(self, wire, place, keep, payload, held, landing, order):
        self.wire, self.p, self.keep, self.landed = wire, place, keep, None
        self.held, self.landing, self.order, self.payload = held, landing, order, payload

    def stage(self, s):
        p = self.p
        if s > 0:
            self.landed()
            before = self.payload if s == 1 else self.held.at[s - 2]
            for m in range(self.payload.shape[0]):
                stay = self.keep[m][self.order[s - 1]]
                mine, theirs = before[m].astype(F32), self.landing[s - 1, m].astype(F32)
                self.held[s - 1, m] = jnp.where(stay, mine, theirs).astype(self.held.dtype)
        if s < len(self.order):
            device = [p.px, p.py, p.pz1, p.pz2][self.order[s]]
            land = lambda: self.landing.at[s]
            self.landed = self.wire.start(lambda: self.payload if s == 0 else self.held.at[s - 1], land, device, land)


def keep_flags(owners_ref, row, device, levels):
    holders = [device]
    for bit in range(levels):
        stride = 2 ** (bit + 1)
        found = device * 0
        for source in range(owners_ref.shape[1]):
            position = source - source % stride + lax.rem(owners_ref[row, source], stride)
            found = found + jnp.where(position == device, source, 0)
        holders.append(found)
    return [a == b for a, b in zip(holders[:-1], holders[1:])]


def valid_count(lengths_ref, index, seg_len):
    start, valid = index * 0, index * 0
    for j in range(lengths_ref.shape[0]):
        length = lengths_ref[j]
        count = lax.div(length + (seg_len - 1), seg_len)
        inside = (start <= index) & (index < start + count)
        valid = valid + jnp.where(inside, jnp.minimum(length - (index - start) * seg_len, seg_len), 0)
        start = start + count
    return valid


G384 = (('yzx', 0, 128), ('zxy', 128, 256))
G512 = (('yzx', 0, 128), ('zxy', 128, 384))
G768 = (('yzx', 0, 128), ('zxy', 128, 256), ('yzx', 384, 128), ('zxy', 512, 256))
CHUNKS = ((0, 0, G384), (0, 384, G384), (0, 768, G384), (1, 0, G512), (2, 0, G768), (2, 768, G768), (3, 0, G768), (3, 768, G768))
GATHER = (
    ((0, 0, 0), (0, 1, 0), (1, 0, 0), (1, 1, 0), (0, 0, 1), (0, 1, 1), (2, 0, 0), (2, 1, 0), (1, 0, 1), (1, 1, 1), (0, 0, 2), (0, 1, 2), (3, 0, 0), (3, 1, 0), (2, 0, 1), (2, 1, 1), (1, 0, 2), (1, 1, 2), (0, 0, 3), (0, 1, 3)),
    ((4, 0, 0), (4, 1, 0), (3, 0, 1), (3, 1, 1), (2, 0, 2), (2, 1, 2), (1, 0, 3), (1, 1, 3)),
    (),
    ((4, 2, 0), (4, 3, 0), (4, 0, 1), (4, 1, 1), (3, 0, 2), (3, 1, 2), (2, 0, 3), (2, 1, 3)),
    (),
    ((5, 0, 0), (5, 1, 0), (4, 2, 1), (4, 3, 1), (4, 0, 2), (4, 1, 2), (3, 0, 3), (3, 1, 3)),
    (),
    ((5, 2, 0), (5, 3, 0), (5, 0, 1), (5, 1, 1), (4, 2, 2), (4, 3, 2), (4, 0, 3), (4, 1, 3)),
    (),
    ((6, 0, 0), (6, 1, 0), (5, 2, 1), (5, 3, 1), (5, 0, 2), (5, 1, 2), (4, 2, 3), (4, 3, 3)),
    (),
    ((6, 2, 0), (6, 3, 0), (6, 0, 1), (6, 1, 1), (5, 2, 2), (5, 3, 2), (5, 0, 3), (5, 1, 3)),
    (),
    ((7, 0, 0), (7, 1, 0), (6, 2, 1), (6, 3, 1), (6, 0, 2), (6, 1, 2), (5, 2, 3), (5, 3, 3)),
    ((7, 2, 0), (7, 3, 0), (7, 0, 1), (7, 1, 1), (6, 2, 2), (6, 3, 2), (6, 0, 3), (6, 1, 3)),
    (),
    ((7, 2, 1), (7, 3, 1), (7, 0, 2), (7, 1, 2), (6, 2, 3), (6, 3, 3)),
    (),
    ((7, 2, 2), (7, 3, 2), (7, 0, 3), (7, 1, 3)),
    (),
    ((7, 2, 3), (7, 3, 3)),
    (),
    (),
    (),
    (),
    (),
    (),
    (),
    (),
)


class Copies:
    def __init__(self, sems):
        self.sems, self.count = sems, 0

    def start(self, src, dst):
        k = self.count
        self.count += 1
        pltpu.make_async_copy(src(), dst(), self.sems.at[k]).start()
        return lambda: pltpu.make_async_copy(src(), dst(), self.sems.at[k]).wait()


def front_kernel(kernels, mem, seg_len, width, *refs):
    n_in = 14 if kernels else 11
    lengths_ref, owners_ref, bias_in, mem_a, mem_b, tok_in, cot_in = refs[:7]
    weights_in = refs[7:n_in]
    (wqkv_out, wout_out, wup_out, wdown_out, q_out, k_out, v_out, o_out, linv_out, e_out, xt_out, x1t_out, unit_out, inv_out,
     dh_out, df_out, dft_out, g_out, d_out, y_out, sums_ref, tail_ref) = refs[n_in:n_in + 22]
    (wqkv, wout, wup, wdown, bias_ref, payload, held, landing, tok_ref, x_ref, cot_ref, vec_ref, o_ref, dh_ref, low_ref, unit_ref,
     inv_ref, flip_ref, send, recv, here, e_sems) = refs[-22:]
    weights = (wqkv, wout, wup, wdown)
    R = 2 * ROWS
    pairs = width // PAIR
    D = x_ref.shape[1]
    hidden = wup.shape[-1]
    copies = Copies(here)
    t = lax.axis_index("tensor")
    device = lax.axis_index("dp")
    loads = []
    for k, (a, s) in enumerate(((tok_in, 0), (tok_in, 1), (cot_in, 0), (cot_in, 1))):
        loads.append(copies.start(lambda a=a, s=s: a.at[2 * t + s], lambda k=k: tok_ref.at[k]))
    if kernels:
        place = Place()
        wire = Wire(send, recv)

        def mine(c, cols):
            return lambda: weights[c].at[place.t, place.z, place.y, place.x, :, cols]

        own = []
        for i in range(pairs):
            for kind in range(3):
                cols = pl.ds(i * PAIR, PAIR)
                own.append(copies.start(lambda kind=kind, cols=cols: weights_in[kind].at[:, cols], mine(0, pl.ds((3 * i + kind) * PAIR, PAIR))))
        own.append(copies.start(lambda: weights_in[3], mine(1, pl.ds(0, width))))
        own.append(copies.start(lambda: weights_in[6], mine(1, pl.ds(width, PAIR))))
        own.append(copies.start(lambda: weights_in[4], mine(2, pl.ds(0, hidden))))
        own.append(copies.start(lambda: weights_in[5], mine(3, pl.ds(0, hidden))))
        own_bias = copies.start(lambda: bias_in, lambda: bias_ref.at[place.t])
        for m in range(2):
            payload[0, m] = mem_a[2 * t + m]
            payload[1, m] = mem_b[2 * t + m]
        place.greet()
        keep = [keep_flags(owners_ref, 2 * t + m, device, 4) for m in range(2)]
        travel = Travel(wire, place, keep, payload.at[0], held.at[0], landing.at[0], (3, 2, 1, 0))
        second = Travel(wire, place, keep, payload.at[1], held.at[1], landing.at[1], (3, 2, 1, 0))
        parts = []
        for c, at, cuts in CHUNKS:
            parts.append([Gather(wire, place, weights[c], at + first, wide, order) for order, first, wide in cuts])

        def tick(point):
            for c, part, s in GATHER[point]:
                parts[c][part].stage(s)

        def ready(c):
            for part in parts[c]:
                part.whole()

        travel.stage(0)
        for wait in own:
            wait()
        bias_wait = wire.start(lambda: bias_in, lambda: bias_ref.at[place.t], place.pc, lambda: bias_ref.at[place.nt])
        for k, (c, part, s) in enumerate(GATHER[0]):
            parts[c][part].stage(s)
            if k in (1, 5, 11, 19):
                travel.stage((1, 5, 11, 19).index(k) + 1)
        own_bias()
        bias_wait()
        moved, moved_cot = held.at[0, 3], held.at[1, 3]
        later = second.stage
    else:
        fetched = [copies.start(lambda c=c: weights_in[c], lambda c=c: weights[c]) for c in range(4)]
        fetched.append(copies.start(lambda: bias_in, lambda: bias_ref))
        for wait in fetched:
            wait()
        moved, moved_cot = mem_a, mem_b
        tick = ready = later = lambda step: None
    counts = [valid_count(lengths_ref, device * 4 + 2 * t + s, seg_len) for s in range(2)]
    for wait in loads:
        wait()
    for s in range(2):
        for k, ref in enumerate((x_ref, cot_ref)):
            ref[s * ROWS + TOK - 16:(s + 1) * ROWS, :] = jnp.zeros((16 + TAIL, D), LOW)
            ref[s * ROWS:s * ROWS + seg_len, :] = tok_ref[2 * k + s]
        x_ref[s * ROWS + TOK:s * ROWS + TOK + mem, :] = moved[s]
    flip_ref[...] = x_ref[...].T
    saves = [copies.start(lambda: flip_ref, lambda: xt_out)]

    def attention(q_ref, k_ref, v_ref, linv_ref, slots):
        def e_copy(seg, p, slot):
            return pltpu.make_async_copy(slots.at[slot], e_out.at[seg, p], e_sems.at[slot])

        def step(n, carry):
            i, seg, half = n // 4, (n // 2) % 2, n % 2
            for k in range(12):
                @pl.when(n == k)
                def _():
                    tick(1 + k)
                    if k in (1, 3, 5, 7, 9):
                        later(k // 2)
                    if k in (4, 8):
                        ready(k // 4)

            @pl.when(half == 0)
            def _():
                project(x_ref, wqkv, bias_ref, q_ref, k_ref, v_ref, seg, i, pairs)

            count = jnp.where(seg == 0, counts[0], counts[1])

            @pl.when(n > 1)
            def _():
                e_copy(seg, half * pairs + i, half).wait()

            attend(q_ref, k_ref, v_ref, o_ref, linv_ref, slots.at[half], count, mem, seg, half * pairs + i)
            e_copy(seg, half * pairs + i, half).start()
            return carry

        ready(0)
        lax.fori_loop(0, 4 * pairs, step, 0)
        done = []
        for a, b in ((q_ref, q_out), (k_ref, k_out), (v_ref, v_out), (o_ref, o_out), (linv_ref, linv_out), (wqkv, wqkv_out)):
            done.append(copies.start(lambda a=a: a, lambda b=b: b))
        tick(13)
        ready(3)
        done.append(copies.start(lambda: wout, lambda: wout_out))
        for half in range(2):
            e_copy(0, 0, half).wait()
        for wait in done:
            wait()

    six = (2, 2 * pairs, ROWS, PAIR)
    pl.run_scoped(
        attention, pltpu.VMEM((2, 2 * pairs, 2, ROWS, PAIR), LOW), pltpu.VMEM(six, LOW), pltpu.VMEM(six, LOW),
        pltpu.VMEM(six, F32), pltpu.VMEM((2, 2, ROWS, ROWS), LOW))

    sums_ref[...] = jnp.zeros_like(sums_ref)
    vec_ref[...] = mat(wout, 0, slice(width, width + PAIR)).astype(F32).T[:8]
    vec = {n: vec_ref[k:k + 1, :] for k, n in enumerate(("b_out", "b_down", "gain_attn", "shift_attn", "gain_ffn", "shift_ffn"))}

    def out_step(s, carry):
        rows = pl.ds(pl.multiple_of(s * ROWS, ROWS), ROWS)
        h = x_ref[rows, :].astype(F32) + vec["b_out"]
        for t in range(2):
            o = jnp.concatenate([o_ref[s, t * pairs + i] for i in range(pairs)], 1)
            h = h + dot(o, mat(wout, t, slice(0, width)), 1, 1)
        unit, inv = normed(h)
        x1 = unit * vec["gain_attn"] + vec["shift_attn"]
        dh_ref[rows, :] = x1
        low_ref[rows, :] = x1.astype(LOW)
        unit_ref[rows, :] = unit.astype(LOW)
        inv_ref[rows, :] = inv
        return carry

    lax.fori_loop(0, 2, out_step, 0)
    tick(14)
    tick(15)
    for wait in saves:
        wait()
    flip_ref[...] = low_ref[...].T
    saves = [copies.start(lambda a=a: a, lambda b=b: b) for a, b in ((flip_ref, x1t_out), (unit_ref, unit_out), (inv_ref, inv_out))]

    def ffn(g_ref, d_ref):
        for s in range(2):
            cot_ref[s * ROWS + TOK:s * ROWS + TOK + mem, :] = moved_cot[s]
        tile = min(hidden // 2, 256)
        part = R // 4

        def up_cols(first, count, base):
            def up_step(k, carry):
                t = k % 2
                at = first + (k // 2) * tile
                for n in range(2 * count):
                    @pl.when(k == n)
                    def _():
                        tick(base + n)
                        if n == 0:
                            ready(4 + (base - 16) // 6)
                cols = pl.ds(pl.multiple_of(at, PAIR), tile)
                u = dot(low_ref[...], mat(wup, t, cols), 1, 0)
                u = u + bias_ref[t, 0:1, pl.ds(pl.multiple_of(2 * width + at, PAIR), tile)]
                phi = 0.5 * (1.0 + lax.erf(u * (1.0 / math.sqrt(2.0))))
                g_ref[t, :, cols] = (u * phi).astype(LOW)
                d_ref[t, :, cols] = (phi + u * (jnp.exp(-0.5 * u * u) * (1.0 / math.sqrt(2.0 * math.pi)))).astype(LOW)
                return carry

            lax.fori_loop(0, 2 * count, up_step, 0)

        up_cols(0, hidden // 2 // tile, 16)
        up_cols(hidden // 2, hidden // 2 // tile, 22)
        done = [copies.start(lambda a=a: a, lambda b=b: b) for a, b in ((wup, wup_out), (g_ref, g_out), (d_ref, d_out))]
        tick(28)
        ready(6)
        ready(7)
        done.append(copies.start(lambda: wdown, lambda: wdown_out))

        def down_step(s, carry):
            rows = pl.ds(pl.multiple_of(s * part, part), part)
            h = dh_ref[rows, :] + vec["b_down"]
            for t in range(2):
                h = h + dot(g_ref[t, rows, :], mat(wdown, t, slice(None)), 1, 1)
            unit, inv = normed(h)
            count = jnp.where(s < 2, counts[0], counts[1])
            at = lax.broadcasted_iota(jnp.int32, (part, 1), 0) + (s % 2) * part
            live = jnp.where(live_at(at, count, mem), 1.0, 0.0)
            x_ref[rows, :] = ((unit * vec["gain_ffn"] + vec["shift_ffn"]) * live).astype(LOW)
            dy = cot_ref[rows, :].astype(F32) * live
            fold(sums_ref, 4, dy * unit)
            fold(sums_ref, 5, dy)
            dh = norm_back(dy * vec["gain_ffn"], unit, inv)
            fold(sums_ref, 1, dh)
            dh_ref[rows, :] = dh
            cot_ref[rows, :] = dh.astype(LOW)
            return carry

        lax.fori_loop(0, 4, down_step, 0)
        for wait in done:
            wait()

    pl.run_scoped(ffn, pltpu.VMEM((2, R, hidden), LOW), pltpu.VMEM((2, R, hidden), LOW))
    for s in range(2):
        tok_ref[s] = x_ref[s * ROWS:s * ROWS + seg_len, :]
        tail_ref[s] = x_ref[s * ROWS + TOK:s * ROWS + TOK + mem, :]
    ends = [copies.start(lambda a=a: a, lambda b=b: b) for a, b in ((dh_ref, dh_out), (cot_ref, df_out))]
    ends.append(copies.start(lambda: tok_ref.at[pl.ds(0, 2)], lambda: y_out))
    for wait in saves:
        wait()
    flip_ref[...] = cot_ref[...].T
    ends.append(copies.start(lambda: flip_ref, lambda: dft_out))
    for wait in ends:
        wait()
    if kernels:
        wire.drain()


def front(lengths, owners, bias, mem_a, mem_b, tokens, cots, weights, width, hidden, mem, kernels, cid):
    seg_len, D = tokens.shape[1:]
    R = 2 * ROWS
    pairs = width // PAIR
    S, V = jax.ShapeDtypeStruct, pltpu.VMEM
    hbm, vmem, smem = (pl.BlockSpec(memory_space=m) for m in (pl.ANY, pltpu.VMEM, pltpu.SMEM))
    full = (2, *GRID, D // math.prod(GRID)) if kernels else (2, D)
    six = (2, 2 * pairs, ROWS, PAIR)
    payload = (2, mem, D)
    count = 9 + sum(8 if part[0] == "zxy" else 10 for _, _, cuts in CHUNKS for part in cuts)
    shapes = [(*full, w) for w in (3 * width, width + PAIR, hidden, hidden)]
    params = dict(collective_id=cid, has_side_effects=True) if kernels else {}
    return pl.pallas_call(
        functools.partial(front_kernel, kernels, mem, seg_len, width),
        out_shape=[
            *(S(s, LOW) for s in shapes), S((2, 2 * pairs, 2, ROWS, PAIR), LOW), S(six, LOW), S(six, LOW), S(six, LOW), S(six, F32),
            S((2, 2 * pairs, 2, ROWS, ROWS), LOW), S((D, R), LOW), S((D, R), LOW), S((R, D), LOW), S((R, 1), F32), S((R, D), F32),
            S((R, D), LOW), S((D, R), LOW), S((2, R, hidden), LOW), S((2, R, hidden), LOW), S((2, seg_len, D), LOW), S((8, D), F32), S(payload, LOW)],
        in_specs=[smem, smem, vmem, vmem, vmem] + [hbm] * (2 + len(weights)),
        out_specs=[hbm] * 20 + [vmem] * 2,
        scratch_shapes=[
            *(V(s, LOW) for s in shapes), V((2, 1, 2 * width + hidden), F32), V((2, *payload), LOW), V((2, 4, *payload), LOW), V((2, 4, *payload), LOW),
            V((4, seg_len, D), LOW), V((R, D), LOW), V((R, D), LOW), V((8, D), F32), V(six, LOW), V((R, D), F32), V((R, D), LOW),
            V((R, D), LOW), V((R, 1), F32), V((D, R), LOW),
            pltpu.SemaphoreType.DMA((count,)), pltpu.SemaphoreType.DMA((count,)), pltpu.SemaphoreType.DMA((40,)),
            pltpu.SemaphoreType.DMA((2,))],
        compiler_params=pltpu.CompilerParams(vmem_limit_bytes=63 << 20, **params),
    )(lengths, owners, bias, mem_a, mem_b, tokens, cots, *weights)


class Scatter:
    def __init__(self, wire, place, acc, sink, cols, order, landings):
        self.wire, self.p, self.acc, self.sink = wire, place, acc, sink
        self.cols, self.order, self.landed = cols, order, []
        self.r1, self.r2, self.r3 = landings

    def view(self, z, y, x):
        return lambda: self.acc.at[z, y, x, :, self.cols]

    def sum(self, z, y, x, terms):
        total = self.acc[z, y, x, :, self.cols].astype(F32)
        for term in terms:
            total = total + term.astype(F32)
        return total

    def add(self, z, y, x, *terms):
        if len(terms) == 1:
            self.acc[z, y, x, :, self.cols] = self.acc[z, y, x, :, self.cols] + terms[0]
            return
        self.acc[z, y, x, :, self.cols] = self.sum(z, y, x, terms).astype(self.acc.dtype)

    def finish(self, *terms):
        self.sink(self.sum(self.p.z, self.p.y, self.p.x, terms))

    def stage(self, s):
        p, every = self.p, slice(None)
        for wait in self.landed:
            wait()
        self.landed = []
        r1, r2, r3 = self.r1, self.r2, self.r3
        if self.order == "yxz":
            if s == 0:
                self.go(self.view(every, p.ny, every), lambda: r1, p.py)
            elif s == 1:
                for z in range(4):
                    for x in range(2):
                        self.add(z, p.y, x, r1[z, x])
                self.go(self.view(every, p.y, p.nx), lambda: r2, p.px)
            elif s == 2:
                for z in range(4):
                    self.add(z, p.y, p.x, r2[z])
                for k in range(3):
                    self.go(self.view(p.zs[k], p.y, p.x), lambda k=k: r3.at[k], p.pz[k])
            else:
                self.finish(r3[0], r3[1], r3[2])
        else:
            if s == 0:
                self.go(self.view(every, every, p.nx), lambda: r1, p.px)
            elif s == 1:
                for z in range(4):
                    for y in range(2):
                        self.add(z, y, p.x, r1[z, y])
                for k in range(3):
                    self.go(self.view(p.zs[k], every, p.x), lambda k=k: r2.at[k], p.pz[k])
            elif s == 2:
                for y in range(2):
                    self.add(p.z, y, p.x, r2[0, y], r2[1, y], r2[2, y])
                self.go(self.view(p.z, p.ny, p.x), lambda: r3, p.py)
            else:
                self.finish(r3[...])

    def go(self, src, landing, device):
        self.landed.append(self.wire.start(src, landing, device, landing))


def scatter_shapes(rows, order, wide):
    V = pltpu.VMEM
    if order == "xzy":
        return [V((4, 2, rows, wide), LOW), V((3, 2, rows, wide), LOW), V((rows, wide), LOW)]
    return [V((4, 2, rows, wide), LOW), V((4, rows, wide), LOW), V((3, rows, wide), LOW)]


class Total:
    def __init__(self, wire, place, vec, out, hops, vz):
        self.wire, self.p, self.landed = wire, place, []
        self.vec, self.out, self.hops, self.vz = vec, out, hops, vz

    def stage(self, s):
        p, hops = self.p, self.hops
        for wait in self.landed:
            wait()
        self.landed = []
        if s == 0:
            self.go(lambda: self.vec, lambda: hops.at[0], p.pc)
        elif s < 4:
            hops[2 * s - 1] = (self.vec[...] if s == 1 else hops[2 * s - 3]) + hops[2 * s - 2]
            if s < 3:
                self.go(lambda: hops.at[2 * s - 1], lambda: hops.at[2 * s], (p.px, p.py)[s - 1])
            else:
                for k in range(3):
                    self.go(lambda: hops.at[5], lambda k=k: self.vz.at[k], p.pz[k])
        else:
            self.out[...] = hops[5] + self.vz[0] + self.vz[1] + self.vz[2]

    def go(self, src, landing, device):
        self.landed.append(self.wire.start(src, landing, device, landing))


S384 = (('xzy', 0, 128), ('yxz', 128, 256))
S768 = (('xzy', 0, 128), ('yxz', 128, 256), ('xzy', 384, 128), ('yxz', 512, 256))
SUMS = ((0, 0, 768, S768), (0, 768, 768, S768), (1, 0, 768, S768), (1, 768, 768, S768), (2, 0, 384, S384), (3, 0, 384, S384), (3, 384, 384, S384), (3, 768, 384, S384))
SCATTER = (
    ((0, 2, 0), (0, 3, 0), (0, 0, 0), (0, 1, 0)),
    ((1, 2, 0), (1, 3, 0), (1, 0, 0), (1, 1, 0)),
    (),
    ((0, 2, 1), (0, 3, 1), (0, 0, 1), (0, 1, 1)),
    ((2, 2, 0), (2, 3, 0), (2, 0, 0), (2, 1, 0)),
    ((1, 2, 1), (1, 3, 1), (1, 0, 1), (1, 1, 1), (0, 2, 2), (0, 3, 2), (0, 0, 2), (0, 1, 2)),
    ((1, 0, 2), (1, 1, 2), (0, 2, 3), (0, 3, 3), (0, 0, 3), (0, 1, 3)),
    ((1, 2, 2), (1, 3, 2)),
    ((3, 2, 0), (3, 3, 0), (3, 0, 0), (3, 1, 0), (2, 2, 1), (2, 3, 1), (2, 0, 1), (2, 1, 1), (1, 2, 3), (1, 3, 3), (1, 0, 3), (1, 1, 3)),
    (),
    ((2, 2, 2), (2, 3, 2), (2, 0, 2), (2, 1, 2)),
    ((4, 0, 0), (4, 1, 0)),
    ((2, 2, 3), (2, 3, 3), (2, 0, 3), (2, 1, 3)),
    (),
    (),
    (),
    ((3, 2, 1), (3, 3, 1), (3, 0, 1), (3, 1, 1)),
    ((4, 0, 1), (4, 1, 1)),
    ((5, 0, 0), (5, 1, 0), (3, 2, 2), (3, 3, 2), (3, 0, 2), (3, 1, 2)),
    (),
    (),
    ((4, 0, 2), (4, 1, 2), (3, 2, 3), (3, 3, 3), (3, 0, 3), (3, 1, 3)),
    ((6, 0, 0), (6, 1, 0), (5, 0, 1), (5, 1, 1)),
    (),
    ((4, 0, 3), (4, 1, 3)),
    ((5, 0, 2), (5, 1, 2)),
    ((7, 0, 0), (7, 1, 0)),
    ((6, 0, 1), (6, 1, 1), (5, 0, 3), (5, 1, 3)),
    (),
    ((6, 0, 2), (6, 1, 2), (7, 0, 1), (7, 1, 1), (6, 0, 3), (6, 1, 3), (7, 0, 2), (7, 1, 2), (7, 0, 3), (7, 1, 3)),
)
TOTAL = (13, 16, 19, 22, 25)
PART = 768
SUB = 768


def back_kernel(kernels, mem, seg_len, width, hidden, *refs):
    n_land = 3 * sum(len(cuts) for _, _, _, cuts in SUMS)
    (owners_ref, sums_in, wqkv_in, wout_in, wup_in, wdown_in, q_in, k_in, v_in, o_in, linv_in, e_in, xt_in, x1t_in, unit_in, inv_in,
     dh_in, df_in, dft_in, g_in, d_in, y_in, tail_in) = refs[:23]
    (y_out, dx_out, om_out, gm_out, vec_out, late_out, gq_out, gk_out, gv_out, out_out, up_out, down_out) = refs[23:35]
    (tot_ref, late_ref, o_ref, do_ref, dh_ref, low_ref, unit_ref, inv_ref, flip_ref, wout, payload, held, landing,
     hops, vz, hops2, vz2, acc0, acc1, acc2, acc3, oth0, oth1, oth2, oth3, away0, away1, away2, away3) = refs[35:64]
    landings = refs[64:64 + n_land]
    send, recv, here, pair_sems = refs[64 + n_land:]
    R = 2 * ROWS
    pairs = width // PAIR
    D = dh_ref.shape[1]
    grid_rows = (4, 2, 2, D // 16)
    wide_qkv = 3 * PAIR
    steps = hidden // PART
    copies = Copies(here)
    accs, others, aways = (acc0, acc1, acc2, acc3), (oth0, oth1, oth2, oth3), (away0, away1, away2, away3)
    place = Place()
    halves = (place.nt, place.t) if kernels else (0, 1)
    if kernels:
        wire = Wire(send, recv)

        def sink(c, at, first, wide):
            if c < 3:
                out = (down_out, up_out, out_out)[c]

                def put(total):
                    out[:, at + first:at + first + wide] = total

                return put
            cols = slice(at // 3, at // 3 + PAIR)

            def put_q(total):
                gq_out[:, cols] = total

            def put_kv(total):
                gk_out[:, cols] = total[:, :PAIR]
                gv_out[:, cols] = total[:, PAIR:]

            return put_kv if first else put_q

        parts, crossed = [], {}
        taken = 0
        for c, at, _, cuts in SUMS:
            parts.append([])
            for order, first, wide in cuts:
                cols = slice(at + first, at + first + wide)
                parts[-1].append(Scatter(wire, place, accs[c], sink(c, at, first, wide), cols, order, landings[taken:taken + 3]))
                taken += 3
        total = Total(wire, place, tot_ref, vec_out, hops, vz)

    def point(p):
        if not kernels:
            return
        for event in SCATTER[p]:
            run(event)
        if p in TOTAL:
            total.stage(TOTAL.index(p))

    def run(event):
        n, part, s = event
        if n in crossed:
            c, at, wide, _ = SUMS[n]
            crossed.pop(n)()
            cols = slice(at, at + wide)

            def together(z, carry):
                accs[c][z, :, :, :, cols] = accs[c][z, :, :, :, cols] + others[c][z, :, :, :, cols]
                return carry

            lax.fori_loop(0, 4, together, 0)
        parts[n][part].stage(s)

    away_open = {}

    def away_of(n):
        c, at, wide, _ = SUMS[n]
        return aways[c].at[at // wide] if c == 3 else aways[c]

    def fresh(n):
        c = SUMS[n][0]
        if kernels and c in away_open:
            wire.sent(away_open.pop(c))

    def emit(n, h, at, value):
        c, first, wide, _ = SUMS[n]
        size = value.shape[1]
        value = value.astype(LOW)
        if not kernels:
            away_of(n)[:, :, :, :, pl.ds(at, size)] = value.reshape(*grid_rows, size)
        elif h == 0:
            away_of(n)[:, :, :, :, pl.ds(at, size)] = value.reshape(*grid_rows, size)
        else:
            cols = pl.ds(first + at, size) if isinstance(at, int) else pl.ds(pl.multiple_of(first + at, PAIR), size)
            accs[c][:, :, :, :, cols] = value.reshape(*grid_rows, size)

    def emitted(n, h):
        c, at, wide, _ = SUMS[n]
        if kernels:
            if h == 0:
                land = lambda: others[c].at[:, :, :, :, pl.ds(at, wide)]
                away_open[c if c < 3 else (c, n)] = wire.count
                crossed[n] = wire.start(lambda: away_of(n), land, place.pc, land)
        elif c < 3:
            out = (down_out, up_out, out_out)[c]
            copies.start(lambda: away_of(n), lambda: out.at[h, :, :, :, :, pl.ds(at, wide)])()
        else:
            for kind, out in enumerate((gq_out, gk_out, gv_out)):
                copies.start(lambda: away_of(n).at[:, :, :, :, pl.ds(kind * PAIR, PAIR)],
                             lambda: out.at[h, :, :, :, :, pl.ds(at // 3, PAIR)])()

    tot_ref[...] = jnp.zeros_like(tot_ref)
    tot_ref[0:8, :] = sums_in[...]
    late_ref[...] = jnp.zeros_like(late_ref)
    load_flip = copies.start(lambda: dft_in, lambda: flip_ref)

    def both_of(ref, half):
        return ref.at[pl.ds(2 * half, 2)]

    def tile_cols(j):
        return pl.ds(j * PART, PART)

    def ffn(tok_ref, df_ref, x1t_ref, g_slot, d_slot, du_slot, wd_slot, wu_slot):
        def load(a, slot, h, j, weight):
            half = halves[h]
            if weight and kernels:
                return copies.start(lambda: a.at[half, :, :, :, :, tile_cols(j)], lambda: slot.at[h])
            return copies.start(lambda: a.at[half, :, tile_cols(j)], lambda: slot.at[h])

        waits = {}

        def fetch(j, kinds):
            for kind in kinds:
                a, slot, weight = {"g": (g_in, g_slot, 0), "d": (d_in, d_slot, 0), "wd": (wdown_in, wd_slot, 1), "wu": (wup_in, wu_slot, 1)}[kind]
                for h in range(2):
                    waits[kind, h, j] = load(a, slot, h, j, weight)

        fetch(0, ["g"])
        load_df = copies.start(lambda: df_in, lambda: df_ref)
        fetch(0, ["wd", "d"])
        load_x1t = copies.start(lambda: x1t_in, lambda: x1t_ref)
        fetch(0, ["wu"])
        load_dh = copies.start(lambda: dh_in, lambda: dh_ref)
        later = [copies.start(lambda a=a: a, lambda b=b: b) for a, b in ((unit_in, unit_ref), (inv_in, inv_ref), (o_in, o_ref), (wout_in, wout))]
        load_y = copies.start(lambda: y_in, lambda: tok_ref)
        y_waits = []
        if kernels:
            place.greet()
        load_flip()
        part = R // 4
        for j in range(steps):
            fresh(j)
            for h in range(2):
                waits["g", h, j]()

                def down(k, carry):
                    cols = pl.ds(pl.multiple_of(k * SUB, SUB), SUB)
                    emit(j, h, k * SUB, dot(flip_ref[...], g_slot[h, :, cols], 1, 0))
                    return carry

                lax.fori_loop(0, PART // SUB, down, 0)
                emitted(j, h)
                if j + 1 < steps:
                    waits["g", h, j + 1] = load(g_in, g_slot, h, j + 1, 0)
            point(j)
        load_df()
        load_x1t()
        load_y()
        if kernels:
            y_sent = wire.count
            y_waits.append(wire.start(lambda: tok_ref, lambda: both_of(y_out, place.t), place.pc, lambda: both_of(y_out, place.nt)))
            y_waits.append(copies.start(lambda: tok_ref, lambda: both_of(y_out, place.t)))
        else:
            y_waits.append(copies.start(lambda: tok_ref, lambda: y_out))
        for j in range(steps):
            fresh(2 + j)
            for h in range(2):
                waits["wd", h, j]()
                waits["d", h, j]()

                def up(k, carry):
                    cols = pl.ds(pl.multiple_of(k * SUB, SUB), SUB)
                    weight = wd_slot[h, ..., cols].reshape(D, SUB)
                    du = dot(df_ref[...], weight, 1, 0) * d_slot[h, :, cols].astype(F32)
                    tot_ref[pl.ds(8 + 2 * halves[h] + j, 1), cols] = jnp.sum(du, 0, keepdims=True)
                    du_slot[:, cols] = du.astype(LOW)
                    emit(2 + j, h, k * SUB, dot(x1t_ref[...], du_slot[:, cols], 1, 0))
                    return carry

                lax.fori_loop(0, PART // SUB, up, 0)
                emitted(2 + j, h)
                point(2 + 4 * j + 2 * h)
                waits["wu", h, j]()
                if j == 0 and h == 0:
                    load_dh()

                def inward(s, carry):
                    rows = pl.ds(pl.multiple_of(s * part, part), part)
                    dh_ref[rows, :] += dot(du_slot[rows, :], wu_slot[h].reshape(D, PART), 1, 1)
                    return carry

                lax.fori_loop(0, 4, inward, 0)
                if j + 1 < steps:
                    for kind, a, slot, weight in (("wd", wdown_in, wd_slot, 1), ("d", d_in, d_slot, 0), ("wu", wup_in, wu_slot, 1)):
                        waits[kind, h, j + 1] = load(a, slot, h, j + 1, weight)
                point(3 + 4 * j + 2 * h)
        for wait in later:
            wait()
        for wait in y_waits:
            wait()
        if kernels:
            wire.sent(y_sent)

    V = pltpu.VMEM
    weight_tile = (*grid_rows, PART) if kernels else (D, PART)
    pl.run_scoped(ffn, V((2, seg_len, D), LOW), V((R, D), LOW), V((D, R), LOW), V((2, R, PART), LOW), V((2, R, PART), LOW), V((R, PART), LOW),
                  V((2, *weight_tile), LOW), V((2, *weight_tile), LOW))

    vec_gain = mat(wout, 0, slice(width, width + PAIR)).astype(F32).T[2:3]
    quarter = R // 4

    def norm_step(s, carry):
        rows = pl.ds(pl.multiple_of(s * quarter, quarter), quarter)
        dx = dh_ref[rows, :]
        unit = unit_ref[rows, :].astype(F32)
        fold(tot_ref, 2, dx * unit)
        fold(tot_ref, 3, dx)
        dh = norm_back(dx * vec_gain, unit, inv_ref[rows, :])
        fold(tot_ref, 0, dh)
        dh_ref[rows, :] = dh
        low_ref[rows, :] = dh.astype(LOW)
        return carry

    lax.fori_loop(0, 4, norm_step, 0)
    point(10)
    flip_ref[...] = low_ref[...].T
    for h in range(2):
        both = jnp.concatenate([jnp.concatenate([o_ref[s, halves[h] * pairs + i] for i in range(pairs)], 1) for s in range(2)], 0)
        emit(4, h, 0, dot(flip_ref[...], both, 1, 0))
        emitted(4, h)
    load_xt = copies.start(lambda: xt_in, lambda: flip_ref)

    def out_back(s, carry):
        rows = pl.ds(pl.multiple_of(s * ROWS, ROWS), ROWS)
        for t in range(2):
            got = dot(low_ref[rows, :], mat(wout, t, slice(0, width)), 1, 0).astype(LOW)
            for i in range(pairs):
                do_ref[s, t * pairs + i] = got[:, i * PAIR:(i + 1) * PAIR]
        return carry

    def attention(tok_ref, q_s, k_s, v_s, o_s, linv_s, e_s, ds_ref, out_ref, wqkv):
        def place_of(n):
            return n // 4, (n // 2) % 2, n % 2

        def slot_copies(n):
            i, seg, half = place_of(n)
            p, slot = half * pairs + i, n % 2
            table = ((q_in, q_s), (k_in, k_s), (v_in, v_s), (o_in, o_s), (linv_in, linv_s), (e_in, e_s))
            return [pltpu.make_async_copy(a.at[seg, p], b.at[slot], pair_sems.at[slot, k]) for k, (a, b) in enumerate(table)]

        if kernels:
            device = lax.axis_index("dp")
            keep = [keep_flags(owners_ref, 2 * place.t + m, device, 4) for m in range(2)]
            payload[0] = tail_in[...]
            first = Travel(wire, place, keep, payload.at[0], held.at[0], landing.at[0], (0, 1, 2, 3)).stage
            second = Travel(wire, place, keep, payload.at[1], held.at[1], landing.at[1], (0, 1, 2, 3)).stage
        else:
            first = second = lambda s: None
        for copy in slot_copies(0):
            copy.start()
        load_w = copies.start(lambda: wqkv_in, lambda: wqkv)
        point(11)
        lax.fori_loop(0, 2, out_back, 0)
        point(12)
        load_xt()

        def gradients(i):
            cols = pl.ds(i * wide_qkv, wide_qkv)
            for h in range(2):
                emit(5 + i, h, 0, dot(flip_ref[...], out_ref[halves[h], :, cols], 1, 0))
                emitted(5 + i, h)
                late_ref[halves[h], i:i + 1, :] = jnp.sum(out_ref[halves[h], :, cols].astype(F32), 0, keepdims=True)

        def step(n, carry):
            i, seg, half = place_of(n)
            slot = n % 2

            @pl.when(n < 4 * pairs - 1)
            def _():
                for copy in slot_copies(n + 1):
                    copy.start()

            for k in range(12):
                @pl.when(n == k)
                def _():
                    if k in (4, 8):
                        gradients(k // 4 - 1)
                    point(13 + k)
                    if k in (1, 3, 5, 7, 10):
                        first((1, 3, 5, 7, 10).index(k))
            for copy in slot_copies(n):
                copy.wait()
            attend_back(q_s.at[slot], k_s.at[slot], v_s.at[slot], o_s.at[slot], linv_s.at[slot], do_ref, e_s.at[slot], ds_ref, out_ref,
                        seg, half * pairs + i, half, i)
            return carry

        lax.fori_loop(0, 4 * pairs, step, 0)
        gradients(pairs - 1)
        late = Total(wire, place, late_ref, late_out, hops2, vz2).stage if kernels else (lambda s: None)
        late(0)
        point(25)
        load_w()
        ends = [low_ref.at[pl.ds(s * ROWS + TOK, TAIL)] for s in range(2)]

        def inputs(rows):
            dx = dh_ref[rows, :]
            for t in range(2):
                dx = dx + dot(out_ref[t, rows, :], mat(wqkv, t, slice(None)), 1, 1)
            return dx.astype(LOW)

        for s in range(2):
            payload[1, s] = inputs(pl.ds(s * ROWS + TOK, TAIL))[:mem]
        second(0)
        point(26)
        half = ROWS // 2

        def in_step(s, carry):
            rows = pl.ds(pl.multiple_of(s * half, half), half)
            low_ref[rows, :] = inputs(rows)
            return carry

        lax.fori_loop(0, 2, in_step, 0)
        second(1)
        late(1)
        point(27)
        lax.fori_loop(2, 4, in_step, 0)
        second(2)
        late(2)
        for s in range(2):
            tok_ref[s] = low_ref[s * ROWS:s * ROWS + seg_len, :]
        point(28)
        if kernels:
            x_wait = wire.start(lambda: tok_ref, lambda: both_of(dx_out, place.t), place.pc, lambda: both_of(dx_out, place.nt))
            x_own = copies.start(lambda: tok_ref, lambda: both_of(dx_out, place.t))
            om_out[place.t] = held[0, 3]
            waits = [x_wait, x_own, wire.start(lambda: held.at[0, 3], lambda: om_out.at[place.t], place.pc, lambda: om_out.at[place.nt])]
            rest = SCATTER[29]
            for k in range(2):
                for event in rest[k * len(rest) // 2:(k + 1) * len(rest) // 2]:
                    run(event)
                second(3 + k)
                late(3 + k)
            gm_out[place.t] = held[1, 3]
            waits.append(wire.start(lambda: held.at[1, 3], lambda: gm_out.at[place.t], place.pc, lambda: gm_out.at[place.nt]))
            for wait in waits:
                wait()
            wire.drain()
        else:
            copies.start(lambda: tok_ref, lambda: dx_out)()
            om_out[...] = tail_in[...]
            gm_out[...] = payload[1]
            late_out[...] = late_ref[...]
            vec_out[...] = tot_ref[...]

    slot_shapes = [V((2, 2, ROWS, PAIR), LOW)] + [V((2, ROWS, PAIR), LOW)] * 3 + [V((2, ROWS, PAIR), F32)]
    full = (2, *grid_rows, 3 * width) if kernels else (2, D, 3 * width)
    pl.run_scoped(attention, V((2, seg_len, D), LOW), *slot_shapes, V((2, 2, ROWS, ROWS), LOW), V((2, ROWS, ROWS), LOW), V((2, R, 3 * width), LOW), V(full, LOW))


def back(owners, sums, tails, front_outs, width, hidden, mem, rows, kernels, cid):
    dh = front_outs[14]
    R, D = dh.shape
    pairs = width // PAIR
    S, V = jax.ShapeDtypeStruct, pltpu.VMEM
    hbm, vmem, smem = (pl.BlockSpec(memory_space=m) for m in (pl.ANY, pltpu.VMEM, pltpu.SMEM))
    widths = (hidden, hidden, width, 3 * width)
    grid = (*GRID, D // math.prod(GRID))
    if kernels:
        sums_out = [S((rows, w), F32) for w in (width, width, width, width, hidden, hidden)]
        specs = [vmem] * 6
        two, all_of = (2,), 2
        params = dict(collective_id=cid, has_side_effects=True)
        accs = [V((*grid, w), LOW) for w in widths] * 2
        landings = [s for _, _, _, cuts in SUMS for order, _, wide in cuts for s in scatter_shapes(rows, order, wide)]
    else:
        sums_out = [S((2, *grid, w), LOW) for w in (width, width, width, width, hidden, hidden)]
        specs = [hbm] * 6
        two, all_of = (), 1
        params = {}
        accs = [V((8, 128), LOW)] * 8
        landings = [V((8, 128), LOW)] * (3 * sum(len(cuts) for _, _, _, cuts in SUMS))
    aways = [V((*grid, PART), LOW), V((*grid, PART), LOW), V((*grid, width), LOW), V((pairs, *grid, 3 * PAIR), LOW)]
    seg_len = front_outs[19].shape[1]
    payload = (2, mem, D)
    late = (2, 8, 3 * PAIR)
    six = (2, 2 * pairs, ROWS, PAIR)
    count = 33 + 5 * sum(len(cuts) for _, _, _, cuts in SUMS)
    return pl.pallas_call(
        functools.partial(back_kernel, kernels, mem, seg_len, width, hidden),
        out_shape=[S((2 * all_of, seg_len, D), LOW)] * 2 + [S((*two, *payload), LOW)] * 2 + [S((16, D), F32), S(late, F32), *sums_out],
        in_specs=[smem, vmem] + [hbm] * 20 + [vmem],
        out_specs=[hbm, hbm, vmem, vmem, vmem, vmem, *specs],
        scratch_shapes=[
            V((16, D), F32), V(late, F32), V(six, LOW), V(six, LOW), V((R, D), F32), V((R, D), LOW), V((R, D), LOW), V((R, 1), F32), V((D, R), LOW),
            V(front_outs[1].shape, LOW), V((2, *payload), LOW), V((2, 4, *payload), LOW), V((2, 4, *payload), LOW),
            V((6, 16, D), F32), V((3, 16, D), F32), V((6, *late), F32), V((3, *late), F32),
            *accs, *aways, *landings,
            pltpu.SemaphoreType.DMA((count,)), pltpu.SemaphoreType.DMA((count,)), pltpu.SemaphoreType.DMA((64,)), pltpu.SemaphoreType.DMA((2, 6))],
        compiler_params=pltpu.CompilerParams(vmem_limit_bytes=63 << 20, **params),
    )(owners, sums, *front_outs, tails)


def last_kernel(*refs):
    n = len(refs) // 2
    for a, b in zip(refs[:n], refs[n:]):
        b[...] = a[...]


def last(arrays):
    vmem = pl.BlockSpec(memory_space=pltpu.VMEM)
    return pl.pallas_call(
        last_kernel, out_shape=[jax.ShapeDtypeStruct(a.shape, a.dtype) for a in arrays],
        in_specs=[vmem] * len(arrays), out_specs=[vmem] * len(arrays),
    )(*arrays)


def plain_keep(orders, device, levels):
    sources = jnp.arange(orders.shape[1], dtype=jnp.int32)
    holders = [jnp.full((orders.shape[0],), device, jnp.int32)]
    for bit in range(levels):
        stride = 2 ** (bit + 1)
        position = sources - sources % stride + orders % stride
        holders.append(jnp.sum(jnp.where(position == device, sources, 0), 1))
    return jnp.stack([a == b for a, b in zip(holders[:-1], holders[1:])], 1)


def plain_travel(keep, payload, order):
    size = lax.axis_size("dp")
    for bit in order:
        theirs = lax.ppermute(payload, "dp", [(i, i ^ 1 << bit) for i in range(size)])
        payload = jnp.where(keep[:, bit][:, None, None], payload, theirs)
    return payload


def both_cores(value):
    return lax.all_gather(value, "tensor", axis=0)


def plain_scatter(keep, outs):
    y, dx, mem_y, mem_dx, vec, late, *grads = outs
    mem_y, mem_dx = (both_cores(plain_travel(keep, m, range(keep.shape[1]))) for m in (mem_y, mem_dx))
    parts = []
    for g in grads:
        g = lax.psum_scatter(g.reshape(2, -1, g.shape[-1]).astype(F32), "tensor", scatter_dimension=0)
        parts.append(lax.psum_scatter(g, "dp", scatter_dimension=0, tiled=True))
    everywhere = ("dp", "tensor")
    return [both_cores(y), both_cores(dx), mem_y, mem_dx, lax.psum(vec, everywhere), lax.psum(late, everywhere), *parts]


def local(
    tokens, memory, lengths, owners, w_query, w_key, w_value, w_out, w_up, w_down, b_query, b_value, b_up,
    b_out, b_down, gain_attn, shift_attn, gain_ffn, shift_ffn, cot_tokens, cot_memory,
):
    micro, seg_len, depth = tokens.shape
    mem = memory.shape[1]
    size = lax.axis_size("dp")
    device, t = lax.axis_index("dp"), lax.axis_index("tensor")
    kernels = size == math.prod(GRID)
    rows, width = w_query.shape
    hidden = w_up.shape[1]
    pairs = width // PAIR
    vectors = (b_out, b_down, gain_attn, shift_attn, gain_ffn, shift_ffn)
    columns = jnp.pad(jnp.stack(vectors, 1), ((0, 0), (0, PAIR - len(vectors))))
    bias = jnp.concatenate([b_query, b_value, b_up]).astype(F32)[None]
    if kernels:
        weights = [w_query, w_key, w_value, w_out, w_up, w_down, columns]
        mem_a, mem_b = memory, cot_memory
    else:
        mine = micro // 2
        own = lambda array: lax.dynamic_slice_in_dim(array, t * mine, mine, 0)
        keep = plain_keep(own(owners), device, size.bit_length() - 1)
        mem_a, mem_b = (plain_travel(keep, own(m), range(keep.shape[1] - 1, -1, -1)) for m in (memory, cot_memory))
        by_pair = jnp.concatenate([w[:, i * PAIR:(i + 1) * PAIR] for i in range(pairs) for w in (w_query, w_key, w_value)], 1)
        shards = [by_pair, jnp.concatenate([w_out, columns], 1), w_up, w_down]
        weights = [both_cores(lax.all_gather(s, "dp", axis=0, tiled=True)) for s in shards]
        bias = both_cores(bias)
    *kept, sums, tails = front(lengths, owners, bias, mem_a, mem_b, tokens, cot_tokens, weights, width, hidden, mem, kernels, 1)
    outs = back(owners, sums, tails, kept, width, hidden, mem, rows, kernels, 2)
    if not kernels:
        outs = plain_scatter(keep, outs)
    y, dx, mem_y, mem_dx, vec, late, *grads = outs
    out_tok, grad_tok = (a.reshape(micro, seg_len, depth) for a in (y, dx))
    out_mem, grad_mem, *grads = last([mem_y.reshape(micro, mem, depth), mem_dx.reshape(micro, mem, depth), *grads])
    lines = lax.dynamic_slice(vec[:6], (0, device * rows), (6, rows))
    up_sum = lax.dynamic_slice_in_dim(vec, 8 + 2 * t, 2, 0).reshape(hidden)
    late = lax.dynamic_index_in_dim(late, t, 0, False)[:pairs].reshape(pairs, 3, PAIR)
    return (
        out_tok, out_mem, grad_tok, grad_mem, *grads,
        *(lines[i] for i in range(6)), late[:, 0].reshape(width), late[:, 2].reshape(width), up_sum,
    )


def solution(mesh):
    rows, both, split, every = P("dp", None, None), P("dp", "tensor"), P("tensor"), P("dp")
    return jax.shard_map(
        local,
        mesh=mesh,
        in_specs=(rows, rows, P(), P(), *[both] * 6, *[split] * 3, *[every] * 6, rows, rows),
        out_specs=(*[rows] * 4, *[both] * 6, *[every] * 6, *[split] * 3),
        check_vma=False,
    )
```

```python
import functools
import math

import jax
import jax.numpy as jnp
from jax import lax
from jax.experimental import pallas as pl
from jax.experimental.pallas import tpu as pltpu
from jax.sharding import PartitionSpec as P

MESH = pl.DeviceIdType.MESH
GRID = (4, 2, 2)
HEAD = 64
TOK = 512
TAIL = 32
ROWS = TOK + TAIL
PAIR = 128
masked_score = -1000000000.0
epsilon = 1e-05
F32, LOW = jnp.float32, jnp.bfloat16


def dot(a, b, left, right):
    return lax.dot_general(a, b, (((left,), (right,)), ((), ())), preferred_element_type=F32)


def mat(ref, half, cols):
    got = ref[half, ..., cols]
    return got.reshape(-1, got.shape[-1])


def live_at(position, count, mem):
    return (position < count) | ((position >= TOK) & (position < TOK + mem))


def normed(values):
    mean = jnp.mean(values, -1, keepdims=True)
    centered = values - mean
    inv = lax.rsqrt(jnp.mean(centered * centered, -1, keepdims=True) + epsilon)
    return centered * inv, inv


def norm_back(scaled, unit, inv):
    return inv * (scaled - jnp.mean(scaled, -1, keepdims=True) - unit * jnp.mean(scaled * unit, -1, keepdims=True))


def fold(total_ref, row, value):
    total_ref[row:row + 1, :] += jnp.sum(value, 0, keepdims=True)


def project(x_ref, w_ref, bias_ref, q_ref, k_ref, v_ref, seg, i, pairs):
    wide = 3 * PAIR
    cols = pl.ds(pl.multiple_of(i * wide, PAIR), wide)
    rows = x_ref[pl.ds(pl.multiple_of(seg * ROWS, 32), ROWS), :]
    lane = lax.broadcasted_iota(jnp.int32, (1, PAIR), 1)
    got = dot(rows, jnp.concatenate([mat(w_ref, 0, cols), mat(w_ref, 1, cols)], 1), 1, 0)
    for half in range(2):
        p = half * pairs + i
        at = half * wide
        here = pl.ds(pl.multiple_of(i * PAIR, PAIR), PAIR)
        there = pl.ds(pl.multiple_of((pairs + i) * PAIR, PAIR), PAIR)
        q = (got[:, at:at + PAIR] + bias_ref[half, 0:1, here]) * (1.0 / math.sqrt(HEAD))
        q_ref[seg, p, 0] = jnp.where(lane < HEAD, q, 0.0).astype(LOW)
        q_ref[seg, p, 1] = jnp.where(lane < HEAD, 0.0, q).astype(LOW)
        k_ref[seg, p] = got[:, at + PAIR:at + 2 * PAIR].astype(LOW)
        v_ref[seg, p] = (got[:, at + 2 * PAIR:at + 3 * PAIR] + bias_ref[half, 0:1, there]).astype(LOW)


def attend(q_ref, k_ref, v_ref, o_ref, linv_ref, e_slot, count, mem, seg, p):
    col = lax.broadcasted_iota(jnp.int32, (1, ROWS), 1)
    lane = lax.broadcasted_iota(jnp.int32, (1, PAIR), 1)
    masking = jnp.where(live_at(col, count, mem), 0.0, masked_score)
    keys = k_ref[seg, p]
    values = jnp.concatenate([v_ref[seg, p], jnp.ones((ROWS, PAIR), LOW)], 1)
    got = []
    for j in range(2):
        scores = dot(q_ref[seg, p, j], keys, 1, 1) + masking
        peak = jnp.max(scores, -1, keepdims=True)
        e_slot[j] = jnp.exp(scores - peak).astype(LOW)
        got.append(dot(e_slot[j], values, 1, 0))
    first = lane < HEAD
    linv = 1.0 / jnp.where(first, got[0][:, PAIR:], got[1][:, PAIR:])
    linv_ref[seg, p] = linv
    o_ref[seg, p] = (jnp.where(first, got[0][:, :PAIR], got[1][:, :PAIR]) * linv).astype(LOW)


def attend_back(q_ref, k_ref, v_ref, o_ref, linv_ref, do_ref, e_slot, ds_ref, out_ref, seg, p, half, i):
    lane = lax.broadcasted_iota(jnp.int32, (1, PAIR), 1)
    keys, values = k_ref[...], v_ref[...]
    scaled = do_ref[seg, p].astype(F32) * linv_ref[...]
    product = scaled * o_ref[...].astype(F32)
    dq, dk, dv = [], None, None
    for j in range(2):
        mine = (lane < HEAD) if j == 0 else (lane >= HEAD)
        mine_low = jnp.where(mine, scaled, 0.0).astype(LOW)
        delta = jnp.sum(jnp.where(mine, product, 0.0), -1, keepdims=True)
        gap = dot(mine_low, values, 1, 1) - delta
        ds_ref[j] = (e_slot[j].astype(F32) * gap).astype(LOW)
        dq.append(dot(ds_ref[j], keys, 1, 0))
        one_v = dot(e_slot[j], mine_low, 0, 0)
        one_k = dot(ds_ref[j], q_ref[j], 0, 0)
        dv = one_v if dv is None else dv + one_v
        dk = one_k if dk is None else dk + one_k
    rows = pl.ds(pl.multiple_of(seg * ROWS, 32), ROWS)
    dq = jnp.where(lane < HEAD, dq[0], dq[1]) * (1.0 / math.sqrt(HEAD))
    for kind, value in enumerate((dq, dk, dv)):
        out_ref[half, rows, pl.ds(pl.multiple_of((3 * i + kind) * PAIR, PAIR), PAIR)] = value.astype(LOW)


class Place:
    def __init__(self):
        me = lax.axis_index("dp")
        self.t = lax.axis_index("tensor")
        self.x = me % 2
        self.y = (me // 2) % 2
        self.z = me // 4
        self.nt, self.nx, self.ny = 1 - self.t, 1 - self.x, 1 - self.y
        self.px = self.at(self.z, self.y, self.nx)
        self.py = self.at(self.z, self.ny, self.x)
        self.zs = [(self.z + d) % 4 for d in (1, 2, 3)]
        self.zb = [(self.z + 4 - d) % 4 for d in (1, 2, 3)]
        self.pz = [self.at(z, self.y, self.x) for z in self.zs]
        self.pz1 = self.at(self.z + 1 - 2 * (self.z % 2), self.y, self.x)
        self.pz2 = self.at((self.z + 2) % 4, self.y, self.x)
        self.pc = (me, self.nt)

    def at(self, z, y, x):
        return (z * 4 + y * 2 + x, self.t)

    def greet(self):
        barrier = pltpu.get_barrier_semaphore()
        devices = [self.px, self.py, *self.pz, self.pc]
        for device in devices:
            pl.semaphore_signal(barrier, inc=1, device_id=device, device_id_type=MESH)
        pl.semaphore_wait(barrier, len(devices))


class Wire:
    def __init__(self, send, recv):
        self.send, self.recv, self.count, self.open = send, recv, 0, {}

    def start(self, src, dst, device, landing):
        k = self.count
        self.count += 1

        def copy(a, b):
            return pltpu.make_async_remote_copy(
                src_ref=a, dst_ref=b, send_sem=self.send.at[k], recv_sem=self.recv.at[k],
                device_id=device, device_id_type=MESH)

        copy(src(), dst()).start()
        self.open[k] = lambda: copy(src(), dst()).wait_send()
        return lambda: copy(landing(), landing()).wait_recv()

    def sent(self, k):
        self.open.pop(k)()

    def drain(self):
        for k in list(self.open):
            self.sent(k)


class Gather:
    def __init__(self, wire, place, out, at, width, order):
        self.wire, self.p, self.out = wire, place, out
        self.cols, self.order, self.landed, self.crossing = pl.ds(at, width), order, [], []

    def view(self, z, y, x, half=None):
        return lambda: self.out.at[self.p.t if half is None else half, z, y, x, :, self.cols]

    def stage(self, s):
        p, every = self.p, slice(None)
        for wait in self.landed:
            wait()
        self.landed = []
        home = self.view(p.z, p.y, p.x)
        if self.order == "zxy":
            if s == 0:
                for k in range(3):
                    self.go(home, None, p.pz[k], self.view(p.zb[k], p.y, p.x))
            elif s == 1:
                self.go(self.view(every, p.y, p.x), None, p.px, self.view(every, p.y, p.nx))
                self.cross(every, p.y, p.x)
            elif s == 2:
                self.go(self.view(every, p.y, every), None, p.py, self.view(every, p.ny, every))
                self.cross(every, p.y, p.nx)
            else:
                self.cross(every, p.ny, every)
        else:
            if s == 0:
                self.go(home, None, p.py, self.view(p.z, p.ny, p.x))
            elif s == 1:
                for k in range(3):
                    self.go(self.view(p.z, every, p.x), None, p.pz[k], self.view(p.zb[k], every, p.x))
                self.cross(p.z, every, p.x)
            elif s == 2:
                self.go(self.view(every, every, p.x), None, p.px, self.view(every, every, p.nx))
                for k in range(3):
                    self.cross(p.zb[k], every, p.x)
            else:
                self.cross(every, every, p.nx)

    def go(self, src, dst, device, landing):
        self.landed.append(self.wire.start(src, src if dst is None else dst, device, landing))

    def cross(self, z, y, x):
        mine = self.view(z, y, x)
        self.crossing.append(self.wire.start(mine, mine, self.p.pc, self.view(z, y, x, self.p.nt)))

    def whole(self):
        for wait in self.crossing:
            wait()
        self.crossing = []


class Travel:
    def __init__(self, wire, place, keep, payload, held, landing, order):
        self.wire, self.p, self.keep, self.landed = wire, place, keep, None
        self.held, self.landing, self.order, self.payload = held, landing, order, payload

    def stage(self, s):
        p = self.p
        if s > 0:
            self.landed()
            before = self.payload if s == 1 else self.held.at[s - 2]
            for m in range(self.payload.shape[0]):
                stay = self.keep[m][self.order[s - 1]]
                mine, theirs = before[m].astype(F32), self.landing[s - 1, m].astype(F32)
                self.held[s - 1, m] = jnp.where(stay, mine, theirs).astype(self.held.dtype)
        if s < len(self.order):
            device = [p.px, p.py, p.pz1, p.pz2][self.order[s]]
            land = lambda: self.landing.at[s]
            self.landed = self.wire.start(lambda: self.payload if s == 0 else self.held.at[s - 1], land, device, land)


def keep_flags(owners_ref, row, device, levels):
    holders = [device]
    for bit in range(levels):
        stride = 2 ** (bit + 1)
        found = device * 0
        for source in range(owners_ref.shape[1]):
            position = source - source % stride + lax.rem(owners_ref[row, source], stride)
            found = found + jnp.where(position == device, source, 0)
        holders.append(found)
    return [a == b for a, b in zip(holders[:-1], holders[1:])]


def valid_count(lengths_ref, index, seg_len):
    start, valid = index * 0, index * 0
    for j in range(lengths_ref.shape[0]):
        length = lengths_ref[j]
        count = lax.div(length + (seg_len - 1), seg_len)
        inside = (start <= index) & (index < start + count)
        valid = valid + jnp.where(inside, jnp.minimum(length - (index - start) * seg_len, seg_len), 0)
        start = start + count
    return valid


G384 = (('yzx', 0, 128), ('zxy', 128, 256))
G512 = (('yzx', 0, 128), ('zxy', 128, 384))
G768 = (('yzx', 0, 128), ('zxy', 128, 256), ('yzx', 384, 128), ('zxy', 512, 256))
CHUNKS = ((0, 0, G384), (0, 384, G384), (0, 768, G384), (1, 0, G512), (2, 0, G768), (2, 768, G768), (3, 0, G768), (3, 768, G768))
GATHER = (
    ((0, 0, 0), (0, 1, 0), (1, 0, 0), (1, 1, 0), (0, 0, 1), (0, 1, 1), (2, 0, 0), (2, 1, 0), (1, 0, 1), (1, 1, 1), (0, 0, 2), (0, 1, 2), (3, 0, 0), (3, 1, 0), (2, 0, 1), (2, 1, 1), (1, 0, 2), (1, 1, 2), (0, 0, 3), (0, 1, 3)),
    ((4, 0, 0), (4, 1, 0), (3, 0, 1), (3, 1, 1), (2, 0, 2), (2, 1, 2), (1, 0, 3), (1, 1, 3)),
    (),
    ((4, 2, 0), (4, 3, 0), (4, 0, 1), (4, 1, 1), (3, 0, 2), (3, 1, 2), (2, 0, 3), (2, 1, 3)),
    (),
    ((5, 0, 0), (5, 1, 0), (4, 2, 1), (4, 3, 1), (4, 0, 2), (4, 1, 2), (3, 0, 3), (3, 1, 3)),
    (),
    ((5, 2, 0), (5, 3, 0), (5, 0, 1), (5, 1, 1), (4, 2, 2), (4, 3, 2), (4, 0, 3), (4, 1, 3)),
    (),
    ((6, 0, 0), (6, 1, 0), (5, 2, 1), (5, 3, 1), (5, 0, 2), (5, 1, 2), (4, 2, 3), (4, 3, 3)),
    (),
    ((6, 2, 0), (6, 3, 0), (6, 0, 1), (6, 1, 1), (5, 2, 2), (5, 3, 2), (5, 0, 3), (5, 1, 3)),
    (),
    ((7, 0, 0), (7, 1, 0), (6, 2, 1), (6, 3, 1), (6, 0, 2), (6, 1, 2), (5, 2, 3), (5, 3, 3)),
    ((7, 2, 0), (7, 3, 0), (7, 0, 1), (7, 1, 1), (6, 2, 2), (6, 3, 2), (6, 0, 3), (6, 1, 3)),
    (),
    ((7, 2, 1), (7, 3, 1), (7, 0, 2), (7, 1, 2), (6, 2, 3), (6, 3, 3)),
    (),
    ((7, 2, 2), (7, 3, 2), (7, 0, 3), (7, 1, 3)),
    (),
    ((7, 2, 3), (7, 3, 3)),
    (),
    (),
    (),
    (),
    (),
    (),
    (),
    (),
)


class Copies:
    def __init__(self, sems):
        self.sems, self.count = sems, 0

    def start(self, src, dst):
        k = self.count
        self.count += 1
        pltpu.make_async_copy(src(), dst(), self.sems.at[k]).start()
        return lambda: pltpu.make_async_copy(src(), dst(), self.sems.at[k]).wait()


def front_kernel(kernels, mem, seg_len, width, *refs):
    n_in = 14 if kernels else 11
    lengths_ref, owners_ref, bias_in, mem_a, mem_b, tok_in, cot_in = refs[:7]
    weights_in = refs[7:n_in]
    (wqkv_out, wout_out, wup_out, wdown_out, q_out, k_out, v_out, o_out, linv_out, e_out, xt_out, x1t_out, unit_out, inv_out,
     dh_out, df_out, dft_out, g_out, d_out, y_out, sums_ref, tail_ref) = refs[n_in:n_in + 22]
    (wqkv, wout, wup, wdown, bias_ref, payload, held, landing, tok_ref, x_ref, cot_ref, vec_ref, o_ref, dh_ref, low_ref, unit_ref,
     inv_ref, flip_ref, send, recv, here, e_sems) = refs[-22:]
    weights = (wqkv, wout, wup, wdown)
    R = 2 * ROWS
    pairs = width // PAIR
    D = x_ref.shape[1]
    hidden = wup.shape[-1]
    copies = Copies(here)
    t = lax.axis_index("tensor")
    device = lax.axis_index("dp")
    loads = []
    for k, (a, s) in enumerate(((tok_in, 0), (tok_in, 1), (cot_in, 0), (cot_in, 1))):
        loads.append(copies.start(lambda a=a, s=s: a.at[2 * t + s], lambda k=k: tok_ref.at[k]))
    if kernels:
        place = Place()
        wire = Wire(send, recv)

        def mine(c, cols):
            return lambda: weights[c].at[place.t, place.z, place.y, place.x, :, cols]

        own = []
        for i in range(pairs):
            for kind in range(3):
                cols = pl.ds(i * PAIR, PAIR)
                own.append(copies.start(lambda kind=kind, cols=cols: weights_in[kind].at[:, cols], mine(0, pl.ds((3 * i + kind) * PAIR, PAIR))))
        own.append(copies.start(lambda: weights_in[3], mine(1, pl.ds(0, width))))
        own.append(copies.start(lambda: weights_in[6], mine(1, pl.ds(width, PAIR))))
        own.append(copies.start(lambda: weights_in[4], mine(2, pl.ds(0, hidden))))
        own.append(copies.start(lambda: weights_in[5], mine(3, pl.ds(0, hidden))))
        own_bias = copies.start(lambda: bias_in, lambda: bias_ref.at[place.t])
        for m in range(2):
            payload[0, m] = mem_a[2 * t + m]
            payload[1, m] = mem_b[2 * t + m]
        place.greet()
        keep = [keep_flags(owners_ref, 2 * t + m, device, 4) for m in range(2)]
        travel = Travel(wire, place, keep, payload.at[0], held.at[0], landing.at[0], (3, 2, 1, 0))
        second = Travel(wire, place, keep, payload.at[1], held.at[1], landing.at[1], (3, 2, 1, 0))
        parts = []
        for c, at, cuts in CHUNKS:
            parts.append([Gather(wire, place, weights[c], at + first, wide, order) for order, first, wide in cuts])

        def tick(point):
            for c, part, s in GATHER[point]:
                parts[c][part].stage(s)

        def ready(c):
            for part in parts[c]:
                part.whole()

        travel.stage(0)
        for wait in own:
            wait()
        bias_wait = wire.start(lambda: bias_in, lambda: bias_ref.at[place.t], place.pc, lambda: bias_ref.at[place.nt])
        for k, (c, part, s) in enumerate(GATHER[0]):
            parts[c][part].stage(s)
            if k in (1, 5, 11, 19):
                travel.stage((1, 5, 11, 19).index(k) + 1)
        own_bias()
        bias_wait()
        moved, moved_cot = held.at[0, 3], held.at[1, 3]
        later = second.stage
    else:
        fetched = [copies.start(lambda c=c: weights_in[c], lambda c=c: weights[c]) for c in range(4)]
        fetched.append(copies.start(lambda: bias_in, lambda: bias_ref))
        for wait in fetched:
            wait()
        moved, moved_cot = mem_a, mem_b
        tick = ready = later = lambda step: None
    counts = [valid_count(lengths_ref, device * 4 + 2 * t + s, seg_len) for s in range(2)]
    for wait in loads:
        wait()
    for s in range(2):
        for k, ref in enumerate((x_ref, cot_ref)):
            ref[s * ROWS + TOK - 16:(s + 1) * ROWS, :] = jnp.zeros((16 + TAIL, D), LOW)
            ref[s * ROWS:s * ROWS + seg_len, :] = tok_ref[2 * k + s]
        x_ref[s * ROWS + TOK:s * ROWS + TOK + mem, :] = moved[s]
    flip_ref[...] = x_ref[...].T
    saves = [copies.start(lambda: flip_ref, lambda: xt_out)]

    def attention(q_ref, k_ref, v_ref, linv_ref, slots):
        def e_copy(seg, p, slot):
            return pltpu.make_async_copy(slots.at[slot], e_out.at[seg, p], e_sems.at[slot])

        def step(n, carry):
            i, seg, half = n // 4, (n // 2) % 2, n % 2
            for k in range(12):
                @pl.when(n == k)
                def _():
                    tick(1 + k)
                    if k in (1, 3, 5, 7, 9):
                        later(k // 2)
                    if k in (4, 8):
                        ready(k // 4)

            @pl.when(half == 0)
            def _():
                project(x_ref, wqkv, bias_ref, q_ref, k_ref, v_ref, seg, i, pairs)

            count = jnp.where(seg == 0, counts[0], counts[1])

            @pl.when(n > 1)
            def _():
                e_copy(seg, half * pairs + i, half).wait()

            attend(q_ref, k_ref, v_ref, o_ref, linv_ref, slots.at[half], count, mem, seg, half * pairs + i)
            e_copy(seg, half * pairs + i, half).start()
            return carry

        ready(0)
        lax.fori_loop(0, 4 * pairs, step, 0)
        done = []
        for a, b in ((q_ref, q_out), (k_ref, k_out), (v_ref, v_out), (o_ref, o_out), (linv_ref, linv_out), (wqkv, wqkv_out)):
            done.append(copies.start(lambda a=a: a, lambda b=b: b))
        tick(13)
        ready(3)
        done.append(copies.start(lambda: wout, lambda: wout_out))
        for half in range(2):
            e_copy(0, 0, half).wait()
        for wait in done:
            wait()

    six = (2, 2 * pairs, ROWS, PAIR)
    pl.run_scoped(
        attention, pltpu.VMEM((2, 2 * pairs, 2, ROWS, PAIR), LOW), pltpu.VMEM(six, LOW), pltpu.VMEM(six, LOW),
        pltpu.VMEM(six, F32), pltpu.VMEM((2, 2, ROWS, ROWS), LOW))

    sums_ref[...] = jnp.zeros_like(sums_ref)
    vec_ref[...] = mat(wout, 0, slice(width, width + PAIR)).astype(F32).T[:8]
    vec = {n: vec_ref[k:k + 1, :] for k, n in enumerate(("b_out", "b_down", "gain_attn", "shift_attn", "gain_ffn", "shift_ffn"))}

    def out_step(s, carry):
        rows = pl.ds(pl.multiple_of(s * ROWS, ROWS), ROWS)
        h = x_ref[rows, :].astype(F32) + vec["b_out"]
        for t in range(2):
            o = jnp.concatenate([o_ref[s, t * pairs + i] for i in range(pairs)], 1)
            h = h + dot(o, mat(wout, t, slice(0, width)), 1, 1)
        unit, inv = normed(h)
        x1 = unit * vec["gain_attn"] + vec["shift_attn"]
        dh_ref[rows, :] = x1
        low_ref[rows, :] = x1.astype(LOW)
        unit_ref[rows, :] = unit.astype(LOW)
        inv_ref[rows, :] = inv
        return carry

    lax.fori_loop(0, 2, out_step, 0)
    tick(14)
    tick(15)
    for wait in saves:
        wait()
    flip_ref[...] = low_ref[...].T
    saves = [copies.start(lambda a=a: a, lambda b=b: b) for a, b in ((flip_ref, x1t_out), (unit_ref, unit_out), (inv_ref, inv_out))]

    ends = []

    def ffn(g_ref, d_ref):
        for s in range(2):
            cot_ref[s * ROWS + TOK:s * ROWS + TOK + mem, :] = moved_cot[s]
        tile = min(hidden // 2, 256)
        part = R // 4

        def up_cols(first, count, base):
            def up_step(k, carry):
                t = k % 2
                at = first + (k // 2) * tile
                for n in range(2 * count):
                    @pl.when(k == n)
                    def _():
                        tick(base + n)
                        if n == 0:
                            ready(4 + (base - 16) // 6)
                cols = pl.ds(pl.multiple_of(at, PAIR), tile)
                u = dot(low_ref[...], mat(wup, t, cols), 1, 0)
                u = u + bias_ref[t, 0:1, pl.ds(pl.multiple_of(2 * width + at, PAIR), tile)]
                phi = 0.5 * (1.0 + lax.erf(u * (1.0 / math.sqrt(2.0))))
                g_ref[t, :, cols] = (u * phi).astype(LOW)
                d_ref[t, :, cols] = (phi + u * (jnp.exp(-0.5 * u * u) * (1.0 / math.sqrt(2.0 * math.pi)))).astype(LOW)
                return carry

            lax.fori_loop(0, 2 * count, up_step, 0)

        up_cols(0, hidden // 2 // tile, 16)
        up_cols(hidden // 2, hidden // 2 // tile, 22)
        done = [copies.start(lambda a=a: a, lambda b=b: b) for a, b in ((wup, wup_out), (g_ref, g_out), (d_ref, d_out))]
        tick(28)
        ready(6)
        ready(7)
        done.append(copies.start(lambda: wdown, lambda: wdown_out))

        def down_step(s, carry):
            rows = pl.ds(pl.multiple_of(s * part, part), part)
            h = dh_ref[rows, :] + vec["b_down"]
            for t in range(2):
                h = h + dot(g_ref[t, rows, :], mat(wdown, t, slice(None)), 1, 1)
            unit, inv = normed(h)
            count = jnp.where(s < 2, counts[0], counts[1])
            at = lax.broadcasted_iota(jnp.int32, (part, 1), 0) + (s % 2) * part
            live = jnp.where(live_at(at, count, mem), 1.0, 0.0)
            x_ref[rows, :] = ((unit * vec["gain_ffn"] + vec["shift_ffn"]) * live).astype(LOW)
            dy = cot_ref[rows, :].astype(F32) * live
            fold(sums_ref, 4, dy * unit)
            fold(sums_ref, 5, dy)
            dh = norm_back(dy * vec["gain_ffn"], unit, inv)
            fold(sums_ref, 1, dh)
            dh_ref[rows, :] = dh
            cot_ref[rows, :] = dh.astype(LOW)
            return carry

        lax.fori_loop(0, 4, down_step, 0)
        for a, b in ((cot_ref, df_out), (dh_ref, dh_out)):
            ends.append(copies.start(lambda a=a: a, lambda b=b: b))
        for wait in saves:
            wait()
        flip_ref[...] = cot_ref[...].T
        ends.append(copies.start(lambda: flip_ref, lambda: dft_out))
        for s in range(2):
            tok_ref[s] = x_ref[s * ROWS:s * ROWS + seg_len, :]
            tail_ref[s] = x_ref[s * ROWS + TOK:s * ROWS + TOK + mem, :]
        ends.append(copies.start(lambda: tok_ref.at[pl.ds(0, 2)], lambda: y_out))
        for wait in done:
            wait()

    pl.run_scoped(ffn, pltpu.VMEM((2, R, hidden), LOW), pltpu.VMEM((2, R, hidden), LOW))
    for wait in ends:
        wait()
    if kernels:
        wire.drain()


def front(lengths, owners, bias, mem_a, mem_b, tokens, cots, weights, width, hidden, mem, kernels, cid):
    seg_len, D = tokens.shape[1:]
    R = 2 * ROWS
    pairs = width // PAIR
    S, V = jax.ShapeDtypeStruct, pltpu.VMEM
    hbm, vmem, smem = (pl.BlockSpec(memory_space=m) for m in (pl.ANY, pltpu.VMEM, pltpu.SMEM))
    full = (2, *GRID, D // math.prod(GRID)) if kernels else (2, D)
    six = (2, 2 * pairs, ROWS, PAIR)
    payload = (2, mem, D)
    count = 9 + sum(8 if part[0] == "zxy" else 10 for _, _, cuts in CHUNKS for part in cuts)
    shapes = [(*full, w) for w in (3 * width, width + PAIR, hidden, hidden)]
    params = dict(collective_id=cid, has_side_effects=True) if kernels else {}
    return pl.pallas_call(
        functools.partial(front_kernel, kernels, mem, seg_len, width),
        out_shape=[
            *(S(s, LOW) for s in shapes), S((2, 2 * pairs, 2, ROWS, PAIR), LOW), S(six, LOW), S(six, LOW), S(six, LOW), S(six, F32),
            S((2, 2 * pairs, 2, ROWS, ROWS), LOW), S((D, R), LOW), S((D, R), LOW), S((R, D), LOW), S((R, 1), F32), S((R, D), F32),
            S((R, D), LOW), S((D, R), LOW), S((2, R, hidden), LOW), S((2, R, hidden), LOW), S((2, seg_len, D), LOW), S((8, D), F32), S(payload, LOW)],
        in_specs=[smem, smem, vmem, vmem, vmem] + [hbm] * (2 + len(weights)),
        out_specs=[hbm] * 20 + [vmem] * 2,
        scratch_shapes=[
            *(V(s, LOW) for s in shapes), V((2, 1, 2 * width + hidden), F32), V((2, *payload), LOW), V((2, 4, *payload), LOW), V((2, 4, *payload), LOW),
            V((4, seg_len, D), LOW), V((R, D), LOW), V((R, D), LOW), V((8, D), F32), V(six, LOW), V((R, D), F32), V((R, D), LOW),
            V((R, D), LOW), V((R, 1), F32), V((D, R), LOW),
            pltpu.SemaphoreType.DMA((count,)), pltpu.SemaphoreType.DMA((count,)), pltpu.SemaphoreType.DMA((40,)),
            pltpu.SemaphoreType.DMA((2,))],
        compiler_params=pltpu.CompilerParams(vmem_limit_bytes=63 << 20, **params),
    )(lengths, owners, bias, mem_a, mem_b, tokens, cots, *weights)


class Scatter:
    def __init__(self, wire, place, acc, sink, cols, order, landings):
        self.wire, self.p, self.acc, self.sink = wire, place, acc, sink
        self.cols, self.order, self.landed = cols, order, []
        self.r1, self.r2, self.r3 = landings

    def view(self, z, y, x):
        return lambda: self.acc.at[z, y, x, :, self.cols]

    def sum(self, z, y, x, terms):
        total = self.acc[z, y, x, :, self.cols].astype(F32)
        for term in terms:
            total = total + term.astype(F32)
        return total

    def add(self, z, y, x, *terms):
        if len(terms) == 1:
            self.acc[z, y, x, :, self.cols] = self.acc[z, y, x, :, self.cols] + terms[0]
            return
        self.acc[z, y, x, :, self.cols] = self.sum(z, y, x, terms).astype(self.acc.dtype)

    def finish(self, *terms):
        self.sink(self.sum(self.p.z, self.p.y, self.p.x, terms))

    def stage(self, s):
        p, every = self.p, slice(None)
        for wait in self.landed:
            wait()
        self.landed = []
        r1, r2, r3 = self.r1, self.r2, self.r3
        if self.order == "yxz":
            if s == 0:
                self.go(self.view(every, p.ny, every), lambda: r1, p.py)
            elif s == 1:
                for z in range(4):
                    for x in range(2):
                        self.add(z, p.y, x, r1[z, x])
                self.go(self.view(every, p.y, p.nx), lambda: r2, p.px)
            elif s == 2:
                for z in range(4):
                    self.add(z, p.y, p.x, r2[z])
                for k in range(3):
                    self.go(self.view(p.zs[k], p.y, p.x), lambda k=k: r3.at[k], p.pz[k])
            else:
                self.finish(r3[0], r3[1], r3[2])
        else:
            if s == 0:
                self.go(self.view(every, every, p.nx), lambda: r1, p.px)
            elif s == 1:
                for z in range(4):
                    for y in range(2):
                        self.add(z, y, p.x, r1[z, y])
                for k in range(3):
                    self.go(self.view(p.zs[k], every, p.x), lambda k=k: r2.at[k], p.pz[k])
            elif s == 2:
                for y in range(2):
                    self.add(p.z, y, p.x, r2[0, y], r2[1, y], r2[2, y])
                self.go(self.view(p.z, p.ny, p.x), lambda: r3, p.py)
            else:
                self.finish(r3[...])

    def go(self, src, landing, device):
        self.landed.append(self.wire.start(src, landing, device, landing))


def scatter_shapes(rows, order, wide):
    V = pltpu.VMEM
    if order == "xzy":
        return [V((4, 2, rows, wide), LOW), V((3, 2, rows, wide), LOW), V((rows, wide), LOW)]
    return [V((4, 2, rows, wide), LOW), V((4, rows, wide), LOW), V((3, rows, wide), LOW)]


class Total:
    def __init__(self, wire, place, vec, out, hops, vz):
        self.wire, self.p, self.landed = wire, place, []
        self.vec, self.out, self.hops, self.vz = vec, out, hops, vz

    def stage(self, s):
        p, hops = self.p, self.hops
        for wait in self.landed:
            wait()
        self.landed = []
        if s == 0:
            self.go(lambda: self.vec, lambda: hops.at[0], p.pc)
        elif s < 4:
            hops[2 * s - 1] = (self.vec[...] if s == 1 else hops[2 * s - 3]) + hops[2 * s - 2]
            if s < 3:
                self.go(lambda: hops.at[2 * s - 1], lambda: hops.at[2 * s], (p.px, p.py)[s - 1])
            else:
                for k in range(3):
                    self.go(lambda: hops.at[5], lambda k=k: self.vz.at[k], p.pz[k])
        else:
            self.out[...] = hops[5] + self.vz[0] + self.vz[1] + self.vz[2]

    def go(self, src, landing, device):
        self.landed.append(self.wire.start(src, landing, device, landing))


S384 = (('xzy', 0, 128), ('yxz', 128, 256))
S768 = (('xzy', 0, 128), ('yxz', 128, 256), ('xzy', 384, 128), ('yxz', 512, 256))
SUMS = ((0, 0, 768, S768), (0, 768, 768, S768), (1, 0, 768, S768), (1, 768, 768, S768), (2, 0, 384, S384), (3, 0, 384, S384), (3, 384, 384, S384), (3, 768, 384, S384))
SCATTER = (
    ((0, 2, 0), (0, 3, 0), (0, 0, 0), (0, 1, 0)),
    ((1, 2, 0), (1, 3, 0), (1, 0, 0), (1, 1, 0)),
    (),
    ((0, 2, 1), (0, 3, 1), (0, 0, 1), (0, 1, 1)),
    ((2, 2, 0), (2, 3, 0), (2, 0, 0), (2, 1, 0)),
    ((1, 2, 1), (1, 3, 1), (1, 0, 1), (1, 1, 1), (0, 2, 2), (0, 3, 2), (0, 0, 2), (0, 1, 2)),
    ((1, 0, 2), (1, 1, 2), (0, 2, 3), (0, 3, 3), (0, 0, 3), (0, 1, 3)),
    ((1, 2, 2), (1, 3, 2)),
    ((3, 2, 0), (3, 3, 0), (3, 0, 0), (3, 1, 0), (2, 2, 1), (2, 3, 1), (2, 0, 1), (2, 1, 1), (1, 2, 3), (1, 3, 3), (1, 0, 3), (1, 1, 3)),
    (),
    ((2, 2, 2), (2, 3, 2), (2, 0, 2), (2, 1, 2)),
    ((4, 0, 0), (4, 1, 0)),
    ((2, 2, 3), (2, 3, 3), (2, 0, 3), (2, 1, 3)),
    (),
    (),
    (),
    ((3, 2, 1), (3, 3, 1), (3, 0, 1), (3, 1, 1)),
    ((4, 0, 1), (4, 1, 1)),
    ((5, 0, 0), (5, 1, 0), (3, 2, 2), (3, 3, 2), (3, 0, 2), (3, 1, 2)),
    (),
    (),
    ((4, 0, 2), (4, 1, 2), (3, 2, 3), (3, 3, 3), (3, 0, 3), (3, 1, 3)),
    ((6, 0, 0), (6, 1, 0), (5, 0, 1), (5, 1, 1)),
    (),
    ((4, 0, 3), (4, 1, 3)),
    ((5, 0, 2), (5, 1, 2)),
    ((7, 0, 0), (7, 1, 0)),
    ((6, 0, 1), (6, 1, 1), (5, 0, 3), (5, 1, 3)),
    (),
    ((6, 0, 2), (6, 1, 2), (7, 0, 1), (7, 1, 1), (6, 0, 3), (6, 1, 3), (7, 0, 2), (7, 1, 2), (7, 0, 3), (7, 1, 3)),
)
TOTAL = (13, 16, 19, 22, 25)
PART = 768
SUB = 768


def back_kernel(kernels, mem, seg_len, width, hidden, *refs):
    n_land = 3 * sum(len(cuts) for _, _, _, cuts in SUMS)
    (owners_ref, sums_in, wqkv_in, wout_in, wup_in, wdown_in, q_in, k_in, v_in, o_in, linv_in, e_in, xt_in, x1t_in, unit_in, inv_in,
     dh_in, df_in, dft_in, g_in, d_in, y_in, tail_in) = refs[:23]
    (y_out, dx_out, om_out, gm_out, vec_out, late_out, gq_out, gk_out, gv_out, out_out, up_out, down_out) = refs[23:35]
    (tot_ref, late_ref, o_ref, do_ref, dh_ref, low_ref, unit_ref, inv_ref, flip_ref, wout, payload, held, landing,
     hops, vz, hops2, vz2, acc0, acc1, acc2, acc3, oth0, oth1, oth2, oth3, away0, away1, away2, away3) = refs[35:64]
    landings = refs[64:64 + n_land]
    send, recv, here, pair_sems = refs[64 + n_land:]
    R = 2 * ROWS
    pairs = width // PAIR
    D = dh_ref.shape[1]
    grid_rows = (4, 2, 2, D // 16)
    wide_qkv = 3 * PAIR
    steps = hidden // PART
    copies = Copies(here)
    accs, others, aways = (acc0, acc1, acc2, acc3), (oth0, oth1, oth2, oth3), (away0, away1, away2, away3)
    place = Place()
    halves = (place.nt, place.t) if kernels else (0, 1)
    if kernels:
        wire = Wire(send, recv)

        def sink(c, at, first, wide):
            if c < 3:
                out = (down_out, up_out, out_out)[c]

                def put(total):
                    out[:, at + first:at + first + wide] = total

                return put
            cols = slice(at // 3, at // 3 + PAIR)

            def put_q(total):
                gq_out[:, cols] = total

            def put_kv(total):
                gk_out[:, cols] = total[:, :PAIR]
                gv_out[:, cols] = total[:, PAIR:]

            return put_kv if first else put_q

        parts, crossed = [], {}
        taken = 0
        for c, at, _, cuts in SUMS:
            parts.append([])
            for order, first, wide in cuts:
                cols = slice(at + first, at + first + wide)
                parts[-1].append(Scatter(wire, place, accs[c], sink(c, at, first, wide), cols, order, landings[taken:taken + 3]))
                taken += 3
        total = Total(wire, place, tot_ref, vec_out, hops, vz)

    def point(p):
        if not kernels:
            return
        for event in SCATTER[p]:
            run(event)
        if p in TOTAL:
            total.stage(TOTAL.index(p))

    def run(event):
        n, part, s = event
        if n in crossed:
            c, at, wide, _ = SUMS[n]
            crossed.pop(n)()
            cols = slice(at, at + wide)

            def together(z, carry):
                accs[c][z, :, :, :, cols] = accs[c][z, :, :, :, cols] + others[c][z, :, :, :, cols]
                return carry

            lax.fori_loop(0, 4, together, 0)
        parts[n][part].stage(s)

    away_open = {}

    def away_of(n):
        c, at, wide, _ = SUMS[n]
        return aways[c].at[at // wide] if c == 3 else aways[c]

    def fresh(n):
        c = SUMS[n][0]
        if kernels and c in away_open:
            wire.sent(away_open.pop(c))

    def emit(n, h, at, value):
        c, first, wide, _ = SUMS[n]
        size = value.shape[1]
        value = value.astype(LOW)
        if not kernels:
            away_of(n)[:, :, :, :, pl.ds(at, size)] = value.reshape(*grid_rows, size)
        elif h == 0:
            away_of(n)[:, :, :, :, pl.ds(at, size)] = value.reshape(*grid_rows, size)
        else:
            cols = pl.ds(first + at, size) if isinstance(at, int) else pl.ds(pl.multiple_of(first + at, PAIR), size)
            accs[c][:, :, :, :, cols] = value.reshape(*grid_rows, size)

    def emitted(n, h):
        c, at, wide, _ = SUMS[n]
        if kernels:
            if h == 0:
                land = lambda: others[c].at[:, :, :, :, pl.ds(at, wide)]
                away_open[c if c < 3 else (c, n)] = wire.count
                crossed[n] = wire.start(lambda: away_of(n), land, place.pc, land)
        elif c < 3:
            out = (down_out, up_out, out_out)[c]
            copies.start(lambda: away_of(n), lambda: out.at[h, :, :, :, :, pl.ds(at, wide)])()
        else:
            for kind, out in enumerate((gq_out, gk_out, gv_out)):
                copies.start(lambda: away_of(n).at[:, :, :, :, pl.ds(kind * PAIR, PAIR)],
                             lambda: out.at[h, :, :, :, :, pl.ds(at // 3, PAIR)])()

    tot_ref[...] = jnp.zeros_like(tot_ref)
    tot_ref[0:8, :] = sums_in[...]
    late_ref[...] = jnp.zeros_like(late_ref)
    load_flip = copies.start(lambda: dft_in, lambda: flip_ref)

    def both_of(ref, half):
        return ref.at[pl.ds(2 * half, 2)]

    def tile_cols(j):
        return pl.ds(j * PART, PART)

    def ffn(tok_ref, df_ref, x1t_ref, g_slot, d_slot, du_slot, wd_slot, wu_slot):
        def load(a, slot, h, j, weight):
            half = halves[h]
            if weight and kernels:
                return copies.start(lambda: a.at[half, :, :, :, :, tile_cols(j)], lambda: slot.at[h])
            return copies.start(lambda: a.at[half, :, tile_cols(j)], lambda: slot.at[h])

        waits = {}

        def fetch(j, kinds):
            for kind in kinds:
                a, slot, weight = {"g": (g_in, g_slot, 0), "d": (d_in, d_slot, 0), "wd": (wdown_in, wd_slot, 1), "wu": (wup_in, wu_slot, 1)}[kind]
                for h in range(2):
                    waits[kind, h, j] = load(a, slot, h, j, weight)

        fetch(0, ["g"])
        load_df = copies.start(lambda: df_in, lambda: df_ref)
        fetch(0, ["wd", "d"])
        load_x1t = copies.start(lambda: x1t_in, lambda: x1t_ref)
        fetch(0, ["wu"])
        load_dh = copies.start(lambda: dh_in, lambda: dh_ref)
        later = [copies.start(lambda a=a: a, lambda b=b: b) for a, b in ((unit_in, unit_ref), (inv_in, inv_ref), (o_in, o_ref), (wout_in, wout))]
        load_y = copies.start(lambda: y_in, lambda: tok_ref)
        y_waits = []
        if kernels:
            place.greet()
        load_flip()
        part = R // 4
        for j in range(steps):
            fresh(j)
            for h in range(2):
                waits["g", h, j]()

                def down(k, carry):
                    cols = pl.ds(pl.multiple_of(k * SUB, SUB), SUB)
                    emit(j, h, k * SUB, dot(flip_ref[...], g_slot[h, :, cols], 1, 0))
                    return carry

                lax.fori_loop(0, PART // SUB, down, 0)
                emitted(j, h)
                if j + 1 < steps:
                    waits["g", h, j + 1] = load(g_in, g_slot, h, j + 1, 0)
            point(j)
        load_df()
        load_x1t()
        load_y()
        if kernels:
            y_sent = wire.count
            y_waits.append(wire.start(lambda: tok_ref, lambda: both_of(y_out, place.t), place.pc, lambda: both_of(y_out, place.nt)))
            y_waits.append(copies.start(lambda: tok_ref, lambda: both_of(y_out, place.t)))
        else:
            y_waits.append(copies.start(lambda: tok_ref, lambda: y_out))
        for j in range(steps):
            fresh(2 + j)
            for h in range(2):
                waits["wd", h, j]()
                waits["d", h, j]()

                def up(k, carry):
                    cols = pl.ds(pl.multiple_of(k * SUB, SUB), SUB)
                    weight = wd_slot[h, ..., cols].reshape(D, SUB)
                    du = dot(df_ref[...], weight, 1, 0) * d_slot[h, :, cols].astype(F32)
                    tot_ref[pl.ds(8 + 2 * halves[h] + j, 1), cols] = jnp.sum(du, 0, keepdims=True)
                    du_slot[:, cols] = du.astype(LOW)
                    emit(2 + j, h, k * SUB, dot(x1t_ref[...], du_slot[:, cols], 1, 0))
                    return carry

                lax.fori_loop(0, PART // SUB, up, 0)
                emitted(2 + j, h)
                point(2 + 4 * j + 2 * h)
                waits["wu", h, j]()
                if j == 0 and h == 0:
                    load_dh()

                def inward(s, carry):
                    rows = pl.ds(pl.multiple_of(s * part, part), part)
                    dh_ref[rows, :] += dot(du_slot[rows, :], wu_slot[h].reshape(D, PART), 1, 1)
                    return carry

                lax.fori_loop(0, 4, inward, 0)
                if j + 1 < steps:
                    for kind, a, slot, weight in (("wd", wdown_in, wd_slot, 1), ("d", d_in, d_slot, 0), ("wu", wup_in, wu_slot, 1)):
                        waits[kind, h, j + 1] = load(a, slot, h, j + 1, weight)
                point(3 + 4 * j + 2 * h)
        for wait in later:
            wait()
        for wait in y_waits:
            wait()
        if kernels:
            wire.sent(y_sent)

    V = pltpu.VMEM
    weight_tile = (*grid_rows, PART) if kernels else (D, PART)
    pl.run_scoped(ffn, V((2, seg_len, D), LOW), V((R, D), LOW), V((D, R), LOW), V((2, R, PART), LOW), V((2, R, PART), LOW), V((R, PART), LOW),
                  V((2, *weight_tile), LOW), V((2, *weight_tile), LOW))

    vec_gain = mat(wout, 0, slice(width, width + PAIR)).astype(F32).T[2:3]
    quarter = R // 4

    def norm_step(s, carry):
        rows = pl.ds(pl.multiple_of(s * quarter, quarter), quarter)
        dx = dh_ref[rows, :]
        unit = unit_ref[rows, :].astype(F32)
        fold(tot_ref, 2, dx * unit)
        fold(tot_ref, 3, dx)
        dh = norm_back(dx * vec_gain, unit, inv_ref[rows, :])
        fold(tot_ref, 0, dh)
        dh_ref[rows, :] = dh
        low_ref[rows, :] = dh.astype(LOW)
        return carry

    lax.fori_loop(0, 4, norm_step, 0)
    point(10)
    flip_ref[...] = low_ref[...].T
    for h in range(2):
        both = jnp.concatenate([jnp.concatenate([o_ref[s, halves[h] * pairs + i] for i in range(pairs)], 1) for s in range(2)], 0)
        emit(4, h, 0, dot(flip_ref[...], both, 1, 0))
        emitted(4, h)
    load_xt = copies.start(lambda: xt_in, lambda: flip_ref)

    def out_back(s, carry):
        rows = pl.ds(pl.multiple_of(s * ROWS, ROWS), ROWS)
        for t in range(2):
            got = dot(low_ref[rows, :], mat(wout, t, slice(0, width)), 1, 0).astype(LOW)
            for i in range(pairs):
                do_ref[s, t * pairs + i] = got[:, i * PAIR:(i + 1) * PAIR]
        return carry

    def attention(tok_ref, q_s, k_s, v_s, o_s, linv_s, e_s, ds_ref, out_ref, wqkv):
        def place_of(n):
            return n // 4, (n // 2) % 2, n % 2

        def slot_copies(n):
            i, seg, half = place_of(n)
            p, slot = half * pairs + i, n % 2
            table = ((q_in, q_s), (k_in, k_s), (v_in, v_s), (o_in, o_s), (linv_in, linv_s), (e_in, e_s))
            return [pltpu.make_async_copy(a.at[seg, p], b.at[slot], pair_sems.at[slot, k]) for k, (a, b) in enumerate(table)]

        if kernels:
            device = lax.axis_index("dp")
            keep = [keep_flags(owners_ref, 2 * place.t + m, device, 4) for m in range(2)]
            payload[0] = tail_in[...]
            first = Travel(wire, place, keep, payload.at[0], held.at[0], landing.at[0], (0, 1, 2, 3)).stage
            second = Travel(wire, place, keep, payload.at[1], held.at[1], landing.at[1], (0, 1, 2, 3)).stage
        else:
            first = second = lambda s: None
        for copy in slot_copies(0):
            copy.start()
        load_w = copies.start(lambda: wqkv_in, lambda: wqkv)
        point(11)
        lax.fori_loop(0, 2, out_back, 0)
        point(12)
        load_xt()

        def gradients(i):
            cols = pl.ds(i * wide_qkv, wide_qkv)
            for h in range(2):
                emit(5 + i, h, 0, dot(flip_ref[...], out_ref[halves[h], :, cols], 1, 0))
                emitted(5 + i, h)
                late_ref[halves[h], i:i + 1, :] = jnp.sum(out_ref[halves[h], :, cols].astype(F32), 0, keepdims=True)

        def step(n, carry):
            i, seg, half = place_of(n)
            slot = n % 2

            @pl.when(n < 4 * pairs - 1)
            def _():
                for copy in slot_copies(n + 1):
                    copy.start()

            for k in range(12):
                @pl.when(n == k)
                def _():
                    if k in (4, 8):
                        gradients(k // 4 - 1)
                    point(13 + k)
                    if k in (1, 3, 5, 7, 10):
                        first((1, 3, 5, 7, 10).index(k))
            for copy in slot_copies(n):
                copy.wait()
            attend_back(q_s.at[slot], k_s.at[slot], v_s.at[slot], o_s.at[slot], linv_s.at[slot], do_ref, e_s.at[slot], ds_ref, out_ref,
                        seg, half * pairs + i, half, i)
            return carry

        lax.fori_loop(0, 4 * pairs, step, 0)
        gradients(pairs - 1)
        late = Total(wire, place, late_ref, late_out, hops2, vz2).stage if kernels else (lambda s: None)
        late(0)
        point(25)
        load_w()
        ends = [low_ref.at[pl.ds(s * ROWS + TOK, TAIL)] for s in range(2)]

        def inputs(rows):
            dx = dh_ref[rows, :]
            for t in range(2):
                dx = dx + dot(out_ref[t, rows, :], mat(wqkv, t, slice(None)), 1, 1)
            return dx.astype(LOW)

        for s in range(2):
            payload[1, s] = inputs(pl.ds(s * ROWS + TOK, TAIL))[:mem]
        second(0)
        point(26)
        half = ROWS // 2

        def in_step(s, carry):
            rows = pl.ds(pl.multiple_of(s * half, half), half)
            low_ref[rows, :] = inputs(rows)
            return carry

        lax.fori_loop(0, 2, in_step, 0)
        second(1)
        late(1)
        point(27)
        lax.fori_loop(2, 4, in_step, 0)
        second(2)
        late(2)
        for s in range(2):
            tok_ref[s] = low_ref[s * ROWS:s * ROWS + seg_len, :]
        point(28)
        if kernels:
            x_wait = wire.start(lambda: tok_ref, lambda: both_of(dx_out, place.t), place.pc, lambda: both_of(dx_out, place.nt))
            x_own = copies.start(lambda: tok_ref, lambda: both_of(dx_out, place.t))
            om_out[place.t] = held[0, 3]
            waits = [x_wait, x_own, wire.start(lambda: held.at[0, 3], lambda: om_out.at[place.t], place.pc, lambda: om_out.at[place.nt])]
            rest = SCATTER[29]
            for k in range(2):
                for event in rest[k * len(rest) // 2:(k + 1) * len(rest) // 2]:
                    run(event)
                second(3 + k)
                late(3 + k)
            gm_out[place.t] = held[1, 3]
            waits.append(wire.start(lambda: held.at[1, 3], lambda: gm_out.at[place.t], place.pc, lambda: gm_out.at[place.nt]))
            for wait in waits:
                wait()
            wire.drain()
        else:
            copies.start(lambda: tok_ref, lambda: dx_out)()
            om_out[...] = tail_in[...]
            gm_out[...] = payload[1]
            late_out[...] = late_ref[...]
            vec_out[...] = tot_ref[...]

    slot_shapes = [V((2, 2, ROWS, PAIR), LOW)] + [V((2, ROWS, PAIR), LOW)] * 3 + [V((2, ROWS, PAIR), F32)]
    full = (2, *grid_rows, 3 * width) if kernels else (2, D, 3 * width)
    pl.run_scoped(attention, V((2, seg_len, D), LOW), *slot_shapes, V((2, 2, ROWS, ROWS), LOW), V((2, ROWS, ROWS), LOW), V((2, R, 3 * width), LOW), V(full, LOW))


def back(owners, sums, tails, front_outs, width, hidden, mem, rows, kernels, cid):
    dh = front_outs[14]
    R, D = dh.shape
    pairs = width // PAIR
    S, V = jax.ShapeDtypeStruct, pltpu.VMEM
    hbm, vmem, smem = (pl.BlockSpec(memory_space=m) for m in (pl.ANY, pltpu.VMEM, pltpu.SMEM))
    widths = (hidden, hidden, width, 3 * width)
    grid = (*GRID, D // math.prod(GRID))
    if kernels:
        sums_out = [S((rows, w), F32) for w in (width, width, width, width, hidden, hidden)]
        specs = [vmem] * 6
        two, all_of = (2,), 2
        params = dict(collective_id=cid, has_side_effects=True)
        accs = [V((*grid, w), LOW) for w in widths] * 2
        landings = [s for _, _, _, cuts in SUMS for order, _, wide in cuts for s in scatter_shapes(rows, order, wide)]
    else:
        sums_out = [S((2, *grid, w), LOW) for w in (width, width, width, width, hidden, hidden)]
        specs = [hbm] * 6
        two, all_of = (), 1
        params = {}
        accs = [V((8, 128), LOW)] * 8
        landings = [V((8, 128), LOW)] * (3 * sum(len(cuts) for _, _, _, cuts in SUMS))
    aways = [V((*grid, PART), LOW), V((*grid, PART), LOW), V((*grid, width), LOW), V((pairs, *grid, 3 * PAIR), LOW)]
    seg_len = front_outs[19].shape[1]
    payload = (2, mem, D)
    late = (2, 8, 3 * PAIR)
    six = (2, 2 * pairs, ROWS, PAIR)
    count = 33 + 5 * sum(len(cuts) for _, _, _, cuts in SUMS)
    return pl.pallas_call(
        functools.partial(back_kernel, kernels, mem, seg_len, width, hidden),
        out_shape=[S((2 * all_of, seg_len, D), LOW)] * 2 + [S((*two, *payload), LOW)] * 2 + [S((16, D), F32), S(late, F32), *sums_out],
        in_specs=[smem, vmem] + [hbm] * 20 + [vmem],
        out_specs=[hbm, hbm, vmem, vmem, vmem, vmem, *specs],
        scratch_shapes=[
            V((16, D), F32), V(late, F32), V(six, LOW), V(six, LOW), V((R, D), F32), V((R, D), LOW), V((R, D), LOW), V((R, 1), F32), V((D, R), LOW),
            V(front_outs[1].shape, LOW), V((2, *payload), LOW), V((2, 4, *payload), LOW), V((2, 4, *payload), LOW),
            V((6, 16, D), F32), V((3, 16, D), F32), V((6, *late), F32), V((3, *late), F32),
            *accs, *aways, *landings,
            pltpu.SemaphoreType.DMA((count,)), pltpu.SemaphoreType.DMA((count,)), pltpu.SemaphoreType.DMA((64,)), pltpu.SemaphoreType.DMA((2, 6))],
        compiler_params=pltpu.CompilerParams(vmem_limit_bytes=63 << 20, **params),
    )(owners, sums, *front_outs, tails)


def last_kernel(*refs):
    n = len(refs) // 2
    for a, b in zip(refs[:n], refs[n:]):
        b[...] = a[...]


def last(arrays):
    vmem = pl.BlockSpec(memory_space=pltpu.VMEM)
    return pl.pallas_call(
        last_kernel, out_shape=[jax.ShapeDtypeStruct(a.shape, a.dtype) for a in arrays],
        in_specs=[vmem] * len(arrays), out_specs=[vmem] * len(arrays),
    )(*arrays)


def plain_keep(orders, device, levels):
    sources = jnp.arange(orders.shape[1], dtype=jnp.int32)
    holders = [jnp.full((orders.shape[0],), device, jnp.int32)]
    for bit in range(levels):
        stride = 2 ** (bit + 1)
        position = sources - sources % stride + orders % stride
        holders.append(jnp.sum(jnp.where(position == device, sources, 0), 1))
    return jnp.stack([a == b for a, b in zip(holders[:-1], holders[1:])], 1)


def plain_travel(keep, payload, order):
    size = lax.axis_size("dp")
    for bit in order:
        theirs = lax.ppermute(payload, "dp", [(i, i ^ 1 << bit) for i in range(size)])
        payload = jnp.where(keep[:, bit][:, None, None], payload, theirs)
    return payload


def both_cores(value):
    return lax.all_gather(value, "tensor", axis=0)


def plain_scatter(keep, outs):
    y, dx, mem_y, mem_dx, vec, late, *grads = outs
    mem_y, mem_dx = (both_cores(plain_travel(keep, m, range(keep.shape[1]))) for m in (mem_y, mem_dx))
    parts = []
    for g in grads:
        g = lax.psum_scatter(g.reshape(2, -1, g.shape[-1]).astype(F32), "tensor", scatter_dimension=0)
        parts.append(lax.psum_scatter(g, "dp", scatter_dimension=0, tiled=True))
    everywhere = ("dp", "tensor")
    return [both_cores(y), both_cores(dx), mem_y, mem_dx, lax.psum(vec, everywhere), lax.psum(late, everywhere), *parts]


def local(
    tokens, memory, lengths, owners, w_query, w_key, w_value, w_out, w_up, w_down, b_query, b_value, b_up,
    b_out, b_down, gain_attn, shift_attn, gain_ffn, shift_ffn, cot_tokens, cot_memory,
):
    micro, seg_len, depth = tokens.shape
    mem = memory.shape[1]
    size = lax.axis_size("dp")
    device, t = lax.axis_index("dp"), lax.axis_index("tensor")
    kernels = size == math.prod(GRID)
    rows, width = w_query.shape
    hidden = w_up.shape[1]
    pairs = width // PAIR
    vectors = (b_out, b_down, gain_attn, shift_attn, gain_ffn, shift_ffn)
    columns = jnp.pad(jnp.stack(vectors, 1), ((0, 0), (0, PAIR - len(vectors))))
    bias = jnp.concatenate([b_query, b_value, b_up]).astype(F32)[None]
    if kernels:
        weights = [w_query, w_key, w_value, w_out, w_up, w_down, columns]
        mem_a, mem_b = memory, cot_memory
    else:
        mine = micro // 2
        own = lambda array: lax.dynamic_slice_in_dim(array, t * mine, mine, 0)
        keep = plain_keep(own(owners), device, size.bit_length() - 1)
        mem_a, mem_b = (plain_travel(keep, own(m), range(keep.shape[1] - 1, -1, -1)) for m in (memory, cot_memory))
        by_pair = jnp.concatenate([w[:, i * PAIR:(i + 1) * PAIR] for i in range(pairs) for w in (w_query, w_key, w_value)], 1)
        shards = [by_pair, jnp.concatenate([w_out, columns], 1), w_up, w_down]
        weights = [both_cores(lax.all_gather(s, "dp", axis=0, tiled=True)) for s in shards]
        bias = both_cores(bias)
    *kept, sums, tails = front(lengths, owners, bias, mem_a, mem_b, tokens, cot_tokens, weights, width, hidden, mem, kernels, 1)
    outs = back(owners, sums, tails, kept, width, hidden, mem, rows, kernels, 2)
    if not kernels:
        outs = plain_scatter(keep, outs)
    y, dx, mem_y, mem_dx, vec, late, *grads = outs
    out_tok, grad_tok = (a.reshape(micro, seg_len, depth) for a in (y, dx))
    out_mem, grad_mem, *grads = last([mem_y.reshape(micro, mem, depth), mem_dx.reshape(micro, mem, depth), *grads])
    lines = lax.dynamic_slice(vec[:6], (0, device * rows), (6, rows))
    up_sum = lax.dynamic_slice_in_dim(vec, 8 + 2 * t, 2, 0).reshape(hidden)
    late = lax.dynamic_index_in_dim(late, t, 0, False)[:pairs].reshape(pairs, 3, PAIR)
    return (
        out_tok, out_mem, grad_tok, grad_mem, *grads,
        *(lines[i] for i in range(6)), late[:, 0].reshape(width), late[:, 2].reshape(width), up_sum,
    )


def solution(mesh):
    rows, both, split, every = P("dp", None, None), P("dp", "tensor"), P("tensor"), P("dp")
    return jax.shard_map(
        local,
        mesh=mesh,
        in_specs=(rows, rows, P(), P(), *[both] * 6, *[split] * 3, *[every] * 6, rows, rows),
        out_specs=(*[rows] * 4, *[both] * 6, *[every] * 6, *[split] * 3),
        check_vma=False,
    )
```
